32 devices in a mesh: dp: 8 (over y, x, core), head: 4 (over z).
Axes of the slice: x: 2, y: 2, z: 4, core: 2. Of those that a mesh axis runs over, the one named last changes fastest.
Arguments:
- tokens: bfloat16 [24, 2048, 768], P('dp', 'head'), may hold values from -6 to 6
- lengths: int32 [24], P('dp'), may hold values from 128 to 2048, as said below
- weight_in: float32 [768, 2304], P(('dp', 'head')), may hold values from -0.21875 to 0.21875
- bias_in: float32 [2304], P(('dp', 'head')), may hold values from -3 to 3
- weight_out: float32 [768, 768], P(('dp', 'head')), may hold values from -6 to 6
- bias_out: float32 [768], P(('dp', 'head')), may hold values from -2 to 2
- gain_one: float32 [768], P(('dp', 'head')), may hold values from 0.25 to 1.75
- shift_one: float32 [768], P(('dp', 'head')), may hold values from -2 to 2
- weight_up: float32 [768, 3072], P(('dp', 'head')), may hold values from -0.21875 to 0.21875
- bias_up: float32 [3072], P(('dp', 'head')), may hold values from -2 to 2
- weight_down: float32 [3072, 768], P(('dp', 'head')), may hold values from -0.109375 to 0.109375
- bias_down: float32 [768], P(('dp', 'head')), may hold values from -2 to 2
- gain_two: float32 [768], P(('dp', 'head')), may hold values from 0.25 to 1.75
- shift_two: float32 [768], P(('dp', 'head')), may hold values from -2 to 2
- cotangent: bfloat16 [24, 2048, 768], P('dp', 'head'), may hold values from -6 to 6
Outputs:
- activations: bfloat16 [24, 2048, 768], P('dp', 'head')
- input_grad: float32 [24, 2048, 768], P('dp', 'head')
- grad_weight_in: float32 [768, 2304], P(('dp', 'head'))
- grad_bias_in: float32 [1536], P(('dp', 'head'))
- grad_bias_value: float32 [768], P(('dp', 'head'))
- grad_weight_out: float32 [768, 768], P(('dp', 'head'))
- grad_bias_out: float32 [768], P(('dp', 'head'))
- grad_gain_one: float32 [768], P(('dp', 'head'))
- grad_shift_one: float32 [768], P(('dp', 'head'))
- grad_weight_up: float32 [768, 3072], P(('dp', 'head'))
- grad_bias_up: float32 [3072], P(('dp', 'head'))
- grad_weight_down: float32 [3072, 768], P(('dp', 'head'))
- grad_bias_down: float32 [768], P(('dp', 'head'))
- grad_gain_two: float32 [768], P(('dp', 'head'))
- grad_shift_two: float32 [768], P(('dp', 'head'))
The draws below stay inside these ranges and needn't reach their ends.
Inputs may be any that keep to these rules, and one draw needn't show every extreme that they name: `lengths`: in each aligned group of 3 sequences, one, chosen by the seed, has length 2048.
All inputs are finite; a program needn't handle non-finite values.
Results may differ from the reference program's by a relative error of at most 0.015.
Values may be sent and summed in bfloat16 or wider, within the bound.
A program may use at most 384 MiB of HBM per device.

```python
import math
import jax
import jax.numpy as jnp
from jax import lax

D = 768
H = 12
HD = 64
FF = 3072
BLOCK = 64
LEN = 2048
SEQ_GRP = 3
SEQS = 24


def draw_lengths(key, part):
    key = jax.random.fold_in(key, 7)
    first, second, third = jax.random.split(key, 3)
    count = SEQS // SEQ_GRP
    shorter = jax.random.randint(first, (SEQS,), LEN // 16, LEN + 1)
    coins = jax.random.randint(second, (SEQS,), 0, 5)
    chosen = jax.random.randint(third, (count,), 0, SEQ_GRP)
    order = jnp.arange(SEQS)
    forced = order % SEQ_GRP == jnp.repeat(chosen, SEQ_GRP)
    whole = jnp.logical_or(forced, coins < 3)
    return jnp.where(whole, LEN, shorter).astype(jnp.int32)


def strengthened(drawn, stream_key, source, target, blocks, factor):
    def block_of(axis_at):
        return (jnp.arange(drawn.shape[axis_at]) // (drawn.shape[axis_at] // blocks)).reshape((-1,) + (1,) * (drawn.ndim - 1 - axis_at))

    one_side = jax.random.permutation(stream_key, blocks)[block_of(target)]
    second = (block_of(target) + blocks // 2) % blocks
    return jnp.where((block_of(source) == one_side) | (block_of(source) == second), factor * drawn, drawn)


def block_scale(own_key, extent, cuts, smallest, largest):
    def one(axis_at, shards_of):
        draws = jax.random.uniform(jax.random.fold_in(jax.random.fold_in(own_key, 6), axis_at), (shards_of,), jnp.float32, smallest / len(cuts), largest / len(cuts))
        return jnp.repeat(jnp.exp(draws), extent[axis_at] // shards_of).reshape((-1,) + (1,) * (len(extent) - axis_at - 1))

    factor_of = one(*cuts[0])
    for cut in cuts[1:]:
        factor_of = factor_of * one(*cut)
    return factor_of


def centred(rng, shape, deviation, bound, cuts=(), kind=jnp.bfloat16):
    drawn = jax.random.normal(rng, shape, jnp.float32) * deviation
    if len(cuts) > 0:
        drawn = block_scale(rng, shape, cuts, -0.22, 0.18) * drawn
    return jnp.clip(drawn, min=-bound, max=bound).astype(kind)


def bell_draw_with(stream_key, dims, scale, most, pieces, heavy, dtype=jnp.bfloat16):
    values = scale * jax.random.normal(stream_key, dims, jnp.float32)
    if pieces:
        values = values * block_scale(stream_key, dims, pieces, -0.22, 0.18)
    return jnp.clip(strengthened(values, jax.random.fold_in(stream_key, 3), *heavy), -most, most).astype(dtype)


def setup_inputs(seed: int = 0) -> dict:
    key_of = jax.random.split(jax.random.key(seed), 16)
    tokens = centred(key_of[0], (SEQS, LEN, D), 1.0, 6.0, ((0, 8), (1, 4)))
    lengths = draw_lengths(jax.random.fold_in(key_of[15], 71), 0)
    weight_in = centred(key_of[2], (D, 3 * D), D ** -0.5, 0.21875, ((0, 32),), jnp.float32)
    bias_in = centred(key_of[3], (3 * D,), 0.5, 3.0, ((0, 32),), jnp.float32)
    weight_out = centred(key_of[4], (D, D), (max(1, 2 * D // LEN)) ** -0.5, 6.0, ((0, 32),), jnp.float32)
    bias_out = centred(key_of[5], (D,), 0.3, 2.0, ((0, 32),), jnp.float32)
    gain_one = jnp.clip(1.0 + 0.15 * jax.random.normal(key_of[6], (D,), jnp.float32), 0.25, 1.75)
    shift_one = centred(key_of[7], (D,), 0.3, 2.0, ((0, 32),), jnp.float32)
    weight_up = centred(key_of[8], (D, FF), D ** -0.5, 0.21875, ((0, 32),), jnp.float32)
    bias_up = centred(key_of[9], (FF,), 0.3, 2.0, ((0, 32),), jnp.float32)
    weight_down = centred(key_of[10], (FF, D), FF ** -0.5, 0.109375, ((0, 32),), jnp.float32)
    bias_down = centred(key_of[11], (D,), 0.3, 2.0, ((0, 32),), jnp.float32)
    gain_two = jnp.clip(1.0 + 0.15 * jax.random.normal(key_of[12], (D,), jnp.float32), 0.25, 1.75)
    shift_two = centred(key_of[13], (D,), 0.3, 2.0, ((0, 32),), jnp.float32)
    cotangent = bell_draw_with(key_of[14], (SEQS, LEN, D), 1.0, 6.0, ((0, 8), (1, 4)), (0, 2, 8, 2.0))
    return {"tokens": tokens, "lengths": lengths, "weight_in": weight_in, "bias_in": bias_in, "weight_out": weight_out, "bias_out": bias_out, "gain_one": gain_one, "shift_one": shift_one, "weight_up": weight_up, "bias_up": bias_up, "weight_down": weight_down, "bias_down": bias_down, "gain_two": gain_two, "shift_two": shift_two, "cotangent": cotangent}


@jax.custom_vjp
def low(v):
    return lax.optimization_barrier(v.astype(jnp.bfloat16)).astype(jnp.float32)

@jax.custom_vjp
def low_back(v):
    return v

def low_keep(v):
    return (low(v), None)

def low_pass(kept, grad):
    return (grad,)

def back_keep(v):
    return (v, None)

def back_low(kept, grad):
    return (low(grad),)
low.defvjp(low_keep, low_pass)
low_back.defvjp(back_keep, back_low)

def send(value):
    return low_back(low(value))

def project(left, right):
    return jnp.einsum('...i,ij->...j', left, right, precision=lax.Precision.HIGHEST)

def attend(query_cos, query_sin, key_cos, key_sin, values, block):
    batch, length, heads, width = query_cos.shape
    count = length // block
    highest = lax.Precision.HIGHEST

    def blocks(array):
        return array.reshape(batch, count, block, heads, width)
    query_cos, query_sin, key_cos, key_sin, values = (blocks(query_cos), blocks(query_sin), blocks(key_cos), blocks(key_sin), blocks(values))
    scores = jnp.einsum('bnihe,bnjhe->bnhij', query_cos, key_cos, precision=highest)
    scores = scores + jnp.einsum('bnihe,bnjhe->bnhij', query_sin, key_sin, precision=highest)
    lower = jnp.tril(jnp.ones((block, block), jnp.float32))
    scores = scores * lower
    inner_num = jnp.einsum('bnhij,bnjhe->bnihe', scores, values, precision=highest)
    inner_den = jnp.transpose(lax.optimization_barrier(jnp.sum(scores, axis=-1)), (0, 1, 3, 2))
    state_cos = jnp.einsum('bnjhe,bnjhf->bnhef', key_cos, values, precision=highest)
    state_sin = jnp.einsum('bnjhe,bnjhf->bnhef', key_sin, values, precision=highest)
    total_cos = lax.optimization_barrier(jnp.sum(key_cos, axis=2))
    total_sin = lax.optimization_barrier(jnp.sum(key_sin, axis=2))
    prior_cos = jnp.cumsum(state_cos, axis=1) - state_cos
    prior_sin = jnp.cumsum(state_sin, axis=1) - state_sin
    before_cos = jnp.cumsum(total_cos, axis=1) - total_cos
    before_sin = jnp.cumsum(total_sin, axis=1) - total_sin
    outer_num = jnp.einsum('bnihe,bnhef->bnihf', query_cos, prior_cos, precision=highest)
    outer_num = outer_num + jnp.einsum('bnihe,bnhef->bnihf', query_sin, prior_sin, precision=highest)
    outer_den = jnp.einsum('bnihe,bnhe->bnih', query_cos, before_cos, precision=highest)
    outer_den = outer_den + jnp.einsum('bnihe,bnhe->bnih', query_sin, before_sin, precision=highest)
    numer = inner_num + outer_num
    denom = inner_den + outer_den
    result = numer / jnp.maximum(denom, 1.0)[..., None]
    return result.reshape(batch, length, heads, width)

def norm(value, gain, shift):
    centered = value - lax.optimization_barrier(jnp.mean(value, axis=-1, keepdims=True))
    spread = lax.optimization_barrier(jnp.mean(centered * centered, axis=-1, keepdims=True))
    return centered * lax.rsqrt(spread + 1e-05) * gain + shift

def layer(inputs, lengths, params):
    weight_in, bias_in, weight_out, bias_out, gain_one, shift_one, weight_up, bias_up, weight_down, bias_down, gain_two, shift_two = [low(item) for item in params]
    group, length, width = inputs.shape
    mixed = low_back(project(inputs, weight_in) + bias_in)
    shape = (group, length, H, HD)
    query = mixed[..., :width].reshape(shape)
    keys = mixed[..., width:2 * width].reshape(shape)
    values = mixed[..., 2 * width:].reshape(shape)
    places = jnp.arange(length).astype(jnp.float32)
    limits = lengths.astype(jnp.float32)
    valid = (places[None, :] < limits[:, None]).astype(jnp.float32)[:, :, None, None]
    angle = (0.5 * math.pi * places[None, :] / limits[:, None])[:, :, None, None]
    cosine = jnp.cos(angle)
    sine = jnp.sin(angle)
    query_feat = jax.nn.softplus(query) * valid
    key_feat = jax.nn.softplus(keys) * valid
    attended = attend(send(query_feat * cosine), send(query_feat * sine), send(key_feat * cosine), send(key_feat * sine), send(values), BLOCK)
    joined = send(attended).reshape(group, length, width)
    first = inputs + low_back(project(joined, weight_out) + bias_out)
    normed = norm(first, gain_one, shift_one)
    upper = low_back(project(low(normed), weight_up) + bias_up)
    hidden = low(jax.nn.gelu(upper, approximate=False))
    second = normed + low_back(project(hidden, weight_down) + bias_down)
    return norm(second, gain_two, shift_two)

def reference(tokens, lengths, weight_in, bias_in, weight_out, bias_out, gain_one, shift_one, weight_up, bias_up, weight_down, bias_down, gain_two, shift_two, cotangent):
    params = (weight_in, bias_in, weight_out, bias_out, gain_one, shift_one, weight_up, bias_up, weight_down, bias_down, gain_two, shift_two)
    pairs = SEQS // 2
    inputs = tokens.astype(jnp.float32).reshape(pairs, 2, LEN, D)
    limits = lengths.reshape(pairs, 2)
    seeds = cotangent.astype(jnp.float32).reshape(pairs, 2, LEN, D)

    def visit(totals, item):
        block_in, spans, grads = item
        result, pull = jax.vjp(lambda values, weights: layer(values, spans, weights), block_in, params)
        back, terms = pull(grads)
        return (jax.tree.map(jnp.add, totals, terms), (result, back))
    start = tuple((jnp.zeros_like(item) for item in params))
    totals, (results, backs) = lax.scan(visit, start, (inputs, limits, seeds))
    return (results.reshape(SEQS, LEN, D).astype(jnp.bfloat16), backs.reshape(SEQS, LEN, D), totals[0], totals[1][:2 * D], totals[1][2 * D:], totals[2], totals[3], totals[4], totals[5], totals[6], totals[7], totals[8], totals[9], totals[10], totals[11])
```

```python
import functools
import math

import jax
import jax.numpy as jnp
from jax import lax
from jax.experimental import pallas as pl
from jax.experimental.pallas import tpu as pltpu
from jax.sharding import PartitionSpec as P

F32 = jnp.float32
BF16 = jnp.bfloat16
CHUNK = 256
LANES = 128
HALF = 64
BIG = 60 * 1024 * 1024


def dot(a, b):
    return lax.dot_general(a, b, (((1,), (0,)), ((), ())), preferred_element_type=F32)


def dot_t(a, b):
    return lax.dot_general(a, b, (((1,), (1,)), ((), ())), preferred_element_type=F32)


def tdot(a, b):
    return lax.dot_general(a, b, (((0,), (0,)), ((), ())), preferred_element_type=F32)


def iota(shape, dim):
    return lax.broadcasted_iota(jnp.int32, shape, dim)


def block_mask(rows, cols):
    return ((iota((rows, cols), 0) & HALF) == (iota((rows, cols), 1) & HALF)).astype(F32)


def head_masks():
    lane = iota((1, LANES), 1)
    first = (lane < HALF).astype(F32)
    place = lane & (HALF - 1)
    return first, 1.0 - first, (place == 0).astype(F32), (place == 1).astype(F32)


def cos_poly(z):
    t = z * z
    r = -1.0 / 3628800 + t * (1.0 / 479001600)
    r = 1.0 / 40320 + t * r
    r = -1.0 / 720 + t * r
    r = 1.0 / 24 + t * r
    r = -0.5 + t * r
    return 1.0 + t * r


def sin_poly(z):
    t = z * z
    r = -1.0 / 39916800 + t * (1.0 / 6227020800)
    r = 1.0 / 362880 + t * r
    r = -1.0 / 5040 + t * r
    r = 1.0 / 120 + t * r
    r = -1.0 / 6 + t * r
    return z + z * (t * r)


def angles(start, limit, rows):
    place = iota((rows, LANES), 0) + start
    theta = jnp.minimum((0.5 * math.pi * place.astype(F32)) / limit.astype(F32), 0.5 * math.pi)
    return cos_poly(theta), sin_poly(theta), (place < limit).astype(F32)


def weights_within(limit):
    apart = iota((CHUNK, CHUNK), 0) - iota((CHUNK, CHUNK), 1)
    theta = jnp.minimum((0.5 * math.pi * apart.astype(F32)) / limit.astype(F32), 0.5 * math.pi)
    return jnp.where(apart >= 0, cos_poly(theta), 0.0)


def softplus(x):
    t = jnp.exp(-jnp.abs(x))
    tail = jnp.where(t < 1e-3, t * (1.0 - 0.5 * t), jnp.log(1.0 + t))
    return jnp.maximum(x, 0.0) + tail


def slope(feature):
    small = feature * (1.0 - feature * (0.5 - feature * (1.0 / 6)))
    return jnp.where(feature < 0.01, small, 1.0 - jnp.exp(-feature))


def pack(state):
    return jnp.concatenate(
        [state[0:64] + state[64:128], state[128:192] + state[192:256]], axis=0
    )


def unpack(packed, mask):
    top, bottom = packed[0:64], packed[64:128]
    return jnp.concatenate([top, top, bottom, bottom], axis=0) * mask


def spread(feature, cosine, sine):
    return jnp.concatenate([feature * cosine, feature * sine], axis=1).astype(BF16)


def stacked_heads(value, first, second):
    return jnp.concatenate([value * first, value * second], axis=0).astype(BF16)


def rows_of(s, c, local):
    return pl.ds(pl.multiple_of(s * local + c * CHUNK, CHUNK), CHUNK)


def lanes_of(p):
    return pl.ds(pl.multiple_of(p * LANES, LANES), LANES)


def mixed_kernel(groups, local, lens, tok, weight, bias, q_out, k_out, v_out, state_out, cos_s, sin_s, ok_s):
    width = tok.shape[1]
    pairs = width // LANES
    base = lax.axis_index("head") * local
    for s in range(groups):
        cosine, sine, valid = angles(base, lens[s], local)
        cos_s[s * local : (s + 1) * local] = cosine
        sin_s[s * local : (s + 1) * local] = sine
        ok_s[s * local : (s + 1) * local] = valid
    mask = block_mask(256, 256)
    ones = jnp.ones((CHUNK, LANES), BF16)

    def project(i, _):
        r = pl.ds(pl.multiple_of(i * CHUNK, CHUNK), CHUNK)
        x = tok[r]
        valid = ok_s[r]
        for part, out in enumerate((q_out, k_out)):
            for n in range(0, width, 256):
                at = part * width + n
                y = dot(x, weight[:, at : at + 256]) + bias[:, at : at + 256]
                out[r, n : n + 256] = (softplus(y) * jnp.concatenate([valid, valid], axis=1)).astype(BF16)
        for n in range(0, width, 256):
            at = 2 * width + n
            v_out[r, n : n + 256] = (dot(x, weight[:, at : at + 256]) + bias[:, at : at + 256]).astype(BF16)
        return 0

    lax.fori_loop(0, groups * local // CHUNK, project, 0)

    def sums(i, _):
        s, p = i // pairs, i % pairs
        total = jnp.zeros((256, 256), F32)
        for c in range(local // CHUNK):
            r, n = rows_of(s, c, local), lanes_of(p)
            k2 = spread(k_out[r, n].astype(F32), cos_s[r], sin_s[r])
            total = total + tdot(k2, jnp.concatenate([v_out[r, n], ones], axis=1))
        state_out[i] = pack(total * mask)
        return 0

    lax.fori_loop(0, groups * pairs, sums, 0)


def attend_kernel(
    groups, local, lens, q, k, v, prior, joined, rest, inverse, states, fine, cos_s, sin_s, within
):
    pairs = q.shape[1] // LANES
    base = lax.axis_index("head") * local
    for s in range(groups):
        cosine, sine, _ = angles(base, lens[s], local)
        cos_s[s * local : (s + 1) * local] = cosine
        sin_s[s * local : (s + 1) * local] = sine
        within[s] = weights_within(lens[s])
    count = local // CHUNK

    def body(i, _):
        s, p = i // pairs, i % pairs
        n = lanes_of(p)
        first, second, _, _ = head_masks()
        mask = block_mask(256, 256)
        ones = jnp.ones((CHUNK, LANES), BF16)
        state = unpack(prior[i].astype(F32), mask)
        for c in range(count):
            r = rows_of(s, c, local)
            cosine, sine = cos_s[r], sin_s[r]
            feature = q[r, n].astype(F32)
            key = k[r, n]
            value = jnp.concatenate([v[r, n], ones], axis=1)
            low = state.astype(BF16)
            states[i * count + c] = low
            fine[i * count + c] = (state - low.astype(F32)).astype(BF16)
            outer = dot(spread(feature, cosine, sine), low)
            scores = dot_t(stacked_heads(feature, first, second), key)
            m = within[s]
            scores = (scores * jnp.concatenate([m, m], axis=0)).astype(BF16)
            inner = dot(scores, value)
            both = outer + jnp.where(
                jnp.concatenate([first, first], axis=1) > 0, inner[:CHUNK], inner[CHUNK:]
            )
            den = both[:, LANES:]
            above = 1.0 / jnp.maximum(den, 1.0)
            attended = both[:, :LANES] * above
            rounded = attended.astype(BF16)
            joined[r, n] = rounded
            rest[r, n] = (attended - rounded.astype(F32)).astype(BF16)
            inverse[r, n] = jnp.where(den > 1.0, above, -1.0).astype(BF16)
            if c + 1 < count:
                state = state + tdot(spread(key.astype(F32), cosine, sine), value) * mask
        return 0

    lax.fori_loop(0, groups * pairs, body, 0)


def gelu_both(x):
    z = jnp.abs(x) * (1.0 / math.sqrt(2.0))
    t = 1.0 / (1.0 + 0.3275911 * z)
    e = jnp.exp(-0.5 * x * x)
    poly = t * (
        0.254829592 + t * (-0.284496736 + t * (1.421413741 + t * (-1.453152027 + t * 1.061405429)))
    )
    tail = 0.5 * poly * e
    phi = jnp.where(x >= 0, 1.0 - tail, tail)
    return x * phi, phi + x * e * (1.0 / math.sqrt(2.0 * math.pi))


def mean_of(x):
    return jnp.mean(x, axis=1, keepdims=True)


def column_sum(x):
    return jnp.sum(x, axis=0, keepdims=True)


def normalised(x):
    centred = x - mean_of(x)
    inv = lax.rsqrt(mean_of(centred * centred) + 1e-05)
    return centred * inv, inv


def feed_kernel(
    tok, joined, cot, w_out, w_up, w_down, b_out, g_one, s_one, b_up, b_down, g_two, s_two,
    act, g_first, g_joined, gw_out, gw_up, gw_down, gb_out, gg_one, gs_one, gb_up, gb_down, gg_two, gs_two,
    norm_s, low_s, hid_s, der_s, sec_s, branch_s, acc_s,
):
    rows = tok.shape[0]
    ff = w_up.shape[1]
    step = 768
    count = ff // step

    @pl.when(pl.program_id(0) == 0)
    def _():
        for ref in (gw_out, gw_up, gw_down, gb_out, gg_one, gs_one, gb_up, gb_down, gg_two, gs_two):
            ref[...] = jnp.zeros_like(ref)

    first = tok[...].astype(F32) + (dot(joined[...], w_out[...]) + b_out[...])
    unit_one, inv_one = normalised(first)
    norm_s[...] = unit_one
    normed = unit_one * g_one[...] + s_one[...]
    low_s[...] = normed.astype(BF16)
    sec_s[...] = normed + b_down[...]

    def up(j, _):
        n = pl.ds(pl.multiple_of(j * step, step), step)
        x = dot(low_s[...], w_up[:, n]) + b_up[:, n]
        y, d = gelu_both(x)
        hid_s[:, n] = y.astype(BF16)
        der_s[:, n] = d.astype(BF16)
        return 0

    lax.fori_loop(0, count, up, 0)
    second = sec_s[...] + dot(hid_s[...], w_down[...])
    unit_two, inv_two = normalised(second)
    act[...] = (unit_two * g_two[...] + s_two[...]).astype(BF16)
    c = cot[...].astype(F32)
    gg_two[...] += column_sum(c * unit_two)
    gs_two[...] += column_sum(c)
    e = c * g_two[...]
    g_second = inv_two * (e - mean_of(e) - unit_two * mean_of(e * unit_two))
    sec_s[...] = g_second
    branch = g_second.astype(BF16)
    branch_s[...] = branch
    gb_down[...] += column_sum(branch.astype(F32))

    def down(j, _):
        n = pl.ds(pl.multiple_of(j * step, step), step)
        gh = dot_t(branch_s[...], w_down[n, :])
        gu = gh * der_s[:, n].astype(F32)
        gu = gu.astype(BF16)
        der_s[:, n] = gu
        gb_up[:, n] += column_sum(gu.astype(F32))
        gw_down[n, :] += tdot(hid_s[:, n], branch_s[...])
        gw_up[:, n] += tdot(low_s[...], gu)
        return 0

    lax.fori_loop(0, count, down, 0)
    g_normed = sec_s[...] + dot_t(der_s[...], w_up[...])
    unit_one = norm_s[...]
    gg_one[...] += column_sum(g_normed * unit_one)
    gs_one[...] += column_sum(g_normed)
    e = g_normed * g_one[...]
    gf = inv_one * (e - mean_of(e) - unit_one * mean_of(e * unit_one))
    g_first[...] = gf
    go = gf.astype(BF16)
    gb_out[...] += column_sum(go.astype(F32))
    gw_out[...] += tdot(joined[...], go)
    g_joined[...] = dot_t(go, w_out[...]).astype(BF16)


def pulled(gj, joined, rest, inverse, one, two):
    ri = inverse.astype(F32)
    gnum = (gj.astype(F32) * jnp.abs(ri)).astype(BF16)
    product = gnum.astype(F32) * (joined.astype(F32) + rest.astype(F32))
    high = product.astype(BF16)
    low = (product - high.astype(F32)).astype(BF16)
    ones = block_mask(2 * LANES, LANES).astype(BF16)
    gden = jnp.where(ri > 0, -dot(jnp.concatenate([high, low], axis=1), ones), 0.0)
    high = gden.astype(BF16).astype(F32)
    return gnum, (high * one + (gden - high) * two).astype(BF16)


def later_kernel(groups, local, lens, q, gj, joined, rest, inverse, state_out, cos_s, sin_s):
    pairs = q.shape[1] // LANES
    base = lax.axis_index("head") * local
    for s in range(groups):
        cosine, sine, _ = angles(base, lens[s], local)
        cos_s[s * local : (s + 1) * local] = cosine
        sin_s[s * local : (s + 1) * local] = sine

    def body(i, _):
        s, p = i // pairs, i % pairs
        total = jnp.zeros((256, 256), F32)
        for c in range(local // CHUNK):
            r, n = rows_of(s, c, local), lanes_of(p)
            _, _, one, two = head_masks()
            gnum, gden = pulled(gj[r, n], joined[r, n], rest[r, n], inverse[r, n], one, two)
            q2 = spread(q[r, n].astype(F32), cos_s[r], sin_s[r])
            total = total + tdot(q2, jnp.concatenate([gnum, gden], axis=1))
        state_out[i] = pack(total * block_mask(256, 256))
        return 0

    lax.fori_loop(0, groups * pairs, body, 0)


def back_kernel(
    groups, local, lens, q, k, v, gj, joined, rest, inverse, states, fine, after, out, cos_s, sin_s, within
):
    width = q.shape[1]
    pairs = width // LANES
    count = local // CHUNK
    base = lax.axis_index("head") * local
    for s in range(groups):
        cosine, sine, _ = angles(base, lens[s], local)
        cos_s[s * local : (s + 1) * local] = cosine
        sin_s[s * local : (s + 1) * local] = sine
        within[s] = weights_within(lens[s])

    def body(i, _):
        s, p = i // pairs, i % pairs
        n = lanes_of(p)
        first, second, one, two = head_masks()
        mask = block_mask(256, 256)
        ones = jnp.ones((CHUNK, LANES), BF16)
        picks = jnp.broadcast_to(one + two, (CHUNK, LANES)).astype(BF16)
        state = unpack(after[i].astype(F32), mask)
        for c in reversed(range(count)):
            r = rows_of(s, c, local)
            cosine, sine = cos_s[r], sin_s[r]
            feature = q[r, n].astype(F32)
            key_low = k[r, n]
            key = key_low.astype(F32)
            value = v[r, n]
            gnum, gden = pulled(gj[r, n], joined[r, n], rest[r, n], inverse[r, n], one, two)
            m = within[s]
            m = jnp.concatenate([m, m], axis=0)
            q2 = spread(feature, cosine, sine)
            pair = jnp.concatenate([gnum, gden], axis=1)
            outer = dot_t(pair, states[i * count + c]) + dot_t(pair, fine[i * count + c])
            heads = stacked_heads(feature, first, second)
            scores = (dot_t(heads, key_low) * m).astype(BF16)
            gheads = stacked_heads(gnum.astype(F32), first, second)
            left = jnp.concatenate([gheads, stacked_heads(gden.astype(F32), first, second)], axis=1)
            g = (dot_t(left, jnp.concatenate([value, ones], axis=1)) * m).astype(BF16)
            inner = dot(g, key_low)
            gq = outer[:, :LANES] * cosine + outer[:, LANES:] * sine
            gq = gq + jnp.where(first > 0, inner[:CHUNK], inner[CHUNK:])
            low = state.astype(BF16)
            gv = dot(spread(key, cosine, sine), low[:, :LANES]) + tdot(gheads, scores).T
            pick = jnp.concatenate([value, picks], axis=1)
            outer = dot_t(pick, low) + dot_t(pick, (state - low.astype(F32)).astype(BF16))
            gk = outer[:, :LANES] * cosine + outer[:, LANES:] * sine + tdot(heads, g).T
            out[r, n] = (gq * slope(feature)).astype(BF16)
            out[r, pl.ds(pl.multiple_of(width + p * LANES, LANES), LANES)] = (gk * slope(key)).astype(BF16)
            out[r, pl.ds(pl.multiple_of(2 * width + p * LANES, LANES), LANES)] = gv.astype(BF16)
            if c > 0:
                state = state + tdot(q2, pair) * mask
        return 0

    lax.fori_loop(0, groups * pairs, body, 0)


def input_kernel(tok, gm, weight, g_first, grad, gw, gb):
    @pl.when(pl.program_id(0) == 0)
    def _():
        gw[...] = jnp.zeros_like(gw)
        gb[...] = jnp.zeros_like(gb)

    low = gm[...]
    gb[...] += column_sum(low.astype(F32))
    gw[...] += tdot(tok[...], low)
    grad[...] = g_first[...] + dot_t(low, weight[...])


VMEM = pl.BlockSpec(memory_space=pltpu.VMEM)
SMEM = pl.BlockSpec(memory_space=pltpu.SMEM)


def params():
    return pltpu.CompilerParams(vmem_limit_bytes=BIG)


def shape(dims, kind=BF16):
    return jax.ShapeDtypeStruct(dims, kind)


def shards(
    tokens, lengths, weight_in, bias_in, weight_out, bias_out, gain_one, shift_one,
    weight_up, bias_up, weight_down, bias_down, gain_two, shift_two, cotangent,
):
    groups, local, width = tokens.shape
    rows = groups * local
    pairs = width // LANES
    count = local // CHUNK
    axes = ("dp", "head")
    parts = lax.axis_size("head")
    me = lax.axis_index("head")

    def gather(item):
        return lax.all_gather(item.astype(BF16), axes, axis=0, tiled=True)

    w_in, w_out, w_up, w_down = map(gather, (weight_in, weight_out, weight_up, weight_down))
    small = (bias_in, bias_out, gain_one, shift_one, bias_up, bias_down, gain_two, shift_two)
    sizes = [item.shape[0] for item in small]
    gathered = lax.all_gather(jnp.concatenate([item.astype(BF16) for item in small]), axes, axis=0)
    cuts = [sum(sizes[:i]) for i in range(len(sizes) + 1)]
    b_in, b_out, g_one, s_one, b_up, b_down, g_two, s_two = (
        gathered[:, a:b].reshape(1, -1).astype(F32) for a, b in zip(cuts, cuts[1:])
    )
    ff = w_up.shape[1]
    tok = tokens.reshape(rows, width)
    table = pltpu.VMEM((rows, LANES), F32)
    plane = shape((rows, width))
    q, k, v, sums = pl.pallas_call(
        functools.partial(mixed_kernel, groups, local),
        out_shape=(plane, plane, plane, shape((groups * pairs, 128, 256), F32)),
        in_specs=[SMEM, VMEM, VMEM, VMEM],
        out_specs=(VMEM,) * 4,
        scratch_shapes=[table, table, table],
        compiler_params=params(),
    )(lengths, tok, w_in, b_in)

    def scanned(item, keep):
        every = lax.all_gather(item, "head", axis=0)
        use = keep(jnp.arange(parts)).astype(F32).reshape(parts, 1, 1, 1)
        return jnp.sum(every * use, axis=0)

    prior = scanned(sums, lambda at: at < me)
    joined, rest, inverse, states, fine = pl.pallas_call(
        functools.partial(attend_kernel, groups, local),
        out_shape=(plane,) * 3 + (shape((groups * pairs * count, 256, 256)),) * 2,
        in_specs=[SMEM] + [VMEM] * 4,
        out_specs=(VMEM,) * 5,
        scratch_shapes=[table, table, pltpu.VMEM((groups, CHUNK, CHUNK), F32)],
        compiler_params=params(),
    )(lengths, q, k, v, prior)

    tile = local

    def block(cols):
        return pl.BlockSpec((tile, cols), lambda i: (i, 0))

    def fixed(*dims):
        return pl.BlockSpec(dims, lambda i: (0,) * len(dims), pipeline_mode=pl.Buffered(1))

    vectors = [fixed(1, width)] * 3 + [fixed(1, ff)] + [fixed(1, width)] * 3
    weights = [fixed(width, width), fixed(width, ff), fixed(ff, width)]
    vector_shapes = [shape((1, width), F32)] * 3 + [shape((1, ff), F32)] + [shape((1, width), F32)] * 3
    (
        activations, g_first, g_joined, gw_out, gw_up, gw_down,
        gb_out, gg_one, gs_one, gb_up, gb_down, gg_two, gs_two,
    ) = pl.pallas_call(
        feed_kernel,
        grid=(rows // tile,),
        out_shape=[plane, shape((rows, width), F32), plane]
        + [shape((width, width), F32), shape((width, ff), F32), shape((ff, width), F32)]
        + vector_shapes,
        in_specs=[block(width)] * 3 + weights + vectors,
        out_specs=[block(width)] * 3 + weights + vectors,
        scratch_shapes=[
            pltpu.VMEM((tile, width), F32),
            pltpu.VMEM((tile, width), BF16),
            pltpu.VMEM((tile, ff), BF16),
            pltpu.VMEM((tile, ff), BF16),
            pltpu.VMEM((tile, width), F32),
            pltpu.VMEM((tile, width), BF16),
            pltpu.VMEM((8, LANES), F32),
        ],
        compiler_params=params(),
    )(
        tok, joined, cotangent.reshape(rows, width), w_out, w_up, w_down,
        b_out, g_one, s_one, b_up, b_down, g_two, s_two,
    )
    sums = pl.pallas_call(
        functools.partial(later_kernel, groups, local),
        out_shape=shape((groups * pairs, 128, 256), F32),
        in_specs=[SMEM] + [VMEM] * 5,
        out_specs=VMEM,
        scratch_shapes=[table, table],
        compiler_params=params(),
    )(lengths, q, g_joined, joined, rest, inverse)
    after = scanned(sums, lambda at: at > me)
    g_mixed = pl.pallas_call(
        functools.partial(back_kernel, groups, local),
        out_shape=shape((rows, 3 * width)),
        in_specs=[SMEM] + [VMEM] * 10,
        out_specs=VMEM,
        scratch_shapes=[table, table, pltpu.VMEM((groups, CHUNK, CHUNK), F32)],
        compiler_params=params(),
    )(lengths, q, k, v, g_joined, joined, rest, inverse, states, fine, after)
    input_grad, gw_in, gb_in = pl.pallas_call(
        input_kernel,
        grid=(rows // tile,),
        out_shape=[shape((rows, width), F32), shape((width, 3 * width), F32), shape((1, 3 * width), F32)],
        in_specs=[block(width), block(3 * width), fixed(width, 3 * width), block(width)],
        out_specs=[block(width), fixed(width, 3 * width), fixed(1, 3 * width)],
        compiler_params=params(),
    )(tok, g_mixed, w_in, g_first)

    def scatter(item):
        return lax.psum_scatter(item, axes, scatter_dimension=0, tiled=True)

    gb_in = gb_in.reshape(-1)
    cols = [gb_in[: 2 * width], gb_in[2 * width :]] + [
        item.reshape(-1) for item in (gb_out, gg_one, gs_one, gb_up, gb_down, gg_two, gs_two)
    ]
    total = lax.axis_size(axes)
    cut = [item.shape[0] // total for item in cols]
    merged = scatter(jnp.concatenate([item.reshape(total, -1) for item in cols], axis=1).reshape(-1))
    places = [sum(cut[:i]) for i in range(len(cut) + 1)]
    (gb_front, gb_value, gb_out, gg_one, gs_one, gb_up, gb_down, gg_two, gs_two) = (
        merged[a:b] for a, b in zip(places, places[1:])
    )
    return (
        activations.reshape(groups, local, width),
        input_grad.reshape(groups, local, width),
        scatter(gw_in), gb_front, gb_value, scatter(gw_out), gb_out, gg_one, gs_one,
        scatter(gw_up), gb_up, scatter(gw_down), gb_down, gg_two, gs_two,
    )


def solution(mesh):
    spread_rows = P("dp", "head", None)
    matrix = P(("dp", "head"), None)
    vector = P(("dp", "head"))
    return jax.shard_map(
        shards,
        mesh=mesh,
        in_specs=(
            spread_rows, P("dp"), matrix, vector, matrix, vector, vector, vector,
            matrix, vector, matrix, vector, vector, vector, spread_rows,
        ),
        out_specs=(
            spread_rows, spread_rows, matrix, vector, vector, matrix, vector, vector, vector,
            matrix, vector, matrix, vector, vector, vector,
        ),
        check_vma=False,
    )
```

```python
import functools
import math

import jax
import jax.numpy as jnp
from jax import lax
from jax.experimental import pallas as pl
from jax.experimental.pallas import tpu as pltpu
from jax.sharding import PartitionSpec as P

F32 = jnp.float32
BF16 = jnp.bfloat16
CHUNK = 256
LANES = 128
HALF = 64
BIG = 60 * 1024 * 1024
MESH = pl.DeviceIdType.MESH


def dot(a, b):
    return lax.dot_general(a, b, (((1,), (0,)), ((), ())), preferred_element_type=F32)


def dot_t(a, b):
    return lax.dot_general(a, b, (((1,), (1,)), ((), ())), preferred_element_type=F32)


def tdot(a, b):
    return lax.dot_general(a, b, (((0,), (0,)), ((), ())), preferred_element_type=F32)


def iota(shape, dim):
    return lax.broadcasted_iota(jnp.int32, shape, dim)


def block_mask(rows, cols):
    return ((iota((rows, cols), 0) & HALF) == (iota((rows, cols), 1) & HALF)).astype(F32)


def head_masks():
    lane = iota((1, LANES), 1)
    first = (lane < HALF).astype(F32)
    place = lane & (HALF - 1)
    return first, 1.0 - first, (place == 0).astype(F32), (place == 1).astype(F32)


def cos_poly(z):
    t = z * z
    r = -1.0 / 3628800 + t * (1.0 / 479001600)
    r = 1.0 / 40320 + t * r
    r = -1.0 / 720 + t * r
    r = 1.0 / 24 + t * r
    r = -0.5 + t * r
    return 1.0 + t * r


def sin_poly(z):
    t = z * z
    r = -1.0 / 39916800 + t * (1.0 / 6227020800)
    r = 1.0 / 362880 + t * r
    r = -1.0 / 5040 + t * r
    r = 1.0 / 120 + t * r
    r = -1.0 / 6 + t * r
    return z + z * (t * r)


def angles(start, limit, rows):
    place = iota((rows, LANES), 0) + start
    theta = jnp.minimum((0.5 * math.pi * place.astype(F32)) / limit.astype(F32), 0.5 * math.pi)
    return cos_poly(theta), sin_poly(theta), (place < limit).astype(F32)


def weights_within(limit):
    apart = iota((CHUNK, CHUNK), 0) - iota((CHUNK, CHUNK), 1)
    theta = jnp.minimum((0.5 * math.pi * apart.astype(F32)) / limit.astype(F32), 0.5 * math.pi)
    return jnp.where(apart >= 0, cos_poly(theta), 0.0)


def softplus(x):
    t = jnp.exp(-jnp.abs(x))
    tail = jnp.where(t < 1e-3, t * (1.0 - 0.5 * t), jnp.log(1.0 + t))
    return jnp.maximum(x, 0.0) + tail


def slope(feature):
    small = feature * (1.0 - feature * (0.5 - feature * (1.0 / 6)))
    return jnp.where(feature < 0.01, small, 1.0 - jnp.exp(-feature))


def pack(state):
    return jnp.concatenate([state[0:64] + state[64:128], state[128:192] + state[192:256]], axis=0)


def unpack(packed, mask):
    top, bottom = packed[0:64], packed[64:128]
    return jnp.concatenate([top, top, bottom, bottom], axis=0) * mask


def column_of(row, first):
    halves = []
    for at in (0, LANES):
        turned = jnp.broadcast_to(row[:, at : at + LANES], (LANES, LANES)).T
        halves.append(jnp.where(first > 0, turned[0:64], turned[64:128]))
    return jnp.concatenate(halves, axis=0)


def two_parts(state):
    high = state.astype(BF16)
    return jnp.concatenate([high, (state - high.astype(F32)).astype(BF16)], axis=1)


def twice(value):
    return jnp.concatenate([value, value], axis=1)


def spread(feature, cosine, sine):
    return jnp.concatenate([feature * cosine, feature * sine], axis=1).astype(BF16)


def stacked_heads(value, first, second):
    return jnp.concatenate([value * first, value * second], axis=0).astype(BF16)


def rows_of(s, c, local):
    return pl.ds(pl.multiple_of(s * local + c * CHUNK, CHUNK), CHUNK)


def lanes_of(p):
    return pl.ds(pl.multiple_of(p * LANES, LANES), LANES)


def fill_tables(groups, local, base, lens, cos_s, sin_s, ok_s, within):
    for s in range(groups):
        cosine, sine, valid = angles(base, lens[s], local)
        cos_s[s * local : (s + 1) * local] = cosine
        sin_s[s * local : (s + 1) * local] = sine
        if ok_s is not None:
            ok_s[s * local : (s + 1) * local] = valid
        within[s] = weights_within(lens[s])


def meet(targets):
    barrier = pltpu.get_barrier_semaphore()
    for target in targets:
        pl.semaphore_signal(barrier, inc=1, device_id=target, device_id_type=MESH)
    pl.semaphore_wait(barrier, len(targets))


class Chain:
    def __init__(self, step, pairs, refs):
        self.at, self.parts, self.pairs = lax.axis_index("head"), lax.axis_size("head"), pairs
        self.out_state, self.out_rows, self.in_state, self.in_rows, self.send, self.recv = refs
        self.before = {"head": lax.rem(self.at + self.parts - step, self.parts)}
        self.after = {"head": lax.rem(self.at + self.parts + step, self.parts)}
        last = self.parts - 1
        self.is_first = self.at == (0 if step > 0 else last)
        self.is_last = self.at == (last if step > 0 else 0)

    def copies(self, s):
        some = pl.ds(s * self.pairs, self.pairs)
        return [
            pltpu.make_async_remote_copy(
                src_ref=src.at[some], dst_ref=dst.at[some],
                send_sem=self.send.at[s, j], recv_sem=self.recv.at[s, j],
                device_id=self.after, device_id_type=MESH,
            )
            for j, (src, dst) in enumerate(
                ((self.out_state, self.in_state), (self.out_rows, self.in_rows))
            )
        ]

    def start(self, s):
        for copy in self.copies(s):
            copy.start()

    def arrive(self, s):
        for copy in self.copies(s):
            copy.wait_recv()

    def sent(self, s):
        for copy in self.copies(s):
            copy.wait_send()


def chain_scratch(groups, pairs):
    return [
        pltpu.VMEM((groups * pairs, 128, LANES), BF16),
        pltpu.VMEM((groups * pairs, 8, 256), F32),
        pltpu.VMEM((groups * pairs, 128, LANES), BF16),
        pltpu.VMEM((groups * pairs, 8, 256), F32),
        pltpu.SemaphoreType.DMA((groups, 2)),
        pltpu.SemaphoreType.DMA((groups, 2)),
    ]


def attend_kernel(
    groups, local, lens, tok, weight, bias,
    q, k, v, joined, rest, inverse, states, rows_out,
    cos_s, sin_s, ok_s, within, own, own_rows, part, part_rows, came, came_rows, num_s, den_s, *link,
):
    width = tok.shape[1]
    pairs = width // LANES
    count = local // CHUNK
    chain = Chain(1, pairs, link)
    meet([chain.before, chain.after])
    fill_tables(groups, local, chain.at * local, lens, cos_s, sin_s, ok_s, within)

    def project(i, _):
        r = pl.ds(pl.multiple_of(i * CHUNK, CHUNK), CHUNK)
        x = tok[r]
        valid = ok_s[r]
        for piece, out in enumerate((q, k)):
            for n in range(0, width, 256):
                m = piece * width + n
                y = dot(x, weight[:, m : m + 256]) + bias[:, m : m + 256]
                out[r, n : n + 256] = (softplus(y) * twice(valid)).astype(BF16)
        for n in range(0, width, 256):
            m = 2 * width + n
            v[r, n : n + 256] = (dot(x, weight[:, m : m + 256]) + bias[:, m : m + 256]).astype(BF16)
        return 0

    def sums(i, _):
        s, p = i // pairs, i % pairs
        mask = block_mask(256, LANES)
        total = jnp.zeros((256, LANES), F32)
        row = jnp.zeros((1, 256), F32)
        for c in range(count):
            r, n = rows_of(s, c, local), lanes_of(p)
            k2 = spread(k[r, n].astype(F32), cos_s[r], sin_s[r])
            total = total + tdot(k2, v[r, n])
            row = row + column_sum(k2.astype(F32))
            if c + 1 < count:
                part[i * (count - 1) + c] = pack(total * mask)
                part_rows[i * (count - 1) + c] = jnp.broadcast_to(row, (8, 256))
        own[i] = pack(total * mask)
        own_rows[i] = jnp.broadcast_to(row, (8, 256))
        came[i] = jnp.zeros((128, LANES), F32)
        came_rows[i] = jnp.zeros((8, 256), F32)
        return 0

    def arrive(s):
        chain.arrive(s)

        def one(p, _):
            i = s * pairs + p
            rows = chain.in_rows[i]
            column = column_of(rows[0:1], head_masks()[0])
            came[i] = chain.in_state[i].astype(F32) + column * rows[1:2, 0:LANES]
            came_rows[i] = rows
            return 0

        lax.fori_loop(0, pairs, one, 0)

    def leave(s):
        def one(p, _):
            i = s * pairs + p
            total = came[i] + own[i]
            row = came_rows[i][0:1] + own_rows[i][0:1]
            column = column_of(row, head_masks()[0])
            centre = column_sum(total) / jnp.maximum(column_sum(column), 1e-30)
            centre = centre.astype(BF16).astype(F32)
            chain.out_state[i] = (total - column * centre).astype(BF16)
            chain.out_rows[i] = jnp.concatenate([row, twice(centre), jnp.zeros((6, 256), F32)], axis=0)
            return 0

        lax.fori_loop(0, pairs, one, 0)
        chain.start(s)

    def intra(i, _):
        s, p = i // pairs, i % pairs
        n = lanes_of(p)
        first, second, _, _ = head_masks()
        ones = jnp.ones((CHUNK, LANES), BF16)
        m = within[s]
        m = jnp.concatenate([m, m], axis=0)
        for c in range(count):
            r = rows_of(s, c, local)
            scores = dot_t(stacked_heads(q[r, n].astype(F32), first, second), k[r, n])
            inner = dot((scores * m).astype(BF16), jnp.concatenate([v[r, n], ones], axis=1))
            both = jnp.where(twice(first) > 0, inner[:CHUNK], inner[CHUNK:])
            num_s[r, n] = both[:, :LANES]
            den_s[r, n] = both[:, LANES:]
        return 0

    def inter(i, _):
        s, p = i // pairs, i % pairs
        n = lanes_of(p)
        mask = block_mask(256, LANES)
        ones = block_mask(LANES, LANES).astype(BF16)
        for c in range(count):
            r = rows_of(s, c, local)
            state, row = came[i], came_rows[i][0:1]
            if c > 0:
                state = state + part[i * (count - 1) + c - 1]
                row = row + part_rows[i * (count - 1) + c - 1][0:1]
            state = two_parts(unpack(state, mask))
            states[i * count + c] = state
            rows_out[i * count + c] = jnp.broadcast_to(row, (8, 256))
            q2 = spread(q[r, n].astype(F32), cos_s[r], sin_s[r])
            both = dot(q2, state)
            num = both[:, :LANES] + both[:, LANES:] + num_s[r, n]
            weighed = q2.astype(F32) * row
            weighed = (weighed[:, :LANES] + weighed[:, LANES:]).astype(BF16)
            den = dot(weighed, ones) + den_s[r, n]
            above = 1.0 / jnp.maximum(den, 1.0)
            attended = num * above
            rounded = attended.astype(BF16)
            joined[r, n] = rounded
            rest[r, n] = (attended - rounded.astype(F32)).astype(BF16)
            inverse[r, n] = jnp.where(den > 1.0, above, -1.0).astype(BF16)
        return 0

    lax.fori_loop(0, groups * count, project, 0)
    lax.fori_loop(0, groups * pairs, sums, 0)

    @pl.when(chain.is_first)
    def _():
        for s in range(groups):
            leave(s)

    lax.fori_loop(0, groups * pairs, intra, 0)

    @pl.when(jnp.logical_not(chain.is_first))
    def _():
        for s in range(groups):
            arrive(s)

            @pl.when(jnp.logical_not(chain.is_last))
            def _():
                leave(s)

    lax.fori_loop(0, groups * pairs, inter, 0)

    @pl.when(jnp.logical_not(chain.is_last))
    def _():
        for s in range(groups):
            chain.sent(s)


def gelu_both(x):
    z = jnp.abs(x) * (1.0 / math.sqrt(2.0))
    t = 1.0 / (1.0 + 0.3275911 * z)
    e = jnp.exp(-0.5 * x * x)
    poly = t * (
        0.254829592 + t * (-0.284496736 + t * (1.421413741 + t * (-1.453152027 + t * 1.061405429)))
    )
    tail = 0.5 * poly * e
    phi = jnp.where(x >= 0, 1.0 - tail, tail)
    return x * phi, phi + x * e * (1.0 / math.sqrt(2.0 * math.pi))


def mean_of(x):
    return jnp.mean(x, axis=1, keepdims=True)


def column_sum(x):
    return jnp.sum(x, axis=0, keepdims=True)


def normalised(x):
    centred = x - mean_of(x)
    inv = lax.rsqrt(mean_of(centred * centred) + 1e-05)
    return centred * inv, inv


def feed_kernel(
    tok, joined, cot, w_out, w_up, w_down, b_out, g_one, s_one, b_up, b_down, g_two, s_two,
    act, g_first, g_joined, gw_out, gw_up, gw_down, gb_out, gg_one, gs_one, gb_up, gb_down, gg_two, gs_two,
    norm_s, low_s, hid_s, der_s, sec_s, branch_s, acc_s,
):
    rows = tok.shape[0]
    ff = w_up.shape[1]
    step = 768
    count = ff // step

    @pl.when(pl.program_id(0) == 0)
    def _():
        for ref in (gw_out, gw_up, gw_down, gb_out, gg_one, gs_one, gb_up, gb_down, gg_two, gs_two):
            ref[...] = jnp.zeros_like(ref)

    first = tok[...].astype(F32) + (dot(joined[...], w_out[...]) + b_out[...])
    unit_one, inv_one = normalised(first)
    norm_s[...] = unit_one
    normed = unit_one * g_one[...] + s_one[...]
    low_s[...] = normed.astype(BF16)
    sec_s[...] = normed + b_down[...]

    def up(j, _):
        n = pl.ds(pl.multiple_of(j * step, step), step)
        x = dot(low_s[...], w_up[:, n]) + b_up[:, n]
        y, d = gelu_both(x)
        hid_s[:, n] = y.astype(BF16)
        der_s[:, n] = d.astype(BF16)
        return 0

    lax.fori_loop(0, count, up, 0)
    second = sec_s[...] + dot(hid_s[...], w_down[...])
    unit_two, inv_two = normalised(second)
    act[...] = (unit_two * g_two[...] + s_two[...]).astype(BF16)
    c = cot[...].astype(F32)
    gg_two[...] += column_sum(c * unit_two)
    gs_two[...] += column_sum(c)
    e = c * g_two[...]
    g_second = inv_two * (e - mean_of(e) - unit_two * mean_of(e * unit_two))
    sec_s[...] = g_second
    branch = g_second.astype(BF16)
    branch_s[...] = branch
    gb_down[...] += column_sum(branch.astype(F32))

    def down(j, _):
        n = pl.ds(pl.multiple_of(j * step, step), step)
        gh = dot_t(branch_s[...], w_down[n, :])
        gu = gh * der_s[:, n].astype(F32)
        gu = gu.astype(BF16)
        der_s[:, n] = gu
        gb_up[:, n] += column_sum(gu.astype(F32))
        gw_down[n, :] += tdot(hid_s[:, n], branch_s[...])
        gw_up[:, n] += tdot(low_s[...], gu)
        return 0

    lax.fori_loop(0, count, down, 0)
    g_normed = sec_s[...] + dot_t(der_s[...], w_up[...])
    unit_one = norm_s[...]
    gg_one[...] += column_sum(g_normed * unit_one)
    gs_one[...] += column_sum(g_normed)
    e = g_normed * g_one[...]
    gf = inv_one * (e - mean_of(e) - unit_one * mean_of(e * unit_one))
    g_first[...] = gf
    go = gf.astype(BF16)
    gb_out[...] += column_sum(go.astype(F32))
    gw_out[...] += tdot(joined[...], go)
    g_joined[...] = dot_t(go, w_out[...]).astype(BF16)


def back_kernel(
    groups, local, lens, q, k, v, gj, joined, rest, inverse, states, rows_in, out,
    cos_s, sin_s, within, own, own_rows, part, part_rows, came, came_rows, gnum_s, gden_s, lane_s, *link,
):
    width = q.shape[1]
    pairs = width // LANES
    count = local // CHUNK
    chain = Chain(-1, pairs, link)
    meet([chain.before, chain.after])
    fill_tables(groups, local, chain.at * local, lens, cos_s, sin_s, None, within)

    def sums(i, _):
        s, p = i // pairs, i % pairs
        n = lanes_of(p)
        _, _, one, two = head_masks()
        mask = block_mask(256, LANES)
        ones = block_mask(2 * LANES, LANES).astype(BF16)
        total = jnp.zeros((256, LANES), F32)
        row = jnp.zeros((1, 256), F32)
        for c in reversed(range(count)):
            r = rows_of(s, c, local)
            ri = inverse[r, n].astype(F32)
            gnum = (gj[r, n].astype(F32) * jnp.abs(ri)).astype(BF16)
            product = gnum.astype(F32) * (joined[r, n].astype(F32) + rest[r, n].astype(F32))
            gden = jnp.where(ri > 0, -dot(two_parts(product), ones), 0.0)
            high = gden.astype(BF16).astype(F32)
            gnum_s[r, n] = gnum
            gden_s[r, n] = gden
            lane_s[r, n] = (high * one + (gden - high) * two).astype(BF16)
            q2 = spread(q[r, n].astype(F32), cos_s[r], sin_s[r])
            total = total + tdot(q2, gnum)
            row = row + column_sum(q2.astype(F32) * twice(gden))
            if c > 0:
                part[i * (count - 1) + c - 1] = pack(total * mask)
                part_rows[i * (count - 1) + c - 1] = jnp.broadcast_to(row, (8, 256))
        own[i] = pack(total * mask)
        own_rows[i] = jnp.broadcast_to(row, (8, 256))
        came[i] = jnp.zeros((128, LANES), F32)
        came_rows[i] = jnp.zeros((8, 256), F32)
        return 0

    def arrive(s):
        chain.arrive(s)

        def one(p, _):
            i = s * pairs + p
            came[i] = chain.in_state[i].astype(F32)
            came_rows[i] = chain.in_rows[i]
            return 0

        lax.fori_loop(0, pairs, one, 0)

    def leave(s):
        def one(p, _):
            i = s * pairs + p
            n = lanes_of(p)
            total = came[i] + own[i]
            low = total.astype(BF16)
            chain.out_state[i] = low
            lost = unpack(total - low.astype(F32), block_mask(256, LANES)).astype(BF16)
            mean = column_sum(v[pl.ds(s * local, local), n].astype(F32)) * (1.0 / local)
            row = dot_t(jnp.broadcast_to(mean, (8, LANES)).astype(BF16), lost)
            chain.out_rows[i] = came_rows[i] + own_rows[i] + row
            return 0

        lax.fori_loop(0, pairs, one, 0)
        chain.start(s)

    def main(i, _):
        s, p = i // pairs, i % pairs
        n = lanes_of(p)
        first, second, one, two = head_masks()
        mask = block_mask(256, LANES)
        ones = jnp.ones((CHUNK, LANES), BF16)
        m = within[s]
        m = jnp.concatenate([m, m], axis=0)
        for c in range(count):
            r = rows_of(s, c, local)
            cosine, sine = cos_s[r], sin_s[r]
            feature, key, value = q[r, n].astype(F32), k[r, n], v[r, n]
            gnum, gden, lane = gnum_s[r, n], gden_s[r, n], lane_s[r, n].astype(F32)
            row = rows_in[i * count + c][0:1]
            outer = dot_t(twice(gnum), states[i * count + c]) + twice(gden) * row
            gq = outer[:, :LANES] * cosine + outer[:, LANES:] * sine
            heads = stacked_heads(feature, first, second)
            scores = (dot_t(heads, key) * m).astype(BF16)
            gheads = stacked_heads(gnum.astype(F32), first, second)
            left = jnp.concatenate([gheads, stacked_heads(lane, first, second)], axis=1)
            g = (dot_t(left, jnp.concatenate([value, ones], axis=1)) * m).astype(BF16)
            inner = dot(g, key)
            gq = gq + jnp.where(first > 0, inner[:CHUNK], inner[CHUNK:])
            state, row = came[i], came_rows[i][0:1]
            if c + 1 < count:
                state = state + part[i * (count - 1) + c]
                row = row + part_rows[i * (count - 1) + c][0:1]
            state = two_parts(unpack(state, mask))
            k2 = spread(key.astype(F32), cosine, sine)
            gv = dot(k2, state[:, :LANES]) + tdot(gheads, scores).T
            outer = dot_t(twice(value), state) + row
            gk = outer[:, :LANES] * cosine + outer[:, LANES:] * sine + tdot(heads, g).T
            out[r, n] = (gq * slope(feature)).astype(BF16)
            out[r, pl.ds(pl.multiple_of(width + p * LANES, LANES), LANES)] = (
                gk * slope(key.astype(F32))
            ).astype(BF16)
            out[r, pl.ds(pl.multiple_of(2 * width + p * LANES, LANES), LANES)] = gv.astype(BF16)
        return 0

    lax.fori_loop(0, groups * pairs, sums, 0)

    @pl.when(chain.is_first)
    def _():
        for s in range(groups):
            leave(s)

    @pl.when(jnp.logical_not(chain.is_first))
    def _():
        for s in range(groups):
            arrive(s)

            @pl.when(jnp.logical_not(chain.is_last))
            def _():
                leave(s)

    lax.fori_loop(0, groups * pairs, main, 0)

    @pl.when(jnp.logical_not(chain.is_last))
    def _():
        for s in range(groups):
            chain.sent(s)


def input_kernel(tok, gm, weight, g_first, grad, gw, gb):
    @pl.when(pl.program_id(0) == 0)
    def _():
        gw[...] = jnp.zeros_like(gw)
        gb[...] = jnp.zeros_like(gb)

    low = gm[...]
    gb[...] += column_sum(low.astype(F32))
    gw[...] += tdot(tok[...], low)
    grad[...] = g_first[...] + dot_t(low, weight[...])


def peers():
    dp, z = lax.axis_index("dp"), lax.axis_index("head")
    core, x, y = lax.rem(dp, 2), lax.rem(dp // 2, 2), dp // 4
    twin = dp + 1 - 2 * core
    along_x, along_y = dp + 2 - 4 * x, dp + 4 - 8 * y
    one = along_x + core * (along_y - along_x)
    two = along_y + core * (along_x - along_y)
    return dp, z, twin, one, two, one + two - dp


class Copies:
    def __init__(self, send, recv):
        self.send, self.recv, self.all = send, recv, []

    def start(self, a, slot, src, dst, target):
        copy = pltpu.make_async_remote_copy(
            src_ref=src, dst_ref=dst, send_sem=self.send.at[a, slot], recv_sem=self.recv.at[a, slot],
            device_id=target, device_id_type=MESH,
        )
        copy.start()
        self.all.append(copy)
        return copy

    def finish(self):
        for copy in self.all:
            copy.wait_send()


class Gather:
    def __init__(self, ins, outs, local, send, recv):
        self.ins, self.outs, self.local = ins, outs, local
        self.copies, self.had = Copies(send, recv), {}
        self.dp, self.z, twin, one, two, self.far = peers()
        self.one, self.two = one, two
        self.to_z = [{"dp": self.dp, "head": lax.rem(self.z + k, 4)} for k in (1, 2, 3)]
        self.to_twin, self.to_one, self.to_two = (
            {"dp": d, "head": self.z} for d in (twin, one, two)
        )

    def targets(self):
        return self.to_z + [self.to_twin, self.to_one, self.to_two]

    def own(self, a):
        return pltpu.make_async_copy(self.ins[a], self.outs[a].at[self.dp * 4 + self.z], self.local.at[a])

    def begin(self, a):
        self.own(a).start()
        for k in range(3):
            place = self.outs[a].at[self.dp * 4 + self.z]
            self.had[a, k] = self.copies.start(a, k, self.ins[a], place, self.to_z[k])

    def pass_on(self, a, slot, block, target):
        ref = self.outs[a].at[pl.ds(block * 4, 4)]
        self.had[a, slot] = self.copies.start(a, slot, ref, ref, target)

    def stage(self, a, step):
        if step == 0:
            self.own(a).wait()
            for k in range(3):
                self.had[a, k].wait_recv()
            self.pass_on(a, 3, self.dp, self.to_one)
            self.pass_on(a, 4, self.dp, self.to_two)
            self.pass_on(a, 5, self.dp, self.to_twin)
        elif step == 1:
            self.had[a, 3].wait_recv()
            self.pass_on(a, 6, self.one, self.to_two)
            self.pass_on(a, 7, self.one, self.to_twin)
        elif step == 2:
            self.had[a, 4].wait_recv()
            self.pass_on(a, 8, self.two, self.to_twin)
        elif step == 3:
            self.had[a, 6].wait_recv()
            self.pass_on(a, 9, self.far, self.to_twin)
        elif step == 4:
            for slot in (5, 7, 8, 9):
                self.had[a, slot].wait_recv()

    def finish(self):
        self.copies.finish()


def gather_kernel(n, *refs):
    ins, outs = refs[:n], refs[n : 2 * n]
    work = Gather(ins, outs, *refs[2 * n :])
    meet(work.targets())
    for a in range(n):
        work.begin(a)
    for t in range(n + 4):
        for a in range(n):
            if 0 <= t - a < 5:
                work.stage(a, t - a)
    work.finish()


def gather_all(blocks):
    n = len(blocks)
    return pl.pallas_call(
        functools.partial(gather_kernel, n),
        out_shape=[shape((32,) + item.shape, item.dtype) for item in blocks],
        in_specs=[ANY] * n,
        out_specs=[ANY] * n,
        scratch_shapes=[
            pltpu.SemaphoreType.DMA((n,)),
            pltpu.SemaphoreType.DMA((n, 10)),
            pltpu.SemaphoreType.DMA((n, 10)),
        ],
        compiler_params=params(3),
    )(*blocks)


def folded(item):
    rows, cols = item.shape
    if rows % 16 == 0:
        return item
    return jnp.concatenate([item[:, : cols // 2], item[:, cols // 2 :]], axis=0)


def unfolded(item, rows):
    n, have, cols = item.shape
    if have == rows:
        return item.reshape(n * rows, cols)
    return item.reshape(n, 2, rows, cols).transpose(0, 2, 1, 3).reshape(n * rows, 2 * cols)


class Scatter:
    def __init__(self, bufs, boxes, outs, send, recv):
        self.bufs, self.boxes, self.outs = bufs, boxes, outs
        self.copies, self.had = Copies(send, recv), {}
        self.dp, self.z, self.twin, self.one, self.two, self.far = peers()
        self.to_z = [{"dp": self.dp, "head": lax.rem(self.z + k, 4)} for k in (1, 2, 3)]
        self.to_twin, self.to_one, self.to_two = (
            {"dp": d, "head": self.z} for d in (self.twin, self.one, self.two)
        )

    def targets(self):
        return self.to_z + [self.to_twin, self.to_one, self.to_two]

    def block(self, a, dp):
        return self.bufs[a].at[pl.ds(dp * 4, 4)]

    def begin(self, a):
        shift = self.twin - self.dp
        for slot, dp in enumerate((self.far, self.two, self.one, self.dp)):
            other = (self.far, self.one, self.two, self.dp)[slot] + shift
            self.had[a, slot] = self.copies.start(
                a, slot, self.block(a, other), self.boxes[a].at[pl.ds(slot * 4, 4)], self.to_twin
            )

    def add(self, a, dp, slots):
        buf, box = self.bufs[a], self.boxes[a]

        def one(j, _):
            total = buf[dp * 4 + j].astype(F32)
            for slot in slots:
                total = total + box[slot * 4 + j].astype(F32)
            buf[dp * 4 + j] = total.astype(BF16)
            return 0

        lax.fori_loop(0, 4, one, 0)

    def stage(self, a, step):
        box = self.boxes[a]
        if step == 0:
            self.had[a, 0].wait_recv()
            self.add(a, self.far, (0,))
            self.had[a, 4] = self.copies.start(a, 4, self.block(a, self.far), box.at[pl.ds(16, 4)], self.to_two)
            self.had[a, 1].wait_recv()
            self.add(a, self.two, (1,))
            self.had[a, 5] = self.copies.start(a, 5, self.block(a, self.two), box.at[pl.ds(20, 4)], self.to_two)
        elif step == 1:
            self.had[a, 2].wait_recv()
            self.had[a, 4].wait_recv()
            self.add(a, self.one, (2, 4))
            self.had[a, 6] = self.copies.start(a, 6, self.block(a, self.one), box.at[pl.ds(24, 4)], self.to_one)
        elif step == 2:
            for slot in (3, 5, 6):
                self.had[a, slot].wait_recv()
            self.add(a, self.dp, (3, 5, 6))
            for k in range(3):
                src = self.bufs[a].at[self.dp * 4 + lax.rem(self.z + k + 1, 4)]
                self.had[a, 7 + k] = self.copies.start(a, 7 + k, src, box.at[28 + k], self.to_z[k])
        elif step == 3:
            for k in range(3):
                self.had[a, 7 + k].wait_recv()
            total = self.bufs[a][self.dp * 4 + self.z].astype(F32)
            for k in range(3):
                total = total + box[28 + k].astype(F32)
            out = self.outs[a]
            rows, cols = total.shape
            if out.shape[0] == rows:
                out[...] = total
            else:
                out[:, :cols] = total[: rows // 2]
                out[:, cols:] = total[rows // 2 :]

    def finish(self):
        self.copies.finish()


class Total:
    def __init__(self, scatter, value, box, send, recv):
        self.value, self.box, self.to = value, box, scatter
        self.copies, self.had = Copies(send, recv), {}

    def pass_on(self, slot, target):
        self.had[slot] = self.copies.start(0, slot, self.value.at[slot if slot < 3 else 3], self.box.at[slot], target)

    def stage(self, step):
        value, box = self.value, self.box
        targets = (self.to.to_twin, self.to.to_two, self.to.to_one)
        if step > 0 and step < 4:
            self.had[step - 1].wait_recv()
            value[step] = value[step - 1] + box[step - 1]
        if step < 3:
            self.pass_on(step, targets[step])
        elif step == 3:
            for k in range(3):
                self.pass_on(3 + k, self.to.to_z[k])
        elif step == 4:
            for k in range(3):
                self.had[3 + k].wait_recv()
            value[4] = (value[3] + box[3]) + (box[4] + box[5])

    def finish(self):
        self.copies.finish()


def scatter_kernel(n, *refs):
    ins, small, outs, small_out = refs[:n], refs[n], refs[n + 1 : 2 * n + 1], refs[2 * n + 1]
    bufs, boxes = refs[2 * n + 2 : 3 * n + 2], refs[3 * n + 2 : 4 * n + 2]
    value, box, local, send, recv, small_send, small_recv = refs[4 * n + 2 :]
    work = Scatter(bufs, boxes, outs, send, recv)
    total = Total(work, value, box, small_send, small_recv)
    loads = [pltpu.make_async_copy(ins[a], bufs[a], local.at[a]) for a in range(n)]
    for load in loads:
        load.start()
    meet(work.targets())
    value[0] = small[...]
    for a in range(n):
        loads[a].wait()
        work.begin(a)
    for t in range(max(n + 3, 5)):
        if t < 5:
            total.stage(t)
        for a in range(n):
            if 0 <= t - a < 4:
                work.stage(a, t - a)
    small_out[...] = value[4]
    work.finish()
    total.finish()


def scatter_all(terms, small, places):
    n = len(terms)
    return pl.pallas_call(
        functools.partial(scatter_kernel, n),
        out_shape=[shape(place, F32) for place in places] + [shape(small.shape, F32)],
        in_specs=[ANY] * n + [VMEM],
        out_specs=[VMEM] * (n + 1),
        scratch_shapes=[pltpu.VMEM(item.shape, BF16) for item in terms]
        + [pltpu.VMEM((31,) + item.shape[1:], BF16) for item in terms]
        + [
            pltpu.VMEM((5,) + small.shape, F32),
            pltpu.VMEM((6,) + small.shape, F32),
            pltpu.SemaphoreType.DMA((n,)),
            pltpu.SemaphoreType.DMA((n, 10)),
            pltpu.SemaphoreType.DMA((n, 10)),
            pltpu.SemaphoreType.DMA((1, 6)),
            pltpu.SemaphoreType.DMA((1, 6)),
        ],
        compiler_params=params(4),
    )(*terms, small)


VMEM = pl.BlockSpec(memory_space=pltpu.VMEM)
SMEM = pl.BlockSpec(memory_space=pltpu.SMEM)
ANY = pl.BlockSpec(memory_space=pl.ANY)


def params(collective=None):
    if collective is None:
        return pltpu.CompilerParams(vmem_limit_bytes=BIG)
    return pltpu.CompilerParams(vmem_limit_bytes=BIG, collective_id=collective, has_side_effects=True)


def shape(dims, kind=BF16):
    return jax.ShapeDtypeStruct(dims, kind)


def shards(
    tokens, lengths, weight_in, bias_in, weight_out, bias_out, gain_one, shift_one,
    weight_up, bias_up, weight_down, bias_down, gain_two, shift_two, cotangent,
):
    groups, local, width = tokens.shape
    rows = groups * local
    pairs = width // LANES
    count = local // CHUNK
    axes = ("dp", "head")
    parts = lax.axis_size("head")
    me = lax.axis_index("head")

    by_kernel = lax.axis_size("dp") == 8 and parts == 4
    small = (bias_in, bias_out, gain_one, shift_one, bias_up, bias_down, gain_two, shift_two)
    if by_kernel:
        blocks = [folded(item.astype(BF16)) for item in (weight_in, weight_out, weight_up, weight_down)]
        slab = jnp.stack([jnp.pad(item.astype(BF16), (0, LANES - item.shape[0])) for item in small] * 2)
        *full, slabs = gather_all(blocks + [slab])
        w_in, w_out, w_up, w_down = (
            unfolded(item, own.shape[0])
            for item, own in zip(full, (weight_in, weight_out, weight_up, weight_down))
        )
        vectors = [slabs[:, j, : item.shape[0]] for j, item in enumerate(small)]
    else:

        def gather(item):
            return lax.all_gather(item.astype(BF16), axes, axis=0, tiled=True)

        w_in, w_out, w_up, w_down = map(gather, (weight_in, weight_out, weight_up, weight_down))
        sizes = [item.shape[0] for item in small]
        gathered = lax.all_gather(jnp.concatenate([item.astype(BF16) for item in small]), axes, axis=0)
        cuts = [sum(sizes[:i]) for i in range(len(sizes) + 1)]
        vectors = [gathered[:, a:b] for a, b in zip(cuts, cuts[1:])]
    b_in, b_out, g_one, s_one, b_up, b_down, g_two, s_two = (
        item.reshape(1, -1).astype(F32) for item in vectors
    )
    ff = w_up.shape[1]
    tok = tokens.reshape(rows, width)
    table = pltpu.VMEM((rows, LANES), F32)
    plane = shape((rows, width))
    units = groups * pairs

    def sums_scratch():
        return [
            pltpu.VMEM((units, 128, LANES), F32),
            pltpu.VMEM((units, 8, 256), F32),
            pltpu.VMEM((units * max(count - 1, 1), 128, LANES), F32),
            pltpu.VMEM((units * max(count - 1, 1), 8, 256), F32),
            pltpu.VMEM((units, 128, LANES), F32),
            pltpu.VMEM((units, 8, 256), F32),
        ]

    within = pltpu.VMEM((groups, CHUNK, CHUNK), F32)
    tall = pltpu.VMEM((rows, width), F32)
    q, k, v, joined, rest, inverse, states, state_rows = pl.pallas_call(
        functools.partial(attend_kernel, groups, local),
        out_shape=(plane,) * 6 + (shape((units * count, 256, 256)), shape((units * count, 8, 256), F32)),
        in_specs=[SMEM, VMEM, VMEM, VMEM],
        out_specs=(VMEM,) * 8,
        scratch_shapes=[table, table, table, within] + sums_scratch() + [tall, tall] + chain_scratch(groups, pairs),
        compiler_params=params(1),
    )(lengths, tok, w_in, b_in)

    tile = local

    def block(cols):
        return pl.BlockSpec((tile, cols), lambda i: (i, 0))

    def fixed(*dims):
        return pl.BlockSpec(dims, lambda i: (0,) * len(dims), pipeline_mode=pl.Buffered(1))

    vectors = [fixed(1, width)] * 3 + [fixed(1, ff)] + [fixed(1, width)] * 3
    weights = [fixed(width, width), fixed(width, ff), fixed(ff, width)]
    vector_shapes = [shape((1, width), F32)] * 3 + [shape((1, ff), F32)] + [shape((1, width), F32)] * 3
    (
        activations, g_first, g_joined, gw_out, gw_up, gw_down,
        gb_out, gg_one, gs_one, gb_up, gb_down, gg_two, gs_two,
    ) = pl.pallas_call(
        feed_kernel,
        grid=(rows // tile,),
        out_shape=[plane, shape((rows, width), F32), plane]
        + [shape((width, width), F32), shape((width, ff), F32), shape((ff, width), F32)]
        + vector_shapes,
        in_specs=[block(width)] * 3 + weights + vectors,
        out_specs=[block(width)] * 3 + weights + vectors,
        scratch_shapes=[
            pltpu.VMEM((tile, width), F32),
            pltpu.VMEM((tile, width), BF16),
            pltpu.VMEM((tile, ff), BF16),
            pltpu.VMEM((tile, ff), BF16),
            pltpu.VMEM((tile, width), F32),
            pltpu.VMEM((tile, width), BF16),
            pltpu.VMEM((8, LANES), F32),
        ],
        compiler_params=params(),
    )(
        tok, joined, cotangent.reshape(rows, width), w_out, w_up, w_down,
        b_out, g_one, s_one, b_up, b_down, g_two, s_two,
    )
    g_mixed = pl.pallas_call(
        functools.partial(back_kernel, groups, local),
        out_shape=shape((rows, 3 * width)),
        in_specs=[SMEM] + [VMEM] * 9,
        out_specs=VMEM,
        scratch_shapes=[table, table, within] + sums_scratch()
        + [pltpu.VMEM((rows, width), BF16), tall, pltpu.VMEM((rows, width), BF16)] + chain_scratch(groups, pairs),
        compiler_params=params(2),
    )(lengths, q, k, v, g_joined, joined, rest, inverse, states, state_rows)
    input_grad, gw_in, gb_in = pl.pallas_call(
        input_kernel,
        grid=(rows // tile,),
        out_shape=[shape((rows, width), F32), shape((width, 3 * width), F32), shape((1, 3 * width), F32)],
        in_specs=[block(width), block(3 * width), fixed(width, 3 * width), block(width)],
        out_specs=[block(width), fixed(width, 3 * width), fixed(1, 3 * width)],
        compiler_params=params(),
    )(tok, g_mixed, w_in, g_first)

    gb_in = gb_in.reshape(-1)
    cols = [gb_in[: 2 * width], gb_in[2 * width :]] + [
        item.reshape(-1) for item in (gb_out, gg_one, gs_one, gb_up, gb_down, gg_two, gs_two)
    ]
    total = lax.axis_size(axes)
    if by_kernel:
        terms = (gw_down, gw_up, gw_out, gw_in)
        places = [(item.shape[0] // 32, item.shape[1]) for item in terms]
        cut = []
        for item in terms:
            item = item.reshape(32, -1, item.shape[1])
            cut.append(jax.vmap(folded)(item).astype(BF16))
        flat = jnp.concatenate(cols).reshape(-1, width)
        flat = jnp.pad(flat, ((0, -flat.shape[0] % 8), (0, 0)))
        gw_down, gw_up, gw_out, gw_in, flat = scatter_all(cut, flat, places)
        flat = flat.reshape(-1)
        me = lax.axis_index(axes)
        mine, at = [], 0
        for item in cols:
            size = item.shape[0] // 32
            mine.append(lax.dynamic_slice(flat, (at + me * size,), (size,)))
            at += item.shape[0]
        gb_front, gb_value, gb_out, gg_one, gs_one, gb_up, gb_down, gg_two, gs_two = mine
        return (
            activations.reshape(groups, local, width),
            input_grad.reshape(groups, local, width),
            gw_in, gb_front, gb_value, gw_out, gb_out, gg_one, gs_one,
            gw_up, gb_up, gw_down, gb_down, gg_two, gs_two,
        )

    def scatter(item):
        return lax.psum_scatter(item, axes, scatter_dimension=0, tiled=True)

    cut = [item.shape[0] // total for item in cols]
    merged = scatter(jnp.concatenate([item.reshape(total, -1) for item in cols], axis=1).reshape(-1))
    places = [sum(cut[:i]) for i in range(len(cut) + 1)]
    (gb_front, gb_value, gb_out, gg_one, gs_one, gb_up, gb_down, gg_two, gs_two) = (
        merged[a:b] for a, b in zip(places, places[1:])
    )
    return (
        activations.reshape(groups, local, width),
        input_grad.reshape(groups, local, width),
        scatter(gw_in), gb_front, gb_value, scatter(gw_out), gb_out, gg_one, gs_one,
        scatter(gw_up), gb_up, scatter(gw_down), gb_down, gg_two, gs_two,
    )


def solution(mesh):
    spread_rows = P("dp", "head", None)
    matrix = P(("dp", "head"), None)
    vector = P(("dp", "head"))
    return jax.shard_map(
        shards,
        mesh=mesh,
        in_specs=(
            spread_rows, P("dp"), matrix, vector, matrix, vector, vector, vector,
            matrix, vector, matrix, vector, vector, vector, spread_rows,
        ),
        out_specs=(
            spread_rows, spread_rows, matrix, vector, vector, matrix, vector, vector, vector,
            matrix, vector, matrix, vector, vector, vector,
        ),
        check_vma=False,
    )
```

```python
import functools
import math

import jax
import jax.numpy as jnp
from jax import lax
from jax.experimental import pallas as pl
from jax.experimental.pallas import tpu as pltpu
from jax.sharding import PartitionSpec as P

F32 = jnp.float32
BF16 = jnp.bfloat16
CHUNK = 256
LANES = 128
HALF = 64
BIG = 62 * 1024 * 1024
MESH = pl.DeviceIdType.MESH


def dot(a, b):
    return lax.dot_general(a, b, (((1,), (0,)), ((), ())), preferred_element_type=F32)


def dot_t(a, b):
    return lax.dot_general(a, b, (((1,), (1,)), ((), ())), preferred_element_type=F32)


def tdot(a, b):
    return lax.dot_general(a, b, (((0,), (0,)), ((), ())), preferred_element_type=F32)


def iota(shape, dim):
    return lax.broadcasted_iota(jnp.int32, shape, dim)


def block_mask(rows, cols):
    return ((iota((rows, cols), 0) & HALF) == (iota((rows, cols), 1) & HALF)).astype(F32)


def head_masks():
    lane = iota((1, LANES), 1)
    first = (lane < HALF).astype(F32)
    place = lane & (HALF - 1)
    return first, 1.0 - first, (place == 0).astype(F32), (place == 1).astype(F32)


def cos_poly(z):
    t = z * z
    r = -1.0 / 3628800 + t * (1.0 / 479001600)
    r = 1.0 / 40320 + t * r
    r = -1.0 / 720 + t * r
    r = 1.0 / 24 + t * r
    r = -0.5 + t * r
    return 1.0 + t * r


def sin_poly(z):
    t = z * z
    r = -1.0 / 39916800 + t * (1.0 / 6227020800)
    r = 1.0 / 362880 + t * r
    r = -1.0 / 5040 + t * r
    r = 1.0 / 120 + t * r
    r = -1.0 / 6 + t * r
    return z + z * (t * r)


def angles(start, limit, rows):
    place = iota((rows, LANES), 0) + start
    theta = jnp.minimum((0.5 * math.pi * place.astype(F32)) / limit.astype(F32), 0.5 * math.pi)
    return cos_poly(theta), sin_poly(theta), (place < limit).astype(F32)


def weights_within(limit):
    apart = iota((CHUNK, CHUNK), 0) - iota((CHUNK, CHUNK), 1)
    theta = jnp.minimum((0.5 * math.pi * apart.astype(F32)) / limit.astype(F32), 0.5 * math.pi)
    return jnp.where(apart >= 0, cos_poly(theta), 0.0)


def softplus(x):
    t = jnp.exp(-jnp.abs(x))
    tail = jnp.where(t < 1e-3, t * (1.0 - 0.5 * t), jnp.log(1.0 + t))
    return jnp.maximum(x, 0.0) + tail


def slope(feature):
    small = feature * (1.0 - feature * (0.5 - feature * (1.0 / 6)))
    return jnp.where(feature < 0.01, small, 1.0 - jnp.exp(-feature))


def pack(state):
    return jnp.concatenate([state[0:64] + state[64:128], state[128:192] + state[192:256]], axis=0)


def unpack(packed, mask):
    top, bottom = packed[0:64], packed[64:128]
    return jnp.concatenate([top, top, bottom, bottom], axis=0) * mask


def column_of(row, first):
    halves = []
    for at in (0, LANES):
        turned = jnp.broadcast_to(row[:, at : at + LANES], (LANES, LANES)).T
        halves.append(jnp.where(first > 0, turned[0:64], turned[64:128]))
    return jnp.concatenate(halves, axis=0)


def two_parts(state):
    high = state.astype(BF16)
    return jnp.concatenate([high, (state - high.astype(F32)).astype(BF16)], axis=1)


def twice(value):
    return jnp.concatenate([value, value], axis=1)


def spread(feature, cosine, sine):
    return jnp.concatenate([feature * cosine, feature * sine], axis=1).astype(BF16)


def stacked_heads(value, first, second):
    return jnp.concatenate([value * first, value * second], axis=0).astype(BF16)


def rows_of(s, c, local):
    return pl.ds(pl.multiple_of(s * local + c * CHUNK, CHUNK), CHUNK)


def lanes_of(p):
    return pl.ds(pl.multiple_of(p * LANES, LANES), LANES)


def fill_tables(groups, local, base, lens, cos_s, sin_s, ok_s, within):
    for s in range(groups):
        cosine, sine, valid = angles(base, lens[s], local)
        cos_s[s * local : (s + 1) * local] = cosine
        sin_s[s * local : (s + 1) * local] = sine
        if ok_s is not None:
            ok_s[s * local : (s + 1) * local] = valid
        within[s] = weights_within(lens[s])


def meet(targets):
    barrier = pltpu.get_barrier_semaphore()
    for target in targets:
        pl.semaphore_signal(barrier, inc=1, device_id=target, device_id_type=MESH)
    pl.semaphore_wait(barrier, len(targets))


class Chain:
    def __init__(self, step, pairs, refs):
        self.at, self.parts, self.pairs = lax.axis_index("head"), lax.axis_size("head"), pairs
        self.out_state, self.out_rows, self.in_state, self.in_rows, self.send, self.recv = refs
        self.before = {"head": lax.rem(self.at + self.parts - step, self.parts)}
        self.after = {"head": lax.rem(self.at + self.parts + step, self.parts)}
        last = self.parts - 1
        self.is_first = self.at == (0 if step > 0 else last)
        self.is_last = self.at == (last if step > 0 else 0)

    def copies(self, s):
        some = pl.ds(s * self.pairs, self.pairs)
        return [
            pltpu.make_async_remote_copy(
                src_ref=src.at[some], dst_ref=dst.at[some],
                send_sem=self.send.at[s, j], recv_sem=self.recv.at[s, j],
                device_id=self.after, device_id_type=MESH,
            )
            for j, (src, dst) in enumerate(
                ((self.out_state, self.in_state), (self.out_rows, self.in_rows))
            )
        ]

    def start(self, s):
        for copy in self.copies(s):
            copy.start()

    def arrive(self, s):
        for copy in self.copies(s):
            copy.wait_recv()

    def sent(self, s):
        for copy in self.copies(s):
            copy.wait_send()


def chain_scratch(groups, pairs):
    return [
        pltpu.VMEM((groups * pairs, 128, LANES), BF16),
        pltpu.VMEM((groups * pairs, 8, 256), F32),
        pltpu.VMEM((groups * pairs, 128, LANES), BF16),
        pltpu.VMEM((groups * pairs, 8, 256), F32),
        pltpu.SemaphoreType.DMA((groups, 2)),
        pltpu.SemaphoreType.DMA((groups, 2)),
    ]


class Forward:
    def __init__(self, groups, local, lens, chain, outs, tables, sums):
        self.groups, self.local, self.lens, self.chain = groups, local, lens, chain
        self.outs, self.tables, self.sums_refs = outs, tables, sums
        self.pairs = outs[0].shape[1] // LANES
        self.count = local // CHUNK

    def prepare(self):
        cos_s, sin_s, ok_s, within = self.tables[:4]
        fill_tables(self.groups, self.local, self.chain.at * self.local, self.lens, cos_s, sin_s, ok_s, within)

    def project(self, piece, tok, weight, bias):
        out, ok_s, width = self.outs[piece], self.tables[2], tok.shape[1]

        def body(i, _):
            r = pl.ds(pl.multiple_of(i * CHUNK, CHUNK), CHUNK)
            x = tok[r]
            valid = twice(ok_s[r])
            for n in range(0, width, 256):
                m = piece * width + n
                y = dot(x, weight[:, n : n + 256]) + bias[:, m : m + 256]
                out[r, n : n + 256] = (softplus(y) * valid if piece < 2 else y).astype(BF16)
            return 0

        lax.fori_loop(0, self.groups * self.count, body, 0)

    def over(self, step, s=None):
        low, high = (0, self.groups) if s is None else (s, s + 1)
        lax.fori_loop(low * self.pairs, high * self.pairs, step, 0)

    def names(self):
        return (self.local, self.pairs, self.count, self.chain) + tuple(self.outs) + tuple(self.tables) + tuple(self.sums_refs)

    def steps(self):
        (
            local, pairs, count, chain, q, k, v, joined, rest, inverse, states, rows_out,
            cos_s, sin_s, ok_s, within, num_s, den_s, own, own_rows, part, part_rows, came, came_rows,
        ) = self.names()

        def sums(i, _):
            s, p = i // pairs, i % pairs
            mask = block_mask(256, LANES)
            total = jnp.zeros((256, LANES), F32)
            row = jnp.zeros((1, 256), F32)
            for c in range(count):
                r, n = rows_of(s, c, local), lanes_of(p)
                k2 = spread(k[r, n].astype(F32), cos_s[r], sin_s[r])
                total = total + tdot(k2, v[r, n])
                row = row + column_sum(k2.astype(F32))
                if c + 1 < count:
                    part[i * (count - 1) + c] = pack(total * mask)
                    part_rows[i * (count - 1) + c] = jnp.broadcast_to(row, (8, 256))
            own[i] = pack(total * mask)
            own_rows[i] = jnp.broadcast_to(row, (8, 256))
            came[i] = jnp.zeros((128, LANES), F32)
            came_rows[i] = jnp.zeros((8, 256), F32)
            return 0

        def arrive(s):
            chain.arrive(s)

            def one(p, _):
                i = s * pairs + p
                rows = chain.in_rows[i]
                column = column_of(rows[0:1], head_masks()[0])
                came[i] = chain.in_state[i].astype(F32) + column * rows[1:2, 0:LANES]
                came_rows[i] = rows
                return 0

            lax.fori_loop(0, pairs, one, 0)

        def leave(s):
            def one(p, _):
                i = s * pairs + p
                total = came[i] + own[i]
                row = came_rows[i][0:1] + own_rows[i][0:1]
                column = column_of(row, head_masks()[0])
                centre = column_sum(total) / jnp.maximum(column_sum(column), 1e-30)
                centre = centre.astype(BF16).astype(F32)
                chain.out_state[i] = (total - column * centre).astype(BF16)
                chain.out_rows[i] = jnp.concatenate([row, twice(centre), jnp.zeros((6, 256), F32)], axis=0)
                return 0

            lax.fori_loop(0, pairs, one, 0)
            chain.start(s)

        def intra(i, _):
            s, p = i // pairs, i % pairs
            n = lanes_of(p)
            first, second, _, _ = head_masks()
            ones = jnp.ones((CHUNK, LANES), BF16)
            m = within[s]
            m = jnp.concatenate([m, m], axis=0)
            for c in range(count):
                r = rows_of(s, c, local)
                scores = dot_t(stacked_heads(q[r, n].astype(F32), first, second), k[r, n])
                inner = dot((scores * m).astype(BF16), jnp.concatenate([v[r, n], ones], axis=1))
                both = jnp.where(twice(first) > 0, inner[:CHUNK], inner[CHUNK:])
                num_s[r, n] = both[:, :LANES]
                den_s[r, n] = both[:, LANES:]
            return 0

        def inter(i, _):
            s, p = i // pairs, i % pairs
            n = lanes_of(p)
            mask = block_mask(256, LANES)
            ones = block_mask(LANES, LANES).astype(BF16)
            for c in range(count):
                r = rows_of(s, c, local)
                state, row = came[i], came_rows[i][0:1]
                if c > 0:
                    state = state + part[i * (count - 1) + c - 1]
                    row = row + part_rows[i * (count - 1) + c - 1][0:1]
                state = two_parts(unpack(state, mask))
                states[i * count + c] = state
                rows_out[i * count + c] = jnp.broadcast_to(row, (8, 256))
                q2 = spread(q[r, n].astype(F32), cos_s[r], sin_s[r])
                both = dot(q2, state)
                num = both[:, :LANES] + both[:, LANES:] + num_s[r, n]
                weighed = q2.astype(F32) * row
                weighed = (weighed[:, :LANES] + weighed[:, LANES:]).astype(BF16)
                den = dot(weighed, ones) + den_s[r, n]
                above = 1.0 / jnp.maximum(den, 1.0)
                attended = num * above
                rounded = attended.astype(BF16)
                joined[r, n] = rounded
                rest[r, n] = (attended - rounded.astype(F32)).astype(BF16)
                inverse[r, n] = jnp.where(den > 1.0, above, -1.0).astype(BF16)
            return 0

        return sums, arrive, leave, intra, inter


def attend_kernel(
    groups, local, lens, tok, w_q, w_k, w_v, bias,
    q, k, v, joined, rest, inverse, states, rows_out,
    cos_s, sin_s, ok_s, within, own, own_rows, part, part_rows, came, came_rows, num_s, den_s, *link,
):
    chain = Chain(1, tok.shape[1] // LANES, link)
    meet([chain.before, chain.after])
    work = Forward(
        groups, local, lens, chain, (q, k, v, joined, rest, inverse, states, rows_out),
        (cos_s, sin_s, ok_s, within, num_s, den_s), (own, own_rows, part, part_rows, came, came_rows),
    )
    work.prepare()
    for piece, weight in enumerate((w_q, w_k, w_v)):
        work.project(piece, tok, weight, bias)
    sums, arrive, leave, intra, inter = work.steps()
    work.over(sums)

    @pl.when(chain.is_first)
    def _():
        for s in range(groups):
            leave(s)

    work.over(intra)

    @pl.when(jnp.logical_not(chain.is_first))
    def _():
        for s in range(groups):
            arrive(s)

            @pl.when(jnp.logical_not(chain.is_last))
            def _():
                leave(s)

    work.over(inter)

    @pl.when(jnp.logical_not(chain.is_last))
    def _():
        for s in range(groups):
            chain.sent(s)


def gelu_both(x):
    z = jnp.abs(x) * (1.0 / math.sqrt(2.0))
    t = 1.0 / (1.0 + 0.3275911 * z)
    e = jnp.exp(-0.5 * x * x)
    poly = t * (
        0.254829592 + t * (-0.284496736 + t * (1.421413741 + t * (-1.453152027 + t * 1.061405429)))
    )
    tail = 0.5 * poly * e
    phi = jnp.where(x >= 0, 1.0 - tail, tail)
    return x * phi, phi + x * e * (1.0 / math.sqrt(2.0 * math.pi))


def mean_of(x):
    return jnp.mean(x, axis=1, keepdims=True)


def column_sum(x):
    return jnp.sum(x, axis=0, keepdims=True)


def normalised(x):
    centred = x - mean_of(x)
    inv = lax.rsqrt(mean_of(centred * centred) + 1e-05)
    return centred * inv, inv


def feed_kernel(
    tok, joined, cot, w_out, w_up, w_down, b_out, g_one, s_one, b_up, b_down, g_two, s_two,
    act, g_first, g_joined, gw_out, gw_up, gw_down, gb_out, gg_one, gs_one, gb_up, gb_down, gg_two, gs_two,
    norm_s, low_s, hid_s, der_s, sec_s, branch_s,
):
    rows = tok.shape[0]
    ff = w_up.shape[1]
    step = 768
    count = ff // step

    @pl.when(pl.program_id(0) == 0)
    def _():
        for ref in (gw_out, gw_up, gw_down, gb_out, gg_one, gs_one, gb_up, gb_down, gg_two, gs_two):
            ref[...] = jnp.zeros_like(ref)

    first = tok[...].astype(F32) + (dot(joined[...], w_out[...]) + b_out[...])
    unit_one, inv_one = normalised(first)
    norm_s[...] = unit_one
    normed = unit_one * g_one[...] + s_one[...]
    low_s[...] = normed.astype(BF16)
    sec_s[...] = normed + b_down[...]

    def up(j, _):
        n = pl.ds(pl.multiple_of(j * step, step), step)
        x = dot(low_s[...], w_up[:, n]) + b_up[:, n]
        y, d = gelu_both(x)
        hid_s[:, n] = y.astype(BF16)
        der_s[:, n] = d.astype(BF16)
        return 0

    lax.fori_loop(0, count, up, 0)
    second = sec_s[...] + dot(hid_s[...], w_down[...])
    unit_two, inv_two = normalised(second)
    act[...] = (unit_two * g_two[...] + s_two[...]).astype(BF16)
    c = cot[...].astype(F32)
    gg_two[...] += column_sum(c * unit_two)
    gs_two[...] += column_sum(c)
    e = c * g_two[...]
    g_second = inv_two * (e - mean_of(e) - unit_two * mean_of(e * unit_two))
    sec_s[...] = g_second
    branch = g_second.astype(BF16)
    branch_s[...] = branch
    gb_down[...] += column_sum(branch.astype(F32))

    def down(j, _):
        n = pl.ds(pl.multiple_of(j * step, step), step)
        gh = dot_t(branch_s[...], w_down[n, :])
        gu = gh * der_s[:, n].astype(F32)
        gu = gu.astype(BF16)
        der_s[:, n] = gu
        gb_up[:, n] += column_sum(gu.astype(F32))
        gw_down[n, :] += tdot(hid_s[:, n], branch_s[...])
        gw_up[:, n] += tdot(low_s[...], gu)
        return 0

    lax.fori_loop(0, count, down, 0)
    g_normed = sec_s[...] + dot_t(der_s[...], w_up[...])
    unit_one = norm_s[...]
    gg_one[...] += column_sum(g_normed * unit_one)
    gs_one[...] += column_sum(g_normed)
    e = g_normed * g_one[...]
    gf = inv_one * (e - mean_of(e) - unit_one * mean_of(e * unit_one))
    g_first[...] = gf
    go = gf.astype(BF16)
    gb_out[...] += column_sum(go.astype(F32))
    gw_out[...] += tdot(joined[...], go)
    g_joined[...] = dot_t(go, w_out[...]).astype(BF16)


def back_kernel(
    groups, local, lens, q, k, v, gj, joined, rest, inverse, states, rows_in, out,
    cos_s, sin_s, within, own, own_rows, part, part_rows, came, came_rows, gnum_s, gden_s, lane_s, *link,
):
    width = q.shape[1]
    pairs = width // LANES
    count = local // CHUNK
    chain = Chain(-1, pairs, link)
    meet([chain.before, chain.after])
    fill_tables(groups, local, chain.at * local, lens, cos_s, sin_s, None, within)

    def sums(i, _):
        s, p = i // pairs, i % pairs
        n = lanes_of(p)
        _, _, one, two = head_masks()
        mask = block_mask(256, LANES)
        ones = block_mask(2 * LANES, LANES).astype(BF16)
        total = jnp.zeros((256, LANES), F32)
        row = jnp.zeros((1, 256), F32)
        for c in reversed(range(count)):
            r = rows_of(s, c, local)
            ri = inverse[r, n].astype(F32)
            gnum = (gj[r, n].astype(F32) * jnp.abs(ri)).astype(BF16)
            product = gnum.astype(F32) * (joined[r, n].astype(F32) + rest[r, n].astype(F32))
            gden = jnp.where(ri > 0, -dot(two_parts(product), ones), 0.0)
            high = gden.astype(BF16).astype(F32)
            gnum_s[r, n] = gnum
            gden_s[r, n] = gden
            lane_s[r, n] = (high * one + (gden - high) * two).astype(BF16)
            q2 = spread(q[r, n].astype(F32), cos_s[r], sin_s[r])
            total = total + tdot(q2, gnum)
            row = row + column_sum(q2.astype(F32) * twice(gden))
            if c > 0:
                part[i * (count - 1) + c - 1] = pack(total * mask)
                part_rows[i * (count - 1) + c - 1] = jnp.broadcast_to(row, (8, 256))
        own[i] = pack(total * mask)
        own_rows[i] = jnp.broadcast_to(row, (8, 256))
        came[i] = jnp.zeros((128, LANES), F32)
        came_rows[i] = jnp.zeros((8, 256), F32)
        return 0

    def arrive(s):
        chain.arrive(s)

        def one(p, _):
            i = s * pairs + p
            came[i] = chain.in_state[i].astype(F32)
            came_rows[i] = chain.in_rows[i]
            return 0

        lax.fori_loop(0, pairs, one, 0)

    def leave(s):
        def one(p, _):
            i = s * pairs + p
            n = lanes_of(p)
            total = came[i] + own[i]
            low = total.astype(BF16)
            chain.out_state[i] = low
            lost = unpack(total - low.astype(F32), block_mask(256, LANES)).astype(BF16)
            mean = column_sum(v[pl.ds(s * local, local), n].astype(F32)) * (1.0 / local)
            row = dot_t(jnp.broadcast_to(mean, (8, LANES)).astype(BF16), lost)
            chain.out_rows[i] = came_rows[i] + own_rows[i] + row
            return 0

        lax.fori_loop(0, pairs, one, 0)
        chain.start(s)

    def main(i, _):
        s, p = i // pairs, i % pairs
        n = lanes_of(p)
        first, second, one, two = head_masks()
        mask = block_mask(256, LANES)
        ones = jnp.ones((CHUNK, LANES), BF16)
        m = within[s]
        m = jnp.concatenate([m, m], axis=0)
        for c in range(count):
            r = rows_of(s, c, local)
            cosine, sine = cos_s[r], sin_s[r]
            feature, key, value = q[r, n].astype(F32), k[r, n], v[r, n]
            gnum, gden, lane = gnum_s[r, n], gden_s[r, n], lane_s[r, n].astype(F32)
            row = rows_in[i * count + c][0:1]
            outer = dot_t(twice(gnum), states[i * count + c]) + twice(gden) * row
            gq = outer[:, :LANES] * cosine + outer[:, LANES:] * sine
            heads = stacked_heads(feature, first, second)
            scores = (dot_t(heads, key) * m).astype(BF16)
            gheads = stacked_heads(gnum.astype(F32), first, second)
            left = jnp.concatenate([gheads, stacked_heads(lane, first, second)], axis=1)
            g = (dot_t(left, jnp.concatenate([value, ones], axis=1)) * m).astype(BF16)
            inner = dot(g, key)
            gq = gq + jnp.where(first > 0, inner[:CHUNK], inner[CHUNK:])
            state, row = came[i], came_rows[i][0:1]
            if c + 1 < count:
                state = state + part[i * (count - 1) + c]
                row = row + part_rows[i * (count - 1) + c][0:1]
            state = two_parts(unpack(state, mask))
            k2 = spread(key.astype(F32), cosine, sine)
            gv = dot(k2, state[:, :LANES]) + tdot(gheads, scores).T
            outer = dot_t(twice(value), state) + row
            gk = outer[:, :LANES] * cosine + outer[:, LANES:] * sine + tdot(heads, g).T
            out[r, n] = (gq * slope(feature)).astype(BF16)
            out[r, pl.ds(pl.multiple_of(width + p * LANES, LANES), LANES)] = (
                gk * slope(key.astype(F32))
            ).astype(BF16)
            out[r, pl.ds(pl.multiple_of(2 * width + p * LANES, LANES), LANES)] = gv.astype(BF16)
        return 0

    lax.fori_loop(0, groups * pairs, sums, 0)

    @pl.when(chain.is_first)
    def _():
        for s in range(groups):
            leave(s)

    @pl.when(jnp.logical_not(chain.is_first))
    def _():
        for s in range(groups):
            arrive(s)

            @pl.when(jnp.logical_not(chain.is_last))
            def _():
                leave(s)

    lax.fori_loop(0, groups * pairs, main, 0)

    @pl.when(jnp.logical_not(chain.is_last))
    def _():
        for s in range(groups):
            chain.sent(s)


def input_kernel(tok, gm, weight, g_first, grad, gw, gb):
    @pl.when(pl.program_id(0) == 0)
    def _():
        gw[...] = jnp.zeros_like(gw)
        gb[...] = jnp.zeros_like(gb)

    low = gm[...]
    gb[...] += column_sum(low.astype(F32))
    gw[...] += tdot(tok[...], low)
    grad[...] = g_first[...] + dot_t(low, weight[...])


def peers():
    dp, z = lax.axis_index("dp"), lax.axis_index("head")
    core, x, y = lax.rem(dp, 2), lax.rem(dp // 2, 2), dp // 4
    twin = dp + 1 - 2 * core
    along_x, along_y = dp + 2 - 4 * x, dp + 4 - 8 * y
    one = along_x + core * (along_y - along_x)
    two = along_y + core * (along_x - along_y)
    return dp, z, twin, one, two, one + two - dp


class Copies:
    def __init__(self, send, recv):
        self.send, self.recv, self.all = send, recv, []

    def start(self, a, slot, src, dst, target):
        copy = pltpu.make_async_remote_copy(
            src_ref=src, dst_ref=dst, send_sem=self.send.at[a, slot], recv_sem=self.recv.at[a, slot],
            device_id=target, device_id_type=MESH,
        )
        copy.start()
        self.all.append(copy)
        return copy

    def finish(self):
        for copy in self.all:
            copy.wait_send()


class Gather:
    def __init__(self, arrays, send, recv):
        self.arrays = arrays
        self.copies, self.had = Copies(send, recv), {}
        self.dp, self.z, twin, one, two, self.far = peers()
        self.me = self.dp * 4 + self.z
        self.one, self.two = one, two
        self.to_z = [{"dp": self.dp, "head": lax.rem(self.z + k, 4)} for k in (1, 2, 3)]
        self.to_twin, self.to_one, self.to_two = (
            {"dp": d, "head": self.z} for d in (twin, one, two)
        )

    def targets(self):
        return self.to_z + [self.to_twin, self.to_one, self.to_two]

    def begin(self, a):
        ref, low, rows = self.arrays[a]
        place = ref.at[self.me, pl.ds(low, rows)]
        for k in range(3):
            self.had[a, k] = self.copies.start(a, k, place, place, self.to_z[k])

    def pass_on(self, a, slot, block, target):
        ref, low, rows = self.arrays[a]
        place = ref.at[pl.ds(block * 4, 4), pl.ds(low, rows)]
        self.had[a, slot] = self.copies.start(a, slot, place, place, target)

    def stage(self, a, step):
        if step == 0:
            for k in range(3):
                self.had[a, k].wait_recv()
            self.pass_on(a, 3, self.dp, self.to_one)
            self.pass_on(a, 4, self.dp, self.to_two)
            self.pass_on(a, 5, self.dp, self.to_twin)
        elif step == 1:
            self.had[a, 3].wait_recv()
            self.pass_on(a, 6, self.one, self.to_two)
            self.pass_on(a, 7, self.one, self.to_twin)
        elif step == 2:
            self.had[a, 4].wait_recv()
            self.pass_on(a, 8, self.two, self.to_twin)
        elif step == 3:
            self.had[a, 6].wait_recv()
            self.pass_on(a, 9, self.far, self.to_twin)
        elif step == 4:
            for slot in (5, 7, 8, 9):
                self.had[a, slot].wait_recv()

    def finish(self):
        self.copies.finish()


class Scatter:
    def __init__(self, bufs, boxes, outs, send, recv, place=lambda dp: dp * 4):
        self.bufs, self.boxes, self.outs, self.place = bufs, boxes, outs, place
        self.copies, self.had = Copies(send, recv), {}
        self.dp, self.z, self.twin, self.one, self.two, self.far = peers()
        self.to_z = [{"dp": self.dp, "head": lax.rem(self.z + k, 4)} for k in (1, 2, 3)]
        self.to_twin, self.to_one, self.to_two = (
            {"dp": d, "head": self.z} for d in (self.twin, self.one, self.two)
        )

    def targets(self):
        return self.to_z + [self.to_twin, self.to_one, self.to_two]

    def block(self, a, dp):
        return self.bufs[a].at[pl.ds(self.place(dp), 4)]

    def begin(self, a):
        shift = self.twin - self.dp
        for slot, dp in enumerate((self.far, self.two, self.one, self.dp)):
            other = (self.far, self.one, self.two, self.dp)[slot] + shift
            self.had[a, slot] = self.copies.start(
                a, slot, self.block(a, other), self.boxes[a].at[pl.ds(slot * 4, 4)], self.to_twin
            )

    def add(self, a, dp, slots):
        buf, box = self.bufs[a], self.boxes[a]
        start = self.place(dp)

        def one(j, _):
            total = buf[start + j].astype(F32)
            for slot in slots:
                total = total + box[slot * 4 + j].astype(F32)
            buf[start + j] = total.astype(BF16)
            return 0

        lax.fori_loop(0, 4, one, 0)

    def stage(self, a, step):
        box = self.boxes[a]
        if step == 0:
            self.had[a, 0].wait_recv()
            self.add(a, self.far, (0,))
            self.had[a, 4] = self.copies.start(a, 4, self.block(a, self.far), box.at[pl.ds(16, 4)], self.to_two)
            self.had[a, 1].wait_recv()
            self.add(a, self.two, (1,))
            self.had[a, 5] = self.copies.start(a, 5, self.block(a, self.two), box.at[pl.ds(20, 4)], self.to_two)
        elif step == 1:
            self.had[a, 2].wait_recv()
            self.had[a, 4].wait_recv()
            self.add(a, self.one, (2, 4))
            self.had[a, 6] = self.copies.start(a, 6, self.block(a, self.one), box.at[pl.ds(24, 4)], self.to_one)
        elif step == 2:
            for slot in (3, 5, 6):
                self.had[a, slot].wait_recv()
            self.add(a, self.dp, (3, 5, 6))
            for k in range(3):
                src = self.bufs[a].at[self.place(self.dp) + lax.rem(self.z + k + 1, 4)]
                self.had[a, 7 + k] = self.copies.start(a, 7 + k, src, box.at[28 + k], self.to_z[k])
        elif step == 3:
            for k in range(3):
                self.had[a, 7 + k].wait_recv()
            total = self.bufs[a][self.place(self.dp) + self.z].astype(F32)
            for k in range(3):
                total = total + box[28 + k].astype(F32)
            out = self.outs[a]
            rows, cols = out.shape[0], total.shape[1]
            for j in range(total.shape[0] // rows):
                out[:, j * cols : (j + 1) * cols] = total[j * rows : (j + 1) * rows]

    def finish(self):
        self.copies.finish()


class Total:
    def __init__(self, scatter, value, box, send, recv):
        self.value, self.box, self.to = value, box, scatter
        self.copies, self.had = Copies(send, recv), {}

    def pass_on(self, slot, target):
        self.had[slot] = self.copies.start(0, slot, self.value.at[slot if slot < 3 else 3], self.box.at[slot], target)

    def stage(self, step):
        value, box = self.value, self.box
        targets = (self.to.to_twin, self.to.to_two, self.to.to_one)
        if step > 0 and step < 4:
            self.had[step - 1].wait_recv()
            value[step] = value[step - 1] + box[step - 1]
        if step < 3:
            self.pass_on(step, targets[step])
        elif step == 3:
            for k in range(3):
                self.pass_on(3 + k, self.to.to_z[k])
        elif step == 4:
            for k in range(3):
                self.had[3 + k].wait_recv()
            value[4] = (value[3] + box[3]) + (box[4] + box[5])

    def finish(self):
        self.copies.finish()


def fold_block(block, parts=2):
    cols = block.shape[1] // parts
    return jnp.concatenate([block[:, j * cols : (j + 1) * cols] for j in range(parts)], axis=0).astype(BF16)


def unfold_into(out, blocks, rows):
    n, have, cols = blocks.shape

    def body(j, _):
        pair = [blocks[2 * j + i].astype(F32) for i in (0, 1)]
        r = pl.ds(pl.multiple_of(2 * rows * j, 2 * rows), 2 * rows)
        for m in range(have // rows):
            both = jnp.concatenate([item[m * rows : (m + 1) * rows] for item in pair], axis=0)
            out[r, m * cols : (m + 1) * cols] = both.astype(BF16)
        return 0

    lax.fori_loop(0, n // 2, body, 0)


def unpack_vectors(slabs, out, sizes):
    n, depth, lanes = slabs.shape
    flat = slabs[...].reshape(n * depth, lanes)
    step = 768
    for size in sorted(set(sizes)):
        for at in range(0, n * size, step):
            lane = iota((1, step), 1) + at
            owner = lane // size
            within = lane - owner * size
            spread_out = dot(flat, (iota((lanes, step), 0) == within).astype(BF16))
            row = iota((n * depth, step), 0) - depth * owner
            for j, other in enumerate(sizes):
                if other == size:
                    out[j : j + 1, at : at + step] = column_sum(jnp.where(row == j, spread_out, 0.0))


def front_kernel(
    groups, local, sizes, lens, tok, slab, s_in, s_out, s_up,
    q, k, v, joined, rest, inverse, states, rows_out, w_q, w_k, w_v, w_out, w_up, vectors,
    cos_s, sin_s, ok_s, within, own, own_rows, part, part_rows, came, came_rows, num_s, den_s,
    g_vec, g_q, g_k, g_v, g_out, g_up, g_send, g_recv, *link,
):
    width = tok.shape[1]
    pairs = width // LANES
    chain = Chain(1, pairs, link)
    refs = (g_vec, g_q, g_k, g_v, g_out)
    half = g_up.shape[1] // 2
    arrays = [(ref, 0, ref.shape[1]) for ref in refs] + [(g_up, 0, half), (g_up, half, half)]
    gather = Gather(arrays, g_send, g_recv)
    me = gather.me
    g_vec[me] = slab[...].astype(BF16)
    for j, ref in enumerate((g_q, g_k, g_v)):
        ref[me] = fold_block(s_in[:, j * width : (j + 1) * width])
    g_out[me] = fold_block(s_out[...])
    g_up[me] = fold_block(s_up[...], 4)
    meet(gather.targets())
    for a in range(7):
        gather.begin(a)
    starts = (0, 0, 1, 2, 4, 5, 6)

    def wave(t):
        for a in range(7):
            if 0 <= t - starts[a] < 5:
                gather.stage(a, t - starts[a])

    work = Forward(
        groups, local, lens, chain, (q, k, v, joined, rest, inverse, states, rows_out),
        (cos_s, sin_s, ok_s, within, num_s, den_s), (own, own_rows, part, part_rows, came, came_rows),
    )
    sums, arrive, leave, intra, inter = work.steps()
    work.prepare()
    for t in range(5):
        wave(t)
    unpack_vectors(g_vec, vectors, sizes)
    bias = vectors.at[0:1]
    unfold_into(w_q, g_q, s_in.shape[0])
    work.project(0, tok, w_q, bias)
    wave(5)
    unfold_into(w_k, g_k, s_in.shape[0])
    work.project(1, tok, w_k, bias)
    wave(6)
    unfold_into(w_v, g_v, s_in.shape[0])
    work.project(2, tok, w_v, bias)
    wave(7)
    work.over(sums)

    @pl.when(chain.is_first)
    def _():
        for s in range(groups):
            leave(s)

    def pass_on():
        for s in range(groups):
            arrive(s)

            @pl.when(jnp.logical_not(chain.is_last))
            def _():
                leave(s)

    for s in range(groups):
        work.over(intra, s)
        wave(8 + s)
        if s == groups - 2:
            pl.when(chain.at == 1)(pass_on)
    unfold_into(w_out, g_out, s_out.shape[0])
    pl.when(chain.at > 1)(pass_on)
    for s in range(groups):
        work.over(inter, s)
        wave(8 + groups + s)
    for t in range(8 + 2 * groups, 11):
        wave(t)
    unfold_into(w_up, g_up, s_up.shape[0])

    @pl.when(jnp.logical_not(chain.is_last))
    def _():
        for s in range(groups):
            chain.sent(s)

    gather.finish()


TALL = 384


def by_eight(x):
    return jnp.sum(x.reshape(x.shape[0] // 8, 8, x.shape[1]), axis=0)


def middle_kernel(
    tok_h, joined_h, cot_h, w_out, up_h, s_down, vectors,
    act_h, first_h, gj_h, gup_h, gout_h, gw_down, small,
    low, joined, cot, branch, norm, sec, inv, hid, der, w_up, w_dn, box, xa, xb, fold_s, acc, acc_up,
    io, g_send, g_recv, r_send, r_recv,
):
    rows, width = joined.shape
    ff = w_up.shape[1]
    chunks = ff // width
    tiles = rows // TALL
    slabs = TALL // 96
    depth = rows // 96
    _, b_out, g_one, s_one, b_up, b_down, g_two, s_two = (
        (lambda j: lambda at=0, n=width: vectors[j : j + 1, at : at + n])(j) for j in range(8)
    )
    half = w_dn.shape[1] // 2
    gather = Gather([(w_dn, 0, half), (w_dn, half, half)], g_send, g_recv)
    scatter = Scatter(
        (hid,), (box,), (gw_down,), r_send, r_recv, lambda dp: depth * (dp // 2) + 4 * lax.rem(dp, 2)
    )
    loads = [
        pltpu.make_async_copy(src, dst, io.at[j])
        for j, (src, dst) in enumerate(((joined_h, joined), (tok_h, low), (up_h, w_up), (cot_h, cot)))
    ]
    for load in loads:
        load.start()
    w_dn[gather.me] = s_down[...].astype(BF16)
    meet(gather.targets())
    gather.begin(0)
    gather.begin(1)
    acc[...] = jnp.zeros_like(acc)
    acc_up[...] = jnp.zeros_like(acc_up)

    def tile(t):
        return pl.ds(t * TALL, TALL) if isinstance(t, int) else pl.ds(pl.multiple_of(t * TALL, TALL), TALL)

    def of_chunk(ref, j, t=None):
        if t is None:
            return ref[pl.ds(depth * j, depth)].reshape(rows, width)
        return ref[pl.ds(depth * j + slabs * t, slabs)].reshape(TALL, width)

    def down_chunk(j):
        return w_dn[pl.ds(8 * j, 8)].reshape(width, width)

    loads[0].wait()
    loads[1].wait()
    def rows32(t, i):
        return pl.ds(pl.multiple_of(t * TALL + i, 32), 32)

    def by_tiles(body, low=0, high=tiles):
        def both(u, _):
            for i in range(2):
                body(2 * u + i, (xa, xb)[i])
            return 0

        lax.fori_loop(low // 2, high // 2, both, 0)

    def enter(t, x):
        x[...] = dot(joined[tile(t)], w_out[...])
        for i in range(0, TALL, 32):
            r = rows32(t, i)
            unit, scale = normalised(low[r].astype(F32) + (x[i : i + 32] + b_out()))
            norm[r] = unit
            inv[r] = jnp.broadcast_to(scale, (32, LANES))
            low[r] = (unit * g_one() + s_one()).astype(BF16)

    by_tiles(enter, 0, tiles // 2)
    gather.stage(0, 0)
    by_tiles(enter, tiles // 2, tiles)
    loads[2].wait()

    def up(t, _):
        for j in range(chunks):
            x = (xa, xb)[j % 2]
            x[...] = dot(low[tile(t)], w_up[:, j * width : (j + 1) * width])
            for i in range(slabs):
                for m in range(0, 96, 32):
                    for n in range(0, width, 256):
                        y, d = gelu_both(x[96 * i + m : 96 * i + m + 32, n : n + 256] + b_up(j * width + n, 256))
                        hid[depth * j + slabs * t + i, m : m + 32, n : n + 256] = y.astype(BF16)
                        der[depth * j + slabs * t + i, m : m + 32, n : n + 256] = d.astype(BF16)
        return 0

    for t in range(tiles):
        lax.fori_loop(t, t + 1, up, 0)
        for a, step in (((1, 0), (0, 1)), ((0, 2), (1, 1)), ((0, 3), (1, 2)), ((0, 4), (1, 3), (1, 4)))[t]:
            gather.stage(a, step)
    loads[3].wait()

    def second(t, x):
        x[...] = dot(of_chunk(hid, 0, t), down_chunk(0))
        for j in range(1, chunks):
            x[...] += dot(of_chunk(hid, j, t), down_chunk(j))
        for i in range(0, TALL, 32):
            r = rows32(t, i)
            unit, scale = normalised(norm[r] * g_one() + (s_one() + b_down()) + x[i : i + 32])
            c = cot[r].astype(F32)
            cot[r] = (unit * g_two() + s_two()).astype(BF16)
            acc[4] += by_eight(c * unit)
            acc[5] += by_eight(c)
            e = c * g_two()
            g = scale * (e - mean_of(e) - unit * mean_of(e * unit))
            sec[r] = g
            g = g.astype(BF16)
            branch[r] = g
            acc[3] += by_eight(g.astype(F32))

    by_tiles(second)
    act = pltpu.make_async_copy(cot, act_h, io.at[3])
    act.start()
    for j in range(chunks):
        for m in range(2):
            x = (xa, xb)[m]
            x[...] = tdot(
                hid[pl.ds(depth * j, depth), :, m * TALL : (m + 1) * TALL].reshape(rows, TALL), branch[...]
            )
        for m in range(2):
            hid[pl.ds(depth * j + 4 * m, 4)] = (xa, xb)[m][...].astype(BF16).reshape(4, 96, width)
    scatter.begin(0)

    def back(t, _):
        for j in range(chunks):
            x = (xa, xb)[j % 2]
            x[...] = dot_t(branch[tile(t)], down_chunk(j))
            for i in range(slabs):
                for m in range(0, 96, 32):
                    at = depth * j + slabs * t + i
                    g = x[96 * i + m : 96 * i + m + 32] * der[at, m : m + 32].astype(F32)
                    g = g.astype(BF16)
                    der[at, m : m + 32] = g
                    acc_up[:, j * width : (j + 1) * width] += by_eight(g.astype(F32))
        return 0

    lax.fori_loop(0, tiles, back, 0)
    scatter.stage(0, 0)
    out = []

    def first(t, x):
        x[...] = dot_t(of_chunk(der, 0, t), w_up[:, 0:width])
        for j in range(1, chunks):
            x[...] += dot_t(of_chunk(der, j, t), w_up[:, j * width : (j + 1) * width])
        for i in range(0, TALL, 32):
            r = rows32(t, i)
            g = sec[r] + x[i : i + 32]
            unit = norm[r]
            acc[1] += by_eight(g * unit)
            acc[2] += by_eight(g)
            e = g * g_one()
            g = inv[r, 0:1] * (e - mean_of(e) - unit * mean_of(e * unit))
            sec[r] = g
            g = g.astype(BF16)
            branch[r] = g
            acc[0] += by_eight(g.astype(F32))

    by_tiles(first)
    out.append(pltpu.make_async_copy(sec, first_h, io.at[0]))
    out[-1].start()
    scatter.stage(0, 1)
    gather.finish()
    for m in range(2):
        for jj in range(chunks // 2):
            for i in range(2):
                (xa, xb)[i][...] = tdot(low[:, m * TALL : (m + 1) * TALL], of_chunk(der, 2 * jj + i))
            for i in range(16):
                both = [x[24 * i : 24 * i + 24] for x in (xa, xb)]
                w_dn[16 * m + i, 48 * jj : 48 * jj + 48] = jnp.concatenate(both, axis=0).astype(BF16)
    out.append(pltpu.make_async_copy(w_dn, gup_h, io.at[1]))
    out[-1].start()
    scatter.stage(0, 2)
    for m in range(2):
        x = (xa, xb)[m]
        x[...] = tdot(joined[:, m * TALL : (m + 1) * TALL], branch[...])
        for i in range(16):
            fold_s[16 * m + i] = fold_block(x[24 * i : 24 * i + 24])
    out.append(pltpu.make_async_copy(fold_s, gout_h, io.at[2]))
    out[-1].start()
    for t in range(tiles):
        joined[tile(t)] = dot_t(branch[tile(t)], w_out[...]).astype(BF16)
    out.append(pltpu.make_async_copy(joined, gj_h, io.at[4]))
    out[-1].start()
    small[...] = jnp.zeros_like(small)
    for row, at in ((3, 0), (4, 1), (5, 2), (10, 3), (11, 4), (12, 5)):
        small[row : row + 1] = column_sum(acc[at])
    for j in range(chunks):
        small[6 + j : 7 + j] = column_sum(acc_up[:, j * width : (j + 1) * width])
    scatter.stage(0, 3)
    act.wait()
    for copy in out:
        copy.wait()
    scatter.finish()


def tail_kernel(
    groups, local, lens, q_h, k_h, v_h, gj_h, joined_h, rest_h, inverse_h, states, rows_in,
    tok_h, wq_h, wk_h, wv_h, first_h, up_h, out_h, small,
    grad_h, gw_up, gw_out, gw_q, gw_k, gw_v, small_out,
    q, k, v, gnum, joined, lane_s, inverse, cos_s, sin_s, within,
    own, own_rows, part, part_rows, came, came_rows, slots, load_sem, slot_sem,
    b_up, b_out, b_q, b_k, b_v, x_up, x_out, x_q, x_k, x_v,
    value, box, r_send, r_recv, t_send, t_recv, *link,
):
    width = q.shape[1]
    rows = q.shape[0]
    pairs = width // LANES
    count = local // CHUNK
    chain = Chain(-1, pairs, link)
    scatter = Scatter(
        (b_up, b_out, b_q, b_k, b_v), (x_up, x_out, x_q, x_k, x_v),
        (gw_up, gw_out, gw_q, gw_k, gw_v), r_send, r_recv,
    )
    total = Total(scatter, value, box, t_send, t_recv)
    places = (
        (inverse_h, inverse), (gj_h, gnum), (joined_h, joined), (rest_h, lane_s), (q_h, q),
        (up_h, b_up), (out_h, b_out), (k_h, k), (v_h, v),
    )
    loads = [pltpu.make_async_copy(src, dst, load_sem.at[j]) for j, (src, dst) in enumerate(places)]
    for load in loads:
        load.start()
    meet(scatter.targets())
    fill_tables(groups, local, chain.at * local, lens, cos_s, sin_s, None, within)

    def sums(i, _):
        s, p = i // pairs, i % pairs
        n = lanes_of(p)
        _, _, one, two = head_masks()
        mask = block_mask(256, LANES)
        ones = block_mask(2 * LANES, LANES).astype(BF16)
        state = jnp.zeros((256, LANES), F32)
        row = jnp.zeros((1, 256), F32)
        for c in reversed(range(count)):
            r = rows_of(s, c, local)
            ri = inverse[r, n].astype(F32)
            gn = (gnum[r, n].astype(F32) * jnp.abs(ri)).astype(BF16)
            product = gn.astype(F32) * (joined[r, n].astype(F32) + lane_s[r, n].astype(F32))
            gden = jnp.where(ri > 0, -dot(two_parts(product), ones), 0.0)
            high = gden.astype(BF16).astype(F32)
            gnum[r, n] = gn
            lane_s[r, n] = (high * one + (gden - high) * two).astype(BF16)
            q2 = spread(q[r, n].astype(F32), cos_s[r], sin_s[r])
            state = state + tdot(q2, gn)
            row = row + column_sum(q2.astype(F32) * twice(gden))
            if c > 0:
                part[i * (count - 1) + c - 1] = pack(state * mask)
                part_rows[i * (count - 1) + c - 1] = jnp.broadcast_to(row, (8, 256))
        own[i] = pack(state * mask)
        own_rows[i] = jnp.broadcast_to(row, (8, 256))
        came[i] = jnp.zeros((128, LANES), F32)
        came_rows[i] = jnp.zeros((8, 256), F32)
        return 0

    def arrive(s):
        chain.arrive(s)

        def one(p, _):
            i = s * pairs + p
            came[i] = chain.in_state[i].astype(F32)
            came_rows[i] = chain.in_rows[i]
            return 0

        lax.fori_loop(0, pairs, one, 0)

    def leave(s):
        def one(p, _):
            i = s * pairs + p
            n = lanes_of(p)
            state = came[i] + own[i]
            low = state.astype(BF16)
            chain.out_state[i] = low
            lost = unpack(state - low.astype(F32), block_mask(256, LANES)).astype(BF16)
            mean = column_sum(v[pl.ds(s * local, local), n].astype(F32)) * (1.0 / local)
            row = dot_t(jnp.broadcast_to(mean, (8, LANES)).astype(BF16), lost)
            chain.out_rows[i] = came_rows[i] + own_rows[i] + row
            return 0

        lax.fori_loop(0, pairs, one, 0)
        chain.start(s)

    def pass_on():
        for s in range(groups):
            arrive(s)

            @pl.when(jnp.logical_not(chain.is_last))
            def _():
                leave(s)

    def intra(i, _):
        s, p = i // pairs, i % pairs
        n = lanes_of(p)
        first, second, one, two = head_masks()
        ones = jnp.ones((CHUNK, LANES), BF16)
        picks = (block_mask(LANES, LANES) * ((iota((LANES, LANES), 0) & (HALF - 1)) < 2).astype(F32)).astype(BF16)
        m = within[s]
        m = jnp.concatenate([m, m], axis=0)
        for c in range(count):
            r = rows_of(s, c, local)
            feature, key, value_low, gn, lane = q[r, n].astype(F32), k[r, n], v[r, n], gnum[r, n], lane_s[r, n]
            gden = dot(lane, picks)
            row = rows_in[i * count + c][0:1]
            outer = dot_t(twice(gn), states[i * count + c]) + twice(gden) * row
            gq = outer[:, :LANES] * cos_s[r] + outer[:, LANES:] * sin_s[r]
            heads = stacked_heads(feature, first, second)
            scores = (dot_t(heads, key) * m).astype(BF16)
            gheads = stacked_heads(gn.astype(F32), first, second)
            left = jnp.concatenate([gheads, stacked_heads(lane.astype(F32), first, second)], axis=1)
            g = (dot_t(left, jnp.concatenate([value_low, ones], axis=1)) * m).astype(BF16)
            inner = dot(g, key)
            gq = gq + jnp.where(first > 0, inner[:CHUNK], inner[CHUNK:])
            joined[r, n] = tdot(heads, g).T.astype(BF16)
            inverse[r, n] = tdot(gheads, scores).T.astype(BF16)
            q[r, n] = (gq * slope(feature)).astype(BF16)
        return 0

    def inter(i, _):
        s, p = i // pairs, i % pairs
        n = lanes_of(p)
        mask = block_mask(256, LANES)
        for c in range(count):
            r = rows_of(s, c, local)
            cosine, sine, key = cos_s[r], sin_s[r], k[r, n].astype(F32)
            state, row = came[i], came_rows[i][0:1]
            if c + 1 < count:
                state = state + part[i * (count - 1) + c]
                row = row + part_rows[i * (count - 1) + c][0:1]
            state = two_parts(unpack(state, mask))
            outer = dot_t(twice(v[r, n]), state) + row
            gk = outer[:, :LANES] * cosine + outer[:, LANES:] * sine + joined[r, n].astype(F32)
            v[r, n] = (dot(spread(key, cosine, sine), state[:, :LANES]) + inverse[r, n].astype(F32)).astype(BF16)
            k[r, n] = (gk * slope(key)).astype(BF16)
        return 0

    def over(step, s, low=0, high=pairs):
        lax.fori_loop(s * pairs + low, s * pairs + high, step, 0)

    def weight_terms(a, g):
        buf = scatter.bufs[a]
        size = width // 32
        for j in range(2):
            term = tdot(gnum[:, j * (width // 2) : (j + 1) * (width // 2)], g[...])
            for i in range(16):
                buf[16 * j + i] = fold_block(term[i * size : (i + 1) * size])

    for load in loads[:5]:
        load.wait()
    for j in range(2):
        loads[5 + j].wait()
        scatter.begin(j)
    for s in range(groups):
        over(sums, s)
    for load in loads[7:]:
        load.wait()

    @pl.when(chain.is_first)
    def _():
        for s in range(groups):
            leave(s)

    half = pairs // 2
    plan = {
        (0, 0): [(0, 0)], (0, 1): [(1, 0)],
        (1, 0): [], (1, 1): [(0, 1), (1, 1)],
        (2, 0): [], (2, 1): [(0, 2), (1, 2)],
    }
    for s in range(groups):
        for j in range(2):
            over(intra, s, j * half, (j + 1) * half)
            for a, step in plan.get((s, j), ()):
                scatter.stage(a, step)
        if s == groups - 2:
            pl.when(chain.at == chain.parts - 2)(pass_on)
    tok_load = pltpu.make_async_copy(tok_h, gnum, load_sem.at[0])
    w_loads = [
        pltpu.make_async_copy(wq_h, lane_s.at[pl.ds(0, width)], load_sem.at[1]),
        pltpu.make_async_copy(wk_h, lane_s.at[pl.ds(width, width)], load_sem.at[2]),
        pltpu.make_async_copy(wv_h, joined.at[pl.ds(0, width)], load_sem.at[3]),
    ]
    for load in [tok_load] + w_loads[:2]:
        load.start()
    pl.when(chain.at < chain.parts - 2)(pass_on)
    tok_load.wait()
    weight_terms(2, q)
    scatter.begin(2)
    for s in range(groups):
        over(inter, s)
        for a, step in (((2, 0),), ((0, 3),), ((1, 3),))[s]:
            scatter.stage(a, step)
    w_loads[2].start()
    weight_terms(3, k)
    scatter.begin(3)
    weight_terms(4, v)
    scatter.begin(4)
    value[0] = small[...]
    for j, ref in enumerate((q, k, v)):
        value[0, j : j + 1, :] = column_sum(ref[...].astype(F32))
    total.stage(0)
    scatter.stage(2, 1)
    for load in w_loads:
        load.wait()

    def slot(i):
        return slots.at[i % 3]

    def rows_at(ref, i):
        return ref.at[pl.ds(i * CHUNK, CHUNK)]

    n_slots = rows // CHUNK
    fetch = [pltpu.make_async_copy(rows_at(first_h, i), slot(i), slot_sem.at[i % 3, 0]) for i in range(n_slots)]
    store = [pltpu.make_async_copy(slot(i), rows_at(grad_h, i), slot_sem.at[i % 3, 1]) for i in range(n_slots)]
    fetch[0].start()
    rest_plan = (((3, 0),), ((4, 0), (2, 2)), ((3, 1),), ((4, 1),), ((2, 3), (3, 2)), ((4, 2),))
    for i in range(n_slots):
        if i + 1 < n_slots:
            if i >= 2:
                store[i - 2].wait()
            fetch[i + 1].start()
        fetch[i].wait()
        r = pl.ds(i * CHUNK, CHUNK)
        slots[i % 3] = (
            slots[i % 3]
            + dot_t(q[r], lane_s[pl.ds(0, width)])
            + dot_t(k[r], lane_s[pl.ds(width, width)])
            + dot_t(v[r], joined[pl.ds(0, width)])
        )
        store[i].start()
        for a, step in rest_plan[i] if i < len(rest_plan) else ():
            scatter.stage(a, step)
        if 1 <= i + 1 < 5:
            total.stage(i + 1)
    scatter.stage(3, 3)
    scatter.stage(4, 3)
    small_out[...] = value[4]
    for i in range(max(n_slots - 3, 0), n_slots):
        store[i].wait()

    @pl.when(jnp.logical_not(chain.is_last))
    def _():
        for s in range(groups):
            chain.sent(s)

    scatter.finish()
    total.finish()


VMEM = pl.BlockSpec(memory_space=pltpu.VMEM)
SMEM = pl.BlockSpec(memory_space=pltpu.SMEM)
ANY = pl.BlockSpec(memory_space=pl.ANY)


def params(collective=None):
    if collective is None:
        return pltpu.CompilerParams(vmem_limit_bytes=BIG)
    return pltpu.CompilerParams(vmem_limit_bytes=BIG, collective_id=collective, has_side_effects=True)


def shape(dims, kind=BF16):
    return jax.ShapeDtypeStruct(dims, kind)


def shards(
    tokens, lengths, weight_in, bias_in, weight_out, bias_out, gain_one, shift_one,
    weight_up, bias_up, weight_down, bias_down, gain_two, shift_two, cotangent,
):
    groups, local, width = tokens.shape
    rows = groups * local
    pairs = width // LANES
    count = local // CHUNK
    axes = ("dp", "head")
    parts = lax.axis_size("head")
    me = lax.axis_index("head")

    by_kernel = lax.axis_size("dp") == 8 and parts == 4
    small = (bias_in, bias_out, gain_one, shift_one, bias_up, bias_down, gain_two, shift_two)
    tok = tokens.reshape(rows, width)
    units = groups * pairs
    plane = shape((rows, width))
    table = pltpu.VMEM((rows, LANES), F32)
    within = pltpu.VMEM((groups, CHUNK, CHUNK), F32)
    tall = pltpu.VMEM((rows, width), F32)
    flat = pltpu.VMEM((rows, width), BF16)

    def sums_scratch():
        return [
            pltpu.VMEM((units, 128, LANES), F32),
            pltpu.VMEM((units, 8, 256), F32),
            pltpu.VMEM((units * max(count - 1, 1), 128, LANES), F32),
            pltpu.VMEM((units * max(count - 1, 1), 8, 256), F32),
            pltpu.VMEM((units, 128, LANES), F32),
            pltpu.VMEM((units, 8, 256), F32),
        ]

    forward_shapes = (plane,) * 6 + (shape((units * count, 256, 256)), shape((units * count, 8, 256), F32))
    forward_scratch = [table, table, table, within] + sums_scratch() + [tall, tall]
    ff = weight_up.shape[1]
    if by_kernel:
        slab = jnp.stack([jnp.pad(item, (0, LANES - item.shape[0])) for item in small] * 2)
        square = shape((width, width))
        sizes = [item.shape[0] for item in small]
        half = (2 * weight_in.shape[0], width // 2)
        (
            q, k, v, joined, rest, inverse, states, state_rows, w_q, w_k, w_v, w_out, w_up, vectors
        ) = pl.pallas_call(
            functools.partial(front_kernel, groups, local, sizes),
            out_shape=forward_shapes
            + (square,) * 4
            + (shape((width, ff)), shape((len(small), ff), F32)),
            in_specs=[SMEM] + [VMEM] * 5,
            out_specs=(VMEM,) * 14,
            scratch_shapes=forward_scratch
            + [pltpu.VMEM((32, 16, LANES), BF16)]
            + [pltpu.VMEM((32,) + half, BF16)] * 4
            + [pltpu.VMEM((32, 4 * weight_up.shape[0], ff // 4), BF16)]
            + [pltpu.SemaphoreType.DMA((7, 10)), pltpu.SemaphoreType.DMA((7, 10))]
            + chain_scratch(groups, pairs),
            compiler_params=params(3),
        )(lengths, tok, slab, weight_in, weight_out, weight_up)
    else:

        def gather(item):
            return lax.all_gather(item.astype(BF16), axes, axis=0, tiled=True)

        w_in, w_out, w_up, w_down = map(gather, (weight_in, weight_out, weight_up, weight_down))
        sizes = [item.shape[0] for item in small]
        gathered = lax.all_gather(jnp.concatenate([item.astype(BF16) for item in small]), axes, axis=0)
        cuts = [sum(sizes[:i]) for i in range(len(sizes) + 1)]
        b_in, b_out, g_one, s_one, b_up, b_down, g_two, s_two = (
            gathered[:, a:b].reshape(1, -1).astype(F32) for a, b in zip(cuts, cuts[1:])
        )
        w_q, w_k, w_v = (w_in[:, j * width : (j + 1) * width] for j in range(3))
        q, k, v, joined, rest, inverse, states, state_rows = pl.pallas_call(
            functools.partial(attend_kernel, groups, local),
            out_shape=forward_shapes,
            in_specs=[SMEM] + [VMEM] * 5,
            out_specs=(VMEM,) * 8,
            scratch_shapes=forward_scratch + chain_scratch(groups, pairs),
            compiler_params=params(1),
        )(lengths, tok, w_q, w_k, w_v, b_in)

    tile = local

    if by_kernel:
        slabs96 = shape((32, 96, width))
        term_out = shape((32,) + half)
        kept = pltpu.VMEM((rows // 96 * (ff // width), 96, width), BF16)
        tile_s = pltpu.VMEM((TALL, width), F32)
        activations, g_first, g_joined, gw_up, gw_out, gw_down, small_sums = pl.pallas_call(
            middle_kernel,
            out_shape=[
                plane, shape((rows, width), F32), plane, slabs96, term_out,
                shape(weight_down.shape, F32), shape((16, width), F32),
            ],
            in_specs=[ANY] * 3 + [VMEM, ANY, VMEM, VMEM],
            out_specs=[ANY] * 5 + [VMEM] * 2,
            scratch_shapes=[flat] * 4
            + [tall, tall, table, kept, kept]
            + [pltpu.VMEM((width, ff), BF16), pltpu.VMEM((32, 96, width), BF16), pltpu.VMEM((31, 96, width), BF16)]
            + [tile_s, tile_s, pltpu.VMEM((32,) + half, BF16)]
            + [pltpu.VMEM((6, 8, width), F32), pltpu.VMEM((8, ff), F32)]
            + [pltpu.SemaphoreType.DMA((5,))]
            + [pltpu.SemaphoreType.DMA((2, 10))] * 2
            + [pltpu.SemaphoreType.DMA((1, 10))] * 2,
            compiler_params=params(5),
        )(tok, joined, cotangent.reshape(rows, width), w_out, w_up, weight_down, vectors)
        terms = [gw_up.shape, gw_out.shape] + [(32,) + half] * 3
        row_shape = (weight_out.shape[0], width)
        input_grad, gw_up, gw_out, gw_q, gw_k, gw_v, sums = pl.pallas_call(
            functools.partial(tail_kernel, groups, local),
            out_shape=[shape((rows, width), F32), shape(weight_up.shape, F32)]
            + [shape(row_shape, F32)] * 4
            + [shape(small_sums.shape, F32)],
            in_specs=[SMEM] + [ANY] * 7 + [VMEM] * 2 + [ANY] * 7 + [VMEM],
            out_specs=[ANY] + [VMEM] * 6,
            scratch_shapes=[flat] * 7
            + [table, table, within]
            + sums_scratch()
            + [pltpu.VMEM((3, CHUNK, width), F32)]
            + [pltpu.SemaphoreType.DMA((9,)), pltpu.SemaphoreType.DMA((3, 2))]
            + [pltpu.VMEM(item, BF16) for item in terms]
            + [pltpu.VMEM((31,) + item[1:], BF16) for item in terms]
            + [pltpu.VMEM((5,) + small_sums.shape, F32), pltpu.VMEM((6,) + small_sums.shape, F32)]
            + [pltpu.SemaphoreType.DMA((5, 10))] * 2
            + [pltpu.SemaphoreType.DMA((1, 6))] * 2
            + chain_scratch(groups, pairs),
            compiler_params=params(4),
        )(
            lengths, q, k, v, g_joined, joined, rest, inverse, states, state_rows,
            tok, w_q, w_k, w_v, g_first, gw_up, gw_out, small_sums,
        )
        sums = sums.reshape(-1)
        me = lax.axis_index(axes)
        mine, at = [], 0
        for item in (2 * width, width, width, width, width, ff, width, width, width):
            mine.append(lax.dynamic_slice(sums, (at + me * (item // 32),), (item // 32,)))
            at += item
        gb_front, gb_value, gb_out, gg_one, gs_one, gb_up, gb_down, gg_two, gs_two = mine
        return (
            activations.reshape(groups, local, width),
            input_grad.reshape(groups, local, width),
            jnp.concatenate([gw_q, gw_k, gw_v], axis=1), gb_front, gb_value, gw_out, gb_out, gg_one, gs_one,
            gw_up, gb_up, gw_down, gb_down, gg_two, gs_two,
        )

    def block(cols):
        return pl.BlockSpec((tile, cols), lambda i: (i, 0))

    def fixed(*dims):
        return pl.BlockSpec(dims, lambda i: (0,) * len(dims), pipeline_mode=pl.Buffered(1))

    vectors = [fixed(1, width)] * 3 + [fixed(1, ff)] + [fixed(1, width)] * 3
    weights = [fixed(width, width), fixed(width, ff), fixed(ff, width)]
    vector_shapes = [shape((1, width), F32)] * 3 + [shape((1, ff), F32)] + [shape((1, width), F32)] * 3
    (
        activations, g_first, g_joined, gw_out, gw_up, gw_down,
        gb_out, gg_one, gs_one, gb_up, gb_down, gg_two, gs_two,
    ) = pl.pallas_call(
        feed_kernel,
        grid=(rows // tile,),
        out_shape=[plane, shape((rows, width), F32), plane]
        + [shape((width, width), F32), shape((width, ff), F32), shape((ff, width), F32)]
        + vector_shapes,
        in_specs=[block(width)] * 3 + weights + vectors,
        out_specs=[block(width)] * 3 + weights + vectors,
        scratch_shapes=[
            pltpu.VMEM((tile, width), F32),
            pltpu.VMEM((tile, width), BF16),
            pltpu.VMEM((tile, ff), BF16),
            pltpu.VMEM((tile, ff), BF16),
            pltpu.VMEM((tile, width), F32),
            pltpu.VMEM((tile, width), BF16),
        ],
        compiler_params=params(),
    )(
        tok, joined, cotangent.reshape(rows, width), w_out, w_up, w_down,
        b_out, g_one, s_one, b_up, b_down, g_two, s_two,
    )
    g_mixed = pl.pallas_call(
        functools.partial(back_kernel, groups, local),
        out_shape=shape((rows, 3 * width)),
        in_specs=[SMEM] + [VMEM] * 9,
        out_specs=VMEM,
        scratch_shapes=[table, table, within] + sums_scratch()
        + [pltpu.VMEM((rows, width), BF16), tall, pltpu.VMEM((rows, width), BF16)] + chain_scratch(groups, pairs),
        compiler_params=params(2),
    )(lengths, q, k, v, g_joined, joined, rest, inverse, states, state_rows)
    input_grad, gw_in, gb_in = pl.pallas_call(
        input_kernel,
        grid=(rows // tile,),
        out_shape=[shape((rows, width), F32), shape((width, 3 * width), F32), shape((1, 3 * width), F32)],
        in_specs=[block(width), block(3 * width), fixed(width, 3 * width), block(width)],
        out_specs=[block(width), fixed(width, 3 * width), fixed(1, 3 * width)],
        compiler_params=params(),
    )(tok, g_mixed, w_in, g_first)

    gb_in = gb_in.reshape(-1)
    cols = [gb_in[: 2 * width], gb_in[2 * width :]] + [
        item.reshape(-1) for item in (gb_out, gg_one, gs_one, gb_up, gb_down, gg_two, gs_two)
    ]
    total = lax.axis_size(axes)
    def scatter(item):
        return lax.psum_scatter(item, axes, scatter_dimension=0, tiled=True)

    cut = [item.shape[0] // total for item in cols]
    merged = scatter(jnp.concatenate([item.reshape(total, -1) for item in cols], axis=1).reshape(-1))
    places = [sum(cut[:i]) for i in range(len(cut) + 1)]
    (gb_front, gb_value, gb_out, gg_one, gs_one, gb_up, gb_down, gg_two, gs_two) = (
        merged[a:b] for a, b in zip(places, places[1:])
    )
    return (
        activations.reshape(groups, local, width),
        input_grad.reshape(groups, local, width),
        scatter(gw_in), gb_front, gb_value, scatter(gw_out), gb_out, gg_one, gs_one,
        scatter(gw_up), gb_up, scatter(gw_down), gb_down, gg_two, gs_two,
    )


def solution(mesh):
    spread_rows = P("dp", "head", None)
    matrix = P(("dp", "head"), None)
    vector = P(("dp", "head"))
    return jax.shard_map(
        shards,
        mesh=mesh,
        in_specs=(
            spread_rows, P("dp"), matrix, vector, matrix, vector, vector, vector,
            matrix, vector, matrix, vector, vector, vector, spread_rows,
        ),
        out_specs=(
            spread_rows, spread_rows, matrix, vector, vector, matrix, vector, vector, vector,
            matrix, vector, matrix, vector, vector, vector,
        ),
        check_vma=False,
    )
```

```python
import functools
import math

import jax
import jax.numpy as jnp
from jax import lax
from jax.experimental import pallas as pl
from jax.experimental.pallas import tpu as pltpu
from jax.sharding import PartitionSpec as P

F32 = jnp.float32
BF16 = jnp.bfloat16
CHUNK = 256
LANES = 128
HALF = 64
BIG = 62 * 1024 * 1024
MESH = pl.DeviceIdType.MESH


def dot(a, b):
    return lax.dot_general(a, b, (((1,), (0,)), ((), ())), preferred_element_type=F32)


def dot_t(a, b):
    return lax.dot_general(a, b, (((1,), (1,)), ((), ())), preferred_element_type=F32)


def tdot(a, b):
    return lax.dot_general(a, b, (((0,), (0,)), ((), ())), preferred_element_type=F32)


def iota(shape, dim):
    return lax.broadcasted_iota(jnp.int32, shape, dim)


def block_mask(rows, cols):
    return ((iota((rows, cols), 0) & HALF) == (iota((rows, cols), 1) & HALF)).astype(F32)


def head_masks():
    lane = iota((1, LANES), 1)
    first = (lane < HALF).astype(F32)
    place = lane & (HALF - 1)
    return first, 1.0 - first, (place == 0).astype(F32), (place == 1).astype(F32)


def cos_poly(z):
    t = z * z
    r = -1.0 / 3628800 + t * (1.0 / 479001600)
    r = 1.0 / 40320 + t * r
    r = -1.0 / 720 + t * r
    r = 1.0 / 24 + t * r
    r = -0.5 + t * r
    return 1.0 + t * r


def sin_poly(z):
    t = z * z
    r = -1.0 / 39916800 + t * (1.0 / 6227020800)
    r = 1.0 / 362880 + t * r
    r = -1.0 / 5040 + t * r
    r = 1.0 / 120 + t * r
    r = -1.0 / 6 + t * r
    return z + z * (t * r)


def angles(start, limit, rows):
    place = iota((rows, LANES), 0) + start
    theta = jnp.minimum((0.5 * math.pi * place.astype(F32)) / limit.astype(F32), 0.5 * math.pi)
    return cos_poly(theta), sin_poly(theta), (place < limit).astype(F32)


def weights_within(limit):
    apart = iota((CHUNK, CHUNK), 0) - iota((CHUNK, CHUNK), 1)
    theta = jnp.minimum((0.5 * math.pi * apart.astype(F32)) / limit.astype(F32), 0.5 * math.pi)
    return jnp.where(apart >= 0, cos_poly(theta), 0.0)


def softplus(x):
    t = jnp.exp(-jnp.abs(x))
    tail = jnp.where(t < 1e-3, t * (1.0 - 0.5 * t), jnp.log(1.0 + t))
    return jnp.maximum(x, 0.0) + tail


def slope(feature):
    small = feature * (1.0 - feature * (0.5 - feature * (1.0 / 6)))
    return jnp.where(feature < 0.01, small, 1.0 - jnp.exp(-feature))


def pack(state):
    return jnp.concatenate([state[0:64] + state[64:128], state[128:192] + state[192:256]], axis=0)


def unpack(packed, mask):
    top, bottom = packed[0:64], packed[64:128]
    return jnp.concatenate([top, top, bottom, bottom], axis=0) * mask


def column_of(row, first):
    halves = []
    for at in (0, LANES):
        turned = jnp.broadcast_to(row[:, at : at + LANES], (LANES, LANES)).T
        halves.append(jnp.where(first > 0, turned[0:64], turned[64:128]))
    return jnp.concatenate(halves, axis=0)


def two_parts(state):
    high = state.astype(BF16)
    return jnp.concatenate([high, (state - high.astype(F32)).astype(BF16)], axis=1)


def twice(value):
    return jnp.concatenate([value, value], axis=1)


def spread(feature, cosine, sine):
    return jnp.concatenate([feature * cosine, feature * sine], axis=1).astype(BF16)


def stacked_heads(value, first, second):
    return jnp.concatenate([value * first, value * second], axis=0).astype(BF16)


def rows_of(s, c, local):
    return pl.ds(pl.multiple_of(s * local + c * CHUNK, CHUNK), CHUNK)


def lanes_of(p):
    return pl.ds(pl.multiple_of(p * LANES, LANES), LANES)


def fill_tables(groups, local, base, lens, cos_s, sin_s, ok_s, within):
    for s in range(groups):
        cosine, sine, valid = angles(base, lens[s], local)
        cos_s[s * local : (s + 1) * local] = cosine
        sin_s[s * local : (s + 1) * local] = sine
        if ok_s is not None:
            ok_s[s * local : (s + 1) * local] = valid
        within[s] = weights_within(lens[s])


def meet(targets):
    barrier = pltpu.get_barrier_semaphore()
    for target in targets:
        pl.semaphore_signal(barrier, inc=1, device_id=target, device_id_type=MESH)
    pl.semaphore_wait(barrier, len(targets))


class Chain:
    def __init__(self, step, pairs, refs):
        self.at, self.parts, self.pairs = lax.axis_index("head"), lax.axis_size("head"), pairs
        self.out_state, self.out_rows, self.in_state, self.in_rows, self.send, self.recv = refs
        self.before = {"head": lax.rem(self.at + self.parts - step, self.parts)}
        self.after = {"head": lax.rem(self.at + self.parts + step, self.parts)}
        last = self.parts - 1
        self.is_first = self.at == (0 if step > 0 else last)
        self.is_last = self.at == (last if step > 0 else 0)

    def copies(self, s):
        some = pl.ds(s * self.pairs, self.pairs)
        return [
            pltpu.make_async_remote_copy(
                src_ref=src.at[some], dst_ref=dst.at[some],
                send_sem=self.send.at[s, j], recv_sem=self.recv.at[s, j],
                device_id=self.after, device_id_type=MESH,
            )
            for j, (src, dst) in enumerate(
                ((self.out_state, self.in_state), (self.out_rows, self.in_rows))
            )
        ]

    def start(self, s):
        for copy in self.copies(s):
            copy.start()

    def arrive(self, s):
        for copy in self.copies(s):
            copy.wait_recv()

    def sent(self, s):
        for copy in self.copies(s):
            copy.wait_send()


def chain_scratch(groups, pairs):
    return [
        pltpu.VMEM((groups * pairs, 128, LANES), BF16),
        pltpu.VMEM((groups * pairs, 8, 256), F32),
        pltpu.VMEM((groups * pairs, 128, LANES), BF16),
        pltpu.VMEM((groups * pairs, 8, 256), F32),
        pltpu.SemaphoreType.DMA((groups, 2)),
        pltpu.SemaphoreType.DMA((groups, 2)),
    ]


class Forward:
    def __init__(self, groups, local, lens, chain, outs, tables, sums):
        self.groups, self.local, self.lens, self.chain = groups, local, lens, chain
        self.outs, self.tables, self.sums_refs = outs, tables, sums
        self.pairs = outs[0].shape[1] // LANES
        self.count = local // CHUNK

    def prepare(self):
        cos_s, sin_s, ok_s, within = self.tables[:4]
        fill_tables(self.groups, self.local, self.chain.at * self.local, self.lens, cos_s, sin_s, ok_s, within)

    def project(self, piece, tok, weight, bias):
        out, ok_s, width = self.outs[piece], self.tables[2], tok.shape[1]

        def body(i, _):
            r = pl.ds(pl.multiple_of(i * CHUNK, CHUNK), CHUNK)
            x = tok[r]
            valid = twice(ok_s[r])
            for n in range(0, width, 256):
                m = piece * width + n
                y = dot(x, weight[:, n : n + 256]) + bias[:, m : m + 256]
                out[r, n : n + 256] = (softplus(y) * valid if piece < 2 else y).astype(BF16)
            return 0

        lax.fori_loop(0, self.groups * self.count, body, 0)

    def over(self, step, s=None):
        low, high = (0, self.groups) if s is None else (s, s + 1)
        lax.fori_loop(low * self.pairs, high * self.pairs, step, 0)

    def names(self):
        return (self.local, self.pairs, self.count, self.chain) + tuple(self.outs) + tuple(self.tables) + tuple(self.sums_refs)

    def steps(self):
        (
            local, pairs, count, chain, q, k, v, joined, rest, inverse, states, rows_out,
            cos_s, sin_s, ok_s, within, num_s, den_s, own, own_rows, part, part_rows, came, came_rows,
        ) = self.names()

        def sums(i, _):
            s, p = i // pairs, i % pairs
            mask = block_mask(256, LANES)
            total = jnp.zeros((256, LANES), F32)
            row = jnp.zeros((1, 256), F32)
            for c in range(count):
                r, n = rows_of(s, c, local), lanes_of(p)
                k2 = spread(k[r, n].astype(F32), cos_s[r], sin_s[r])
                total = total + tdot(k2, v[r, n])
                row = row + column_sum(k2.astype(F32))
                if c + 1 < count:
                    part[i * (count - 1) + c] = pack(total * mask)
                    part_rows[i * (count - 1) + c] = jnp.broadcast_to(row, (8, 256))
            own[i] = pack(total * mask)
            own_rows[i] = jnp.broadcast_to(row, (8, 256))
            came[i] = jnp.zeros((128, LANES), F32)
            came_rows[i] = jnp.zeros((8, 256), F32)
            return 0

        def arrive(s):
            chain.arrive(s)

            def one(p, _):
                i = s * pairs + p
                rows = chain.in_rows[i]
                column = column_of(rows[0:1], head_masks()[0])
                came[i] = chain.in_state[i].astype(F32) + column * rows[1:2, 0:LANES]
                came_rows[i] = rows
                return 0

            lax.fori_loop(0, pairs, one, 0)

        def leave(s):
            def one(p, _):
                i = s * pairs + p
                total = came[i] + own[i]
                row = came_rows[i][0:1] + own_rows[i][0:1]
                column = column_of(row, head_masks()[0])
                centre = column_sum(total) / jnp.maximum(column_sum(column), 1e-30)
                centre = centre.astype(BF16).astype(F32)
                chain.out_state[i] = (total - column * centre).astype(BF16)
                chain.out_rows[i] = jnp.concatenate([row, twice(centre), jnp.zeros((6, 256), F32)], axis=0)
                return 0

            lax.fori_loop(0, pairs, one, 0)
            chain.start(s)

        def intra(i, _):
            s, p = i // pairs, i % pairs
            n = lanes_of(p)
            first, second, _, _ = head_masks()
            ones = jnp.ones((CHUNK, LANES), BF16)
            m = within[s]
            m = jnp.concatenate([m, m], axis=0)
            for c in range(count):
                r = rows_of(s, c, local)
                scores = dot_t(stacked_heads(q[r, n].astype(F32), first, second), k[r, n])
                inner = dot((scores * m).astype(BF16), jnp.concatenate([v[r, n], ones], axis=1))
                both = jnp.where(twice(first) > 0, inner[:CHUNK], inner[CHUNK:])
                num_s[r, n] = both[:, :LANES]
                den_s[r, n] = both[:, LANES:]
            return 0

        def inter(i, _):
            s, p = i // pairs, i % pairs
            n = lanes_of(p)
            mask = block_mask(256, LANES)
            ones = block_mask(LANES, LANES).astype(BF16)
            for c in range(count):
                r = rows_of(s, c, local)
                state, row = came[i], came_rows[i][0:1]
                if c > 0:
                    state = state + part[i * (count - 1) + c - 1]
                    row = row + part_rows[i * (count - 1) + c - 1][0:1]
                state = two_parts(unpack(state, mask))
                states[i * count + c] = state
                rows_out[i * count + c] = jnp.broadcast_to(row, (8, 256))
                q2 = spread(q[r, n].astype(F32), cos_s[r], sin_s[r])
                both = dot(q2, state)
                num = both[:, :LANES] + both[:, LANES:] + num_s[r, n]
                weighed = q2.astype(F32) * row
                weighed = (weighed[:, :LANES] + weighed[:, LANES:]).astype(BF16)
                den = dot(weighed, ones) + den_s[r, n]
                above = 1.0 / jnp.maximum(den, 1.0)
                attended = num * above
                rounded = attended.astype(BF16)
                joined[r, n] = rounded
                rest[r, n] = (attended - rounded.astype(F32)).astype(BF16)
                inverse[r, n] = jnp.where(den > 1.0, above, -1.0).astype(BF16)
            return 0

        return sums, arrive, leave, intra, inter


def attend_kernel(
    groups, local, lens, tok, w_q, w_k, w_v, bias,
    q, k, v, joined, rest, inverse, states, rows_out,
    cos_s, sin_s, ok_s, within, own, own_rows, part, part_rows, came, came_rows, num_s, den_s, *link,
):
    chain = Chain(1, tok.shape[1] // LANES, link)
    meet([chain.before, chain.after])
    work = Forward(
        groups, local, lens, chain, (q, k, v, joined, rest, inverse, states, rows_out),
        (cos_s, sin_s, ok_s, within, num_s, den_s), (own, own_rows, part, part_rows, came, came_rows),
    )
    work.prepare()
    for piece, weight in enumerate((w_q, w_k, w_v)):
        work.project(piece, tok, weight, bias)
    sums, arrive, leave, intra, inter = work.steps()
    work.over(sums)

    @pl.when(chain.is_first)
    def _():
        for s in range(groups):
            leave(s)

    work.over(intra)

    @pl.when(jnp.logical_not(chain.is_first))
    def _():
        for s in range(groups):
            arrive(s)

            @pl.when(jnp.logical_not(chain.is_last))
            def _():
                leave(s)

    work.over(inter)

    @pl.when(jnp.logical_not(chain.is_last))
    def _():
        for s in range(groups):
            chain.sent(s)


def gelu_both(x):
    z = jnp.abs(x) * (1.0 / math.sqrt(2.0))
    t = 1.0 / (1.0 + 0.3275911 * z)
    e = jnp.exp(-0.5 * x * x)
    poly = t * (
        0.254829592 + t * (-0.284496736 + t * (1.421413741 + t * (-1.453152027 + t * 1.061405429)))
    )
    tail = 0.5 * poly * e
    phi = jnp.where(x >= 0, 1.0 - tail, tail)
    return x * phi, phi + x * e * (1.0 / math.sqrt(2.0 * math.pi))


def mean_of(x):
    return jnp.mean(x, axis=1, keepdims=True)


def column_sum(x):
    return jnp.sum(x, axis=0, keepdims=True)


def normalised(x):
    centred = x - mean_of(x)
    inv = lax.rsqrt(mean_of(centred * centred) + 1e-05)
    return centred * inv, inv


def feed_kernel(
    tok, joined, cot, w_out, w_up, w_down, b_out, g_one, s_one, b_up, b_down, g_two, s_two,
    act, g_first, g_joined, gw_out, gw_up, gw_down, gb_out, gg_one, gs_one, gb_up, gb_down, gg_two, gs_two,
    norm_s, low_s, hid_s, der_s, sec_s, branch_s,
):
    rows = tok.shape[0]
    ff = w_up.shape[1]
    step = 768
    count = ff // step

    @pl.when(pl.program_id(0) == 0)
    def _():
        for ref in (gw_out, gw_up, gw_down, gb_out, gg_one, gs_one, gb_up, gb_down, gg_two, gs_two):
            ref[...] = jnp.zeros_like(ref)

    first = tok[...].astype(F32) + (dot(joined[...], w_out[...]) + b_out[...])
    unit_one, inv_one = normalised(first)
    norm_s[...] = unit_one
    normed = unit_one * g_one[...] + s_one[...]
    low_s[...] = normed.astype(BF16)
    sec_s[...] = normed + b_down[...]

    def up(j, _):
        n = pl.ds(pl.multiple_of(j * step, step), step)
        x = dot(low_s[...], w_up[:, n]) + b_up[:, n]
        y, d = gelu_both(x)
        hid_s[:, n] = y.astype(BF16)
        der_s[:, n] = d.astype(BF16)
        return 0

    lax.fori_loop(0, count, up, 0)
    second = sec_s[...] + dot(hid_s[...], w_down[...])
    unit_two, inv_two = normalised(second)
    act[...] = (unit_two * g_two[...] + s_two[...]).astype(BF16)
    c = cot[...].astype(F32)
    gg_two[...] += column_sum(c * unit_two)
    gs_two[...] += column_sum(c)
    e = c * g_two[...]
    g_second = inv_two * (e - mean_of(e) - unit_two * mean_of(e * unit_two))
    sec_s[...] = g_second
    branch = g_second.astype(BF16)
    branch_s[...] = branch
    gb_down[...] += column_sum(branch.astype(F32))

    def down(j, _):
        n = pl.ds(pl.multiple_of(j * step, step), step)
        gh = dot_t(branch_s[...], w_down[n, :])
        gu = gh * der_s[:, n].astype(F32)
        gu = gu.astype(BF16)
        der_s[:, n] = gu
        gb_up[:, n] += column_sum(gu.astype(F32))
        gw_down[n, :] += tdot(hid_s[:, n], branch_s[...])
        gw_up[:, n] += tdot(low_s[...], gu)
        return 0

    lax.fori_loop(0, count, down, 0)
    g_normed = sec_s[...] + dot_t(der_s[...], w_up[...])
    unit_one = norm_s[...]
    gg_one[...] += column_sum(g_normed * unit_one)
    gs_one[...] += column_sum(g_normed)
    e = g_normed * g_one[...]
    gf = inv_one * (e - mean_of(e) - unit_one * mean_of(e * unit_one))
    g_first[...] = gf
    go = gf.astype(BF16)
    gb_out[...] += column_sum(go.astype(F32))
    gw_out[...] += tdot(joined[...], go)
    g_joined[...] = dot_t(go, w_out[...]).astype(BF16)


def back_kernel(
    groups, local, lens, q, k, v, gj, joined, rest, inverse, states, rows_in, out,
    cos_s, sin_s, within, own, own_rows, part, part_rows, came, came_rows, gnum_s, gden_s, lane_s, *link,
):
    width = q.shape[1]
    pairs = width // LANES
    count = local // CHUNK
    chain = Chain(-1, pairs, link)
    meet([chain.before, chain.after])
    fill_tables(groups, local, chain.at * local, lens, cos_s, sin_s, None, within)

    def sums(i, _):
        s, p = i // pairs, i % pairs
        n = lanes_of(p)
        _, _, one, two = head_masks()
        mask = block_mask(256, LANES)
        ones = block_mask(2 * LANES, LANES).astype(BF16)
        total = jnp.zeros((256, LANES), F32)
        row = jnp.zeros((1, 256), F32)
        for c in reversed(range(count)):
            r = rows_of(s, c, local)
            ri = inverse[r, n].astype(F32)
            gnum = (gj[r, n].astype(F32) * jnp.abs(ri)).astype(BF16)
            product = gnum.astype(F32) * (joined[r, n].astype(F32) + rest[r, n].astype(F32))
            gden = jnp.where(ri > 0, -dot(two_parts(product), ones), 0.0)
            high = gden.astype(BF16).astype(F32)
            gnum_s[r, n] = gnum
            gden_s[r, n] = gden
            lane_s[r, n] = (high * one + (gden - high) * two).astype(BF16)
            q2 = spread(q[r, n].astype(F32), cos_s[r], sin_s[r])
            total = total + tdot(q2, gnum)
            row = row + column_sum(q2.astype(F32) * twice(gden))
            if c > 0:
                part[i * (count - 1) + c - 1] = pack(total * mask)
                part_rows[i * (count - 1) + c - 1] = jnp.broadcast_to(row, (8, 256))
        own[i] = pack(total * mask)
        own_rows[i] = jnp.broadcast_to(row, (8, 256))
        came[i] = jnp.zeros((128, LANES), F32)
        came_rows[i] = jnp.zeros((8, 256), F32)
        return 0

    def arrive(s):
        chain.arrive(s)

        def one(p, _):
            i = s * pairs + p
            came[i] = chain.in_state[i].astype(F32)
            came_rows[i] = chain.in_rows[i]
            return 0

        lax.fori_loop(0, pairs, one, 0)

    def leave(s):
        def one(p, _):
            i = s * pairs + p
            n = lanes_of(p)
            total = came[i] + own[i]
            low = total.astype(BF16)
            chain.out_state[i] = low
            lost = unpack(total - low.astype(F32), block_mask(256, LANES)).astype(BF16)
            mean = column_sum(v[pl.ds(s * local, local), n].astype(F32)) * (1.0 / local)
            row = dot_t(jnp.broadcast_to(mean, (8, LANES)).astype(BF16), lost)
            chain.out_rows[i] = came_rows[i] + own_rows[i] + row
            return 0

        lax.fori_loop(0, pairs, one, 0)
        chain.start(s)

    def main(i, _):
        s, p = i // pairs, i % pairs
        n = lanes_of(p)
        first, second, one, two = head_masks()
        mask = block_mask(256, LANES)
        ones = jnp.ones((CHUNK, LANES), BF16)
        m = within[s]
        m = jnp.concatenate([m, m], axis=0)
        for c in range(count):
            r = rows_of(s, c, local)
            cosine, sine = cos_s[r], sin_s[r]
            feature, key, value = q[r, n].astype(F32), k[r, n], v[r, n]
            gnum, gden, lane = gnum_s[r, n], gden_s[r, n], lane_s[r, n].astype(F32)
            row = rows_in[i * count + c][0:1]
            outer = dot_t(twice(gnum), states[i * count + c]) + twice(gden) * row
            gq = outer[:, :LANES] * cosine + outer[:, LANES:] * sine
            heads = stacked_heads(feature, first, second)
            scores = (dot_t(heads, key) * m).astype(BF16)
            gheads = stacked_heads(gnum.astype(F32), first, second)
            left = jnp.concatenate([gheads, stacked_heads(lane, first, second)], axis=1)
            g = (dot_t(left, jnp.concatenate([value, ones], axis=1)) * m).astype(BF16)
            inner = dot(g, key)
            gq = gq + jnp.where(first > 0, inner[:CHUNK], inner[CHUNK:])
            state, row = came[i], came_rows[i][0:1]
            if c + 1 < count:
                state = state + part[i * (count - 1) + c]
                row = row + part_rows[i * (count - 1) + c][0:1]
            state = two_parts(unpack(state, mask))
            k2 = spread(key.astype(F32), cosine, sine)
            gv = dot(k2, state[:, :LANES]) + tdot(gheads, scores).T
            outer = dot_t(twice(value), state) + row
            gk = outer[:, :LANES] * cosine + outer[:, LANES:] * sine + tdot(heads, g).T
            out[r, n] = (gq * slope(feature)).astype(BF16)
            out[r, pl.ds(pl.multiple_of(width + p * LANES, LANES), LANES)] = (
                gk * slope(key.astype(F32))
            ).astype(BF16)
            out[r, pl.ds(pl.multiple_of(2 * width + p * LANES, LANES), LANES)] = gv.astype(BF16)
        return 0

    lax.fori_loop(0, groups * pairs, sums, 0)

    @pl.when(chain.is_first)
    def _():
        for s in range(groups):
            leave(s)

    @pl.when(jnp.logical_not(chain.is_first))
    def _():
        for s in range(groups):
            arrive(s)

            @pl.when(jnp.logical_not(chain.is_last))
            def _():
                leave(s)

    lax.fori_loop(0, groups * pairs, main, 0)

    @pl.when(jnp.logical_not(chain.is_last))
    def _():
        for s in range(groups):
            chain.sent(s)


def input_kernel(tok, gm, weight, g_first, grad, gw, gb):
    @pl.when(pl.program_id(0) == 0)
    def _():
        gw[...] = jnp.zeros_like(gw)
        gb[...] = jnp.zeros_like(gb)

    low = gm[...]
    gb[...] += column_sum(low.astype(F32))
    gw[...] += tdot(tok[...], low)
    grad[...] = g_first[...] + dot_t(low, weight[...])


def peers():
    dp, z = lax.axis_index("dp"), lax.axis_index("head")
    core, x, y = lax.rem(dp, 2), lax.rem(dp // 2, 2), dp // 4
    twin = dp + 1 - 2 * core
    along_x, along_y = dp + 2 - 4 * x, dp + 4 - 8 * y
    one = along_x + core * (along_y - along_x)
    two = along_y + core * (along_x - along_y)
    return dp, z, twin, one, two, one + two - dp


class Copies:
    def __init__(self, send, recv):
        self.send, self.recv, self.all = send, recv, []

    def start(self, a, slot, src, dst, target):
        copy = pltpu.make_async_remote_copy(
            src_ref=src, dst_ref=dst, send_sem=self.send.at[a, slot], recv_sem=self.recv.at[a, slot],
            device_id=target, device_id_type=MESH,
        )
        copy.start()
        self.all.append(copy)
        return copy

    def finish(self):
        for copy in self.all:
            copy.wait_send()


class Gather:
    def __init__(self, arrays, send, recv):
        self.arrays = arrays
        self.copies, self.had = Copies(send, recv), {}
        self.dp, self.z, twin, one, two, self.far = peers()
        self.me = self.dp * 4 + self.z
        self.one, self.two = one, two
        self.to_z = [{"dp": self.dp, "head": lax.rem(self.z + k, 4)} for k in (1, 2, 3)]
        self.to_twin, self.to_one, self.to_two = (
            {"dp": d, "head": self.z} for d in (twin, one, two)
        )

    def targets(self):
        return self.to_z + [self.to_twin, self.to_one, self.to_two]

    def begin(self, a):
        ref, low, rows, fine = self.arrays[a]
        place = ref.at[self.me, pl.ds(low, rows)]
        for k in range(3):
            self.had[a, k] = self.copies.start(a, k, place, place, self.to_z[k])
        if fine:
            self.pass_one(a, 0, self.dp, ((3, self.to_one), (7, self.to_two), (15, self.to_twin)))

    def pass_one(self, a, k, block, ways):
        ref, low, rows, _ = self.arrays[a]
        place = ref.at[block * 4 + lax.rem(self.z + 4 - k, 4), pl.ds(low, rows)]
        for slot, target in ways:
            self.had[a, slot + k] = self.copies.start(a, slot + k, place, place, target)

    def fine_stage(self, a, g):
        if g == 5:
            for slot in range(15, 31):
                self.had[a, slot].wait_recv()
            return
        if g < 3:
            self.had[a, g].wait_recv()
            self.pass_one(a, g + 1, self.dp, ((3, self.to_one), (7, self.to_two), (15, self.to_twin)))
        if g < 4:
            self.had[a, 3 + g].wait_recv()
            self.pass_one(a, g, self.one, ((11, self.to_two), (19, self.to_twin)))
            self.had[a, 7 + g].wait_recv()
            self.pass_one(a, g, self.two, ((23, self.to_twin),))
        if g > 0:
            self.had[a, 10 + g].wait_recv()
            self.pass_one(a, g - 1, self.far, ((27, self.to_twin),))

    def pass_on(self, a, slot, block, target):
        ref, low, rows, _ = self.arrays[a]
        place = ref.at[pl.ds(block * 4, 4), pl.ds(low, rows)]
        self.had[a, slot] = self.copies.start(a, slot, place, place, target)

    def stage(self, a, step):
        if self.arrays[a][3]:
            self.fine_stage(a, step)
        elif step == 0:
            for k in range(3):
                self.had[a, k].wait_recv()
            self.pass_on(a, 3, self.dp, self.to_one)
            self.pass_on(a, 4, self.dp, self.to_two)
            self.pass_on(a, 5, self.dp, self.to_twin)
        elif step == 1:
            self.had[a, 3].wait_recv()
            self.pass_on(a, 6, self.one, self.to_two)
            self.pass_on(a, 7, self.one, self.to_twin)
        elif step == 2:
            self.had[a, 4].wait_recv()
            self.pass_on(a, 8, self.two, self.to_twin)
        elif step == 3:
            self.had[a, 6].wait_recv()
            self.pass_on(a, 9, self.far, self.to_twin)
        elif step == 4:
            for slot in (5, 7, 8, 9):
                self.had[a, slot].wait_recv()

    def finish(self):
        self.copies.finish()


class Scatter:
    def __init__(self, arrays, send, recv, place=lambda dp: dp * 4):
        self.arrays, self.place = arrays, place
        self.copies, self.had = Copies(send, recv), {}
        self.dp, self.z, self.twin, self.one, self.two, self.far = peers()
        self.to_z = [{"dp": self.dp, "head": lax.rem(self.z + k, 4)} for k in (1, 2, 3)]
        self.to_twin, self.to_one, self.to_two = (
            {"dp": d, "head": self.z} for d in (self.twin, self.one, self.two)
        )

    def targets(self):
        return self.to_z + [self.to_twin, self.to_one, self.to_two]

    def send(self, a, slot, src, count, box, target):
        buf, boxes, _, low, rows = self.arrays[a]
        some = pl.ds(low, rows)
        self.had[a, slot] = self.copies.start(
            a, slot, buf.at[pl.ds(src, count), some], boxes.at[pl.ds(box, count), some], target
        )

    def begin(self, a):
        shift = self.twin - self.dp
        for slot, dp in enumerate((self.far, self.one, self.two, self.dp)):
            self.send(a, slot, self.place(dp + shift), 4, slot * 4, self.to_twin)

    def wait(self, a, *slots):
        for slot in slots:
            self.had[a, slot].wait_recv()

    def add(self, a, dp, slots):
        buf, box, _, low, rows = self.arrays[a]
        start, some = self.place(dp), pl.ds(low, rows)

        def one(j, _):
            total = buf[start + j, some].astype(F32)
            for slot in slots:
                total = total + box[slot * 4 + j, some].astype(F32)
            buf[start + j, some] = total.astype(BF16)
            return 0

        lax.fori_loop(0, 4, one, 0)

    def stage(self, a, step):
        if step == 0:
            self.wait(a, 0)
            self.add(a, self.far, (0,))
            self.send(a, 4, self.place(self.far), 4, 16, self.to_two)
            self.wait(a, 1)
            self.add(a, self.two, (1,))
            self.send(a, 5, self.place(self.two), 4, 20, self.to_two)
        elif step == 1:
            self.wait(a, 2, 4)
            self.add(a, self.one, (2, 4))
            self.send(a, 6, self.place(self.one), 4, 24, self.to_one)
        elif step == 2:
            self.wait(a, 3, 5, 6)
            self.add(a, self.dp, (3, 5, 6))
            for k in range(3):
                self.send(a, 7 + k, self.place(self.dp) + lax.rem(self.z + k + 1, 4), 1, 28 + k, self.to_z[k])
        elif step == 3:
            self.wait(a, 7, 8, 9)
            buf, box, out, low, rows = self.arrays[a]
            some = pl.ds(low, rows)
            total = buf[self.place(self.dp) + self.z, some].astype(F32)
            for k in range(3):
                total = total + box[28 + k, some].astype(F32)
            have, cols = out.shape[0], total.shape[1]
            if have >= low + rows:
                out[low : low + rows] = total
            else:
                for j in range(rows // have):
                    m = (low // have + j) * cols
                    out[:, m : m + cols] = total[j * have : (j + 1) * have]

    def finish(self):
        self.copies.finish()


class Total:
    def __init__(self, scatter, value, box, send, recv):
        self.value, self.box, self.to = value, box, scatter
        self.copies, self.had = Copies(send, recv), {}

    def pass_on(self, slot, target):
        self.had[slot] = self.copies.start(0, slot, self.value.at[slot if slot < 3 else 3], self.box.at[slot], target)

    def stage(self, step):
        value, box = self.value, self.box
        targets = (self.to.to_twin, self.to.to_two, self.to.to_one)
        if step > 0 and step < 4:
            self.had[step - 1].wait_recv()
            value[step] = value[step - 1] + box[step - 1]
        if step < 3:
            self.pass_on(step, targets[step])
        elif step == 3:
            for k in range(3):
                self.pass_on(3 + k, self.to.to_z[k])
        elif step == 4:
            for k in range(3):
                self.had[3 + k].wait_recv()
            value[4] = (value[3] + box[3]) + (box[4] + box[5])

    def finish(self):
        self.copies.finish()


def fold_block(block, parts=2):
    cols = block.shape[1] // parts
    return jnp.concatenate([block[:, j * cols : (j + 1) * cols] for j in range(parts)], axis=0).astype(BF16)


def unfold_into(out, blocks, rows):
    n, have, cols = blocks.shape

    def body(j, _):
        pair = [blocks[2 * j + i].astype(F32) for i in (0, 1)]
        r = pl.ds(pl.multiple_of(2 * rows * j, 2 * rows), 2 * rows)
        for m in range(have // rows):
            both = jnp.concatenate([item[m * rows : (m + 1) * rows] for item in pair], axis=0)
            out[r, m * cols : (m + 1) * cols] = both.astype(BF16)
        return 0

    lax.fori_loop(0, n // 2, body, 0)


def unpack_vectors(slabs, out, sizes, some):
    n, _, lanes = slabs.shape
    step = 768
    for size in sorted({sizes[j] for j in some}):
        for at in range(0, n * size, step):
            lane = iota((1, step), 1) + at
            owner = lane // size
            places = (iota((lanes, step), 0) == lane - owner * size).astype(BF16)
            mine = (iota((n, step), 0) == owner).astype(F32)
            for j in some:
                if sizes[j] == size:
                    out[j : j + 1, at : at + step] = column_sum(dot(slabs[:, j, :].astype(BF16), places) * mine)


def front_kernel(
    groups, local, sizes, lens, tok, slab, s_in, s_out, s_up,
    q_h, k_h, v_h, joined_h, rest_h, inverse_h, states_h, rows_out, wq_h, wk_h, wv_h, wout_h, wup_h, vectors,
    cos_s, sin_s, ok_s, within, own, own_rows, part, part_rows, came, came_rows, num_s, den_s,
    q, k, v, joined, rest, inverse, states, w_q, w_k, w_v, w_out, w_up, save_sem,
    g_vec, g_q, g_k, g_v, g_out, g_up, g_send, g_recv, *link,
):
    width = tok.shape[1]
    pairs = width // LANES
    chain = Chain(1, pairs, link)
    saved = []

    def save(*pairs_of_refs):
        for src, dst in pairs_of_refs:
            saved.append(pltpu.make_async_copy(src, dst, save_sem.at[len(saved)]))
            saved[-1].start()

    half = g_up.shape[1] // 2
    arrays = [(ref, 0, ref.shape[1], True) for ref in (g_vec, g_k, g_v, g_q)]
    arrays += [(g_out, 0, g_out.shape[1], False), (g_up, 0, half, False), (g_up, half, half, False)]
    gather = Gather(arrays, g_send, g_recv)
    me = gather.me
    g_vec[me] = slab[...].astype(BF16).astype(F32)
    for j, ref in ((1, g_k), (2, g_v), (0, g_q)):
        ref[me] = fold_block(s_in[:, j * width : (j + 1) * width])
    meet(gather.targets())
    for a in range(4):
        gather.begin(a)
    g_out[me] = fold_block(s_out[...])
    g_up[me] = fold_block(s_up[...], 4)
    starts = (0, 0, 1, 2, 5, 6, 7)

    def wave(t):
        for a in range(7):
            if 0 <= t - starts[a] < (6 if a < 4 else 5):
                gather.stage(a, t - starts[a])

    work = Forward(
        groups, local, lens, chain, (q, k, v, joined, rest, inverse, states, rows_out),
        (cos_s, sin_s, ok_s, within, num_s, den_s), (own, own_rows, part, part_rows, came, came_rows),
    )
    sums, arrive, leave, intra, inter = work.steps()
    work.prepare()
    wave(0)
    wave(1)
    for a in range(4, 7):
        gather.begin(a)
    for t in range(2, 6):
        wave(t)
    unpack_vectors(g_vec, vectors, sizes, (0,))
    bias = vectors.at[0:1]
    unfold_into(w_k, g_k, s_in.shape[0])
    work.project(1, tok, w_k, bias)
    wave(6)
    unfold_into(w_v, g_v, s_in.shape[0])
    work.project(2, tok, w_v, bias)

    def relay(at, *some):
        @pl.when(chain.at == at)
        def _():
            for s in some:
                arrive(s)
                if at < 3:
                    leave(s)

    for s in range(groups):
        work.over(sums, s)
        pl.when(chain.is_first)(functools.partial(leave, s))
    wave(7)
    unfold_into(w_q, g_q, s_in.shape[0])
    work.project(0, tok, w_q, bias)
    save((q, q_h), (k, k_h), (v, v_h), (w_q, wq_h), (w_k, wk_h), (w_v, wv_h))
    relay(1, 0)
    wave(8)
    work.over(intra, 0)
    relay(1, 1)
    wave(9)
    work.over(intra, 1)
    relay(1, 2)
    relay(2, 0)
    unpack_vectors(g_vec, vectors, sizes, range(1, 8))
    wave(10)
    unfold_into(w_out, g_out, s_out.shape[0])
    work.over(intra, 2)
    relay(2, 1)
    wave(11)
    relay(2, 2)
    unfold_into(w_up, g_up, s_up.shape[0])
    save((w_out, wout_h), (w_up, wup_h))
    for s in range(groups):
        relay(3, s)
        work.over(inter, s)
        r = pl.ds(s * local, local)
        u = pl.ds(s * pairs * work.count, pairs * work.count)
        save((joined.at[r], joined_h.at[r]), (rest.at[r], rest_h.at[r]), (inverse.at[r], inverse_h.at[r]))
        save((states.at[u], states_h.at[u]))

    @pl.when(jnp.logical_not(chain.is_last))
    def _():
        for s in range(groups):
            chain.sent(s)

    gather.finish()
    for copy in saved:
        copy.wait()


TALL = 384


def by_eight(x):
    return jnp.sum(x.reshape(x.shape[0] // 8, 8, x.shape[1]), axis=0)


def middle_kernel(
    tok_h, joined_h, cot_h, w_out, up_h, s_down, vectors,
    act_h, first_h, gj_h, gup_h, gout_h, gw_down, small,
    low, joined, cot, branch, norm, sec, inv, hid, der, w_up, w_dn, box, xa, xb, fold_s, acc, acc_up,
    io, g_send, g_recv, r_send, r_recv,
):
    rows, width = joined.shape
    ff = w_up.shape[1]
    chunks = ff // width
    tiles = rows // TALL
    slabs = TALL // 96
    depth = rows // 96
    _, b_out, g_one, s_one, b_up, b_down, g_two, s_two = (
        (lambda j: lambda at=0, n=width: vectors[j : j + 1, at : at + n])(j) for j in range(8)
    )
    gather = Gather([(w_dn, 0, w_dn.shape[1], True)], g_send, g_recv)
    scatter = Scatter(
        [(hid, box, gw_down, 0, 48), (hid, box, gw_down, 48, 48)],
        r_send, r_recv, lambda dp: depth * (dp // 2) + 4 * lax.rem(dp, 2),
    )
    loads = [
        pltpu.make_async_copy(src, dst, io.at[j])
        for j, (src, dst) in enumerate(((joined_h, joined), (tok_h, low), (up_h, w_up), (cot_h, cot)))
    ]
    for load in loads:
        load.start()
    w_dn[gather.me] = s_down[...].astype(BF16)
    meet(gather.targets())
    gather.begin(0)
    acc[...] = jnp.zeros_like(acc)
    acc_up[...] = jnp.zeros_like(acc_up)

    def tile(t):
        return pl.ds(t * TALL, TALL) if isinstance(t, int) else pl.ds(pl.multiple_of(t * TALL, TALL), TALL)

    def of_chunk(ref, j, t=None):
        if t is None:
            return ref[pl.ds(depth * j, depth)].reshape(rows, width)
        return ref[pl.ds(depth * j + slabs * t, slabs)].reshape(TALL, width)

    def down_chunk(j):
        return w_dn[pl.ds(8 * j, 8)].reshape(width, width)

    loads[0].wait()
    loads[1].wait()
    def rows32(t, i):
        return pl.ds(pl.multiple_of(t * TALL + i, 32), 32)

    def by_tiles(body, low=0, high=tiles):
        def both(u, _):
            for i in range(2):
                body(2 * u + i, (xa, xb)[i])
            return 0

        lax.fori_loop(low // 2, high // 2, both, 0)

    def enter(t, x):
        x[...] = dot(joined[tile(t)], w_out[...])
        for i in range(0, TALL, 32):
            r = rows32(t, i)
            unit, scale = normalised(low[r].astype(F32) + (x[i : i + 32] + b_out()))
            norm[r] = unit
            inv[r] = jnp.broadcast_to(scale, (32, LANES))
            low[r] = (unit * g_one() + s_one()).astype(BF16)

    by_tiles(enter)
    gather.stage(0, 0)
    loads[2].wait()

    def up(t, _):
        for j in range(chunks):
            x = (xa, xb)[j % 2]
            x[...] = dot(low[tile(t)], w_up[:, j * width : (j + 1) * width])
            for i in range(slabs):
                for m in range(0, 96, 32):
                    for n in range(0, width, 256):
                        y, d = gelu_both(x[96 * i + m : 96 * i + m + 32, n : n + 256] + b_up(j * width + n, 256))
                        hid[depth * j + slabs * t + i, m : m + 32, n : n + 256] = y.astype(BF16)
                        der[depth * j + slabs * t + i, m : m + 32, n : n + 256] = d.astype(BF16)
        return 0

    for t in range(tiles):
        lax.fori_loop(t, t + 1, up, 0)
        gather.stage(0, t + 1)
    gather.stage(0, 5)
    loads[3].wait()

    def second(t, x):
        x[...] = dot(of_chunk(hid, 0, t), down_chunk(0))
        for j in range(1, chunks):
            x[...] += dot(of_chunk(hid, j, t), down_chunk(j))
        for i in range(0, TALL, 32):
            r = rows32(t, i)
            unit, scale = normalised(norm[r] * g_one() + (s_one() + b_down()) + x[i : i + 32])
            c = cot[r].astype(F32)
            cot[r] = (unit * g_two() + s_two()).astype(BF16)
            acc[4] += by_eight(c * unit)
            acc[5] += by_eight(c)
            e = c * g_two()
            g = scale * (e - mean_of(e) - unit * mean_of(e * unit))
            sec[r] = g
            g = g.astype(BF16)
            branch[r] = g
            acc[3] += by_eight(g.astype(F32))

    by_tiles(second)
    act = pltpu.make_async_copy(cot, act_h, io.at[3])
    act.start()
    for j in range(chunks):
        for m in range(2):
            x = (xa, xb)[m]
            x[...] = tdot(
                hid[pl.ds(depth * j, depth), :, m * TALL : (m + 1) * TALL].reshape(rows, TALL), branch[...]
            )
        for m in range(2):
            hid[pl.ds(depth * j + 4 * m, 4)] = (xa, xb)[m][...].astype(BF16).reshape(4, 96, width)
    scatter.begin(0)
    scatter.begin(1)

    def back(t, _):
        for j in range(chunks):
            x = (xa, xb)[j % 2]
            x[...] = dot_t(branch[tile(t)], down_chunk(j))
            for i in range(slabs):
                for m in range(0, 96, 32):
                    at = depth * j + slabs * t + i
                    g = x[96 * i + m : 96 * i + m + 32] * der[at, m : m + 32].astype(F32)
                    g = g.astype(BF16)
                    der[at, m : m + 32] = g
                    acc_up[:, j * width : (j + 1) * width] += by_eight(g.astype(F32))
        return 0

    lax.fori_loop(0, tiles // 2, back, 0)
    scatter.stage(0, 0)
    lax.fori_loop(tiles // 2, tiles, back, 0)
    scatter.stage(1, 0)
    out = []

    def first(t, x):
        x[...] = dot_t(of_chunk(der, 0, t), w_up[:, 0:width])
        for j in range(1, chunks):
            x[...] += dot_t(of_chunk(der, j, t), w_up[:, j * width : (j + 1) * width])
        for i in range(0, TALL, 32):
            r = rows32(t, i)
            g = sec[r] + x[i : i + 32]
            unit = norm[r]
            acc[1] += by_eight(g * unit)
            acc[2] += by_eight(g)
            e = g * g_one()
            g = inv[r, 0:1] * (e - mean_of(e) - unit * mean_of(e * unit))
            sec[r] = g
            g = g.astype(BF16)
            branch[r] = g
            acc[0] += by_eight(g.astype(F32))

    by_tiles(first)
    out.append(pltpu.make_async_copy(sec, first_h, io.at[0]))
    out[-1].start()
    scatter.stage(0, 1)
    gather.finish()
    for m in range(2):
        for jj in range(chunks // 2):
            for i in range(2):
                (xa, xb)[i][...] = tdot(low[:, m * TALL : (m + 1) * TALL], of_chunk(der, 2 * jj + i))
            for i in range(16):
                both = [x[24 * i : 24 * i + 24] for x in (xa, xb)]
                w_dn[16 * m + i, 48 * jj : 48 * jj + 48] = jnp.concatenate(both, axis=0).astype(BF16)
        scatter.stage(1 - m, 1 + m)
    out.append(pltpu.make_async_copy(w_dn, gup_h, io.at[1]))
    out[-1].start()
    for m in range(2):
        x = (xa, xb)[m]
        x[...] = tdot(joined[:, m * TALL : (m + 1) * TALL], branch[...])
        for i in range(16):
            fold_s[16 * m + i] = fold_block(x[24 * i : 24 * i + 24])
    out.append(pltpu.make_async_copy(fold_s, gout_h, io.at[2]))
    out[-1].start()
    scatter.stage(1, 2)
    for t in range(tiles):
        joined[tile(t)] = dot_t(branch[tile(t)], w_out[...]).astype(BF16)
    out.append(pltpu.make_async_copy(joined, gj_h, io.at[4]))
    out[-1].start()
    small[...] = jnp.zeros_like(small)
    for row, at in ((3, 0), (4, 1), (5, 2), (10, 3), (11, 4), (12, 5)):
        small[row : row + 1] = column_sum(acc[at])
    for j in range(chunks):
        small[6 + j : 7 + j] = column_sum(acc_up[:, j * width : (j + 1) * width])
    scatter.stage(0, 3)
    scatter.stage(1, 3)
    act.wait()
    for copy in out:
        copy.wait()
    scatter.finish()


def tail_kernel(
    groups, local, lens, q_h, k_h, v_h, gj_h, joined_h, rest_h, inverse_h, states, rows_in,
    tok_h, wq_h, wk_h, wv_h, first_h, up_h, out_h, small,
    grad_h, gw_up, gw_out, gw_q, gw_k, gw_v, small_out,
    q, k, v, gnum, joined, lane_s, inverse, cos_s, sin_s, within,
    own, own_rows, part, part_rows, came, came_rows, slots, load_sem, slot_sem,
    b_up, b_out, b_q, b_k, b_v, x_up, x_out, x_q, x_k, x_v,
    value, box, r_send, r_recv, t_send, t_recv, *link,
):
    width = q.shape[1]
    rows = q.shape[0]
    pairs = width // LANES
    count = local // CHUNK
    chain = Chain(-1, pairs, link)
    half = b_up.shape[1] // 2
    arrays = [(b_up, x_up, gw_up, 0, half), (b_up, x_up, gw_up, half, half)]
    arrays += [
        (buf, box, out, 0, buf.shape[1])
        for buf, box, out in ((b_out, x_out, gw_out), (b_q, x_q, gw_q), (b_k, x_k, gw_k), (b_v, x_v, gw_v))
    ]
    scatter = Scatter(arrays, r_send, r_recv)
    total = Total(scatter, value, box, t_send, t_recv)
    places = (
        (inverse_h, inverse), (gj_h, gnum), (joined_h, joined), (rest_h, lane_s), (q_h, q),
        (up_h, b_up), (out_h, b_out), (k_h, k), (v_h, v),
    )
    loads = [pltpu.make_async_copy(src, dst, load_sem.at[j]) for j, (src, dst) in enumerate(places)]
    for load in loads:
        load.start()
    meet(scatter.targets())
    fill_tables(groups, local, chain.at * local, lens, cos_s, sin_s, None, within)

    def sums(i, _):
        s, p = i // pairs, i % pairs
        n = lanes_of(p)
        _, _, one, two = head_masks()
        mask = block_mask(256, LANES)
        ones = block_mask(2 * LANES, LANES).astype(BF16)
        state = jnp.zeros((256, LANES), F32)
        row = jnp.zeros((1, 256), F32)
        for c in reversed(range(count)):
            r = rows_of(s, c, local)
            ri = inverse[r, n].astype(F32)
            gn = (gnum[r, n].astype(F32) * jnp.abs(ri)).astype(BF16)
            product = gn.astype(F32) * (joined[r, n].astype(F32) + lane_s[r, n].astype(F32))
            gden = jnp.where(ri > 0, -dot(two_parts(product), ones), 0.0)
            high = gden.astype(BF16).astype(F32)
            gnum[r, n] = gn
            lane_s[r, n] = (high * one + (gden - high) * two).astype(BF16)
            q2 = spread(q[r, n].astype(F32), cos_s[r], sin_s[r])
            state = state + tdot(q2, gn)
            row = row + column_sum(q2.astype(F32) * twice(gden))
            if c > 0:
                part[i * (count - 1) + c - 1] = pack(state * mask)
                part_rows[i * (count - 1) + c - 1] = jnp.broadcast_to(row, (8, 256))
        own[i] = pack(state * mask)
        own_rows[i] = jnp.broadcast_to(row, (8, 256))
        came[i] = jnp.zeros((128, LANES), F32)
        came_rows[i] = jnp.zeros((8, 256), F32)
        return 0

    def arrive(s):
        chain.arrive(s)

        def one(p, _):
            i = s * pairs + p
            came[i] = chain.in_state[i].astype(F32)
            came_rows[i] = chain.in_rows[i]
            return 0

        lax.fori_loop(0, pairs, one, 0)

    def leave(s):
        def one(p, _):
            i = s * pairs + p
            n = lanes_of(p)
            state = came[i] + own[i]
            low = state.astype(BF16)
            chain.out_state[i] = low
            lost = unpack(state - low.astype(F32), block_mask(256, LANES)).astype(BF16)
            mean = column_sum(v[pl.ds(s * local, local), n].astype(F32)) * (1.0 / local)
            row = dot_t(jnp.broadcast_to(mean, (8, LANES)).astype(BF16), lost)
            chain.out_rows[i] = came_rows[i] + own_rows[i] + row
            return 0

        lax.fori_loop(0, pairs, one, 0)
        chain.start(s)

    def intra(i, _):
        s, p = i // pairs, i % pairs
        n = lanes_of(p)
        first, second, one, two = head_masks()
        ones = jnp.ones((CHUNK, LANES), BF16)
        picks = (block_mask(LANES, LANES) * ((iota((LANES, LANES), 0) & (HALF - 1)) < 2).astype(F32)).astype(BF16)
        m = within[s]
        m = jnp.concatenate([m, m], axis=0)
        for c in range(count):
            r = rows_of(s, c, local)
            feature, key, value_low, gn, lane = q[r, n].astype(F32), k[r, n], v[r, n], gnum[r, n], lane_s[r, n]
            gden = dot(lane, picks)
            row = rows_in[i * count + c][0:1]
            outer = dot_t(twice(gn), states[i * count + c]) + twice(gden) * row
            gq = outer[:, :LANES] * cos_s[r] + outer[:, LANES:] * sin_s[r]
            heads = stacked_heads(feature, first, second)
            scores = (dot_t(heads, key) * m).astype(BF16)
            gheads = stacked_heads(gn.astype(F32), first, second)
            left = jnp.concatenate([gheads, stacked_heads(lane.astype(F32), first, second)], axis=1)
            g = (dot_t(left, jnp.concatenate([value_low, ones], axis=1)) * m).astype(BF16)
            inner = dot(g, key)
            gq = gq + jnp.where(first > 0, inner[:CHUNK], inner[CHUNK:])
            joined[r, n] = tdot(heads, g).T.astype(BF16)
            inverse[r, n] = tdot(gheads, scores).T.astype(BF16)
            q[r, n] = (gq * slope(feature)).astype(BF16)
        return 0

    def inter(i, _):
        s, p = i // pairs, i % pairs
        n = lanes_of(p)
        mask = block_mask(256, LANES)
        for c in range(count):
            r = rows_of(s, c, local)
            cosine, sine, key = cos_s[r], sin_s[r], k[r, n].astype(F32)
            state, row = came[i], came_rows[i][0:1]
            if c + 1 < count:
                state = state + part[i * (count - 1) + c]
                row = row + part_rows[i * (count - 1) + c][0:1]
            state = two_parts(unpack(state, mask))
            outer = dot_t(twice(v[r, n]), state) + row
            gk = outer[:, :LANES] * cosine + outer[:, LANES:] * sine + joined[r, n].astype(F32)
            v[r, n] = (dot(spread(key, cosine, sine), state[:, :LANES]) + inverse[r, n].astype(F32)).astype(BF16)
            k[r, n] = (gk * slope(key)).astype(BF16)
        return 0

    def over(step, s, low=0, high=pairs):
        lax.fori_loop(s * pairs + low, s * pairs + high, step, 0)

    def weight_terms(a, g):
        buf = scatter.arrays[a][0]
        size = width // 32
        for j in range(2):
            term = tdot(gnum[:, j * (width // 2) : (j + 1) * (width // 2)], g[...])
            for i in range(16):
                buf[16 * j + i] = fold_block(term[i * size : (i + 1) * size])

    for load in loads[:5]:
        load.wait()
    loads[5].wait()
    scatter.begin(0)
    scatter.begin(1)
    loads[6].wait()
    scatter.begin(2)
    for load in loads[7:]:
        load.wait()
    for s in reversed(range(groups)):
        over(sums, s)
        pl.when(chain.is_first)(functools.partial(leave, s))
    scatter.stage(0, 0)

    def relay(place, *some):
        @pl.when(chain.at == place)
        def _():
            for s in some:
                arrive(s)
                if place > 0:
                    leave(s)

    cut = pairs // 2
    over(intra, 0, 0, cut)
    scatter.stage(1, 0)
    over(intra, 0, cut, pairs)
    relay(2, 2)
    scatter.stage(2, 0)
    over(intra, 1, 0, cut)
    relay(2, 1)
    scatter.stage(0, 1)
    over(intra, 1, cut, pairs)
    relay(2, 0)
    relay(1, 2)
    scatter.stage(1, 1)
    over(intra, 2, 0, cut)
    relay(1, 1)
    scatter.stage(0, 2)
    scatter.stage(2, 1)
    over(intra, 2, cut, pairs)
    relay(1, 0)
    scatter.stage(1, 2)
    tok_load = pltpu.make_async_copy(tok_h, gnum, load_sem.at[0])
    w_loads = [
        pltpu.make_async_copy(wq_h, lane_s.at[pl.ds(0, width)], load_sem.at[1]),
        pltpu.make_async_copy(wk_h, lane_s.at[pl.ds(width, width)], load_sem.at[2]),
        pltpu.make_async_copy(wv_h, joined.at[pl.ds(0, width)], load_sem.at[3]),
    ]
    for load in [tok_load] + w_loads[:2]:
        load.start()
    tok_load.wait()
    weight_terms(3, q)
    scatter.begin(3)
    steps = (((2, 2), (0, 3)), ((1, 3), (3, 0)), ((2, 3),))
    for j, s in enumerate(reversed(range(groups))):
        relay(0, s)
        over(inter, s)
        for a, step in steps[j]:
            scatter.stage(a, step)
    w_loads[2].start()
    weight_terms(4, k)
    scatter.begin(4)
    scatter.stage(3, 1)
    weight_terms(5, v)
    scatter.begin(5)
    value[0] = small[...]
    for j, ref in enumerate((q, k, v)):
        value[0, j : j + 1, :] = column_sum(ref[...].astype(F32))
    total.stage(0)
    for load in w_loads:
        load.wait()

    def slot(i):
        return slots.at[i % 3]

    def rows_at(ref, i):
        return ref.at[pl.ds(i * CHUNK, CHUNK)]

    n_slots = rows // CHUNK
    fetch = [pltpu.make_async_copy(rows_at(first_h, i), slot(i), slot_sem.at[i % 3, 0]) for i in range(n_slots)]
    store = [pltpu.make_async_copy(slot(i), rows_at(grad_h, i), slot_sem.at[i % 3, 1]) for i in range(n_slots)]
    fetch[0].start()
    rest_plan = (((4, 0), (3, 2)), ((5, 0),), ((4, 1),), ((5, 1), (3, 3)), ((4, 2),), ((5, 2),))
    for i in range(n_slots):
        if i + 1 < n_slots:
            if i >= 2:
                store[i - 2].wait()
            fetch[i + 1].start()
        fetch[i].wait()
        r = pl.ds(i * CHUNK, CHUNK)
        slots[i % 3] = (
            slots[i % 3]
            + dot_t(q[r], lane_s[pl.ds(0, width)])
            + dot_t(k[r], lane_s[pl.ds(width, width)])
            + dot_t(v[r], joined[pl.ds(0, width)])
        )
        store[i].start()
        for a, step in rest_plan[i] if i < len(rest_plan) else ():
            scatter.stage(a, step)
        if 1 <= i + 1 < 5:
            total.stage(i + 1)
    scatter.stage(4, 3)
    scatter.stage(5, 3)
    small_out[...] = value[4]
    for i in range(max(n_slots - 3, 0), n_slots):
        store[i].wait()

    @pl.when(jnp.logical_not(chain.is_last))
    def _():
        for s in range(groups):
            chain.sent(s)

    scatter.finish()
    total.finish()


VMEM = pl.BlockSpec(memory_space=pltpu.VMEM)
SMEM = pl.BlockSpec(memory_space=pltpu.SMEM)
ANY = pl.BlockSpec(memory_space=pl.ANY)


def params(collective=None):
    if collective is None:
        return pltpu.CompilerParams(vmem_limit_bytes=BIG)
    return pltpu.CompilerParams(vmem_limit_bytes=BIG, collective_id=collective, has_side_effects=True)


def shape(dims, kind=BF16):
    return jax.ShapeDtypeStruct(dims, kind)


def shards(
    tokens, lengths, weight_in, bias_in, weight_out, bias_out, gain_one, shift_one,
    weight_up, bias_up, weight_down, bias_down, gain_two, shift_two, cotangent,
):
    groups, local, width = tokens.shape
    rows = groups * local
    pairs = width // LANES
    count = local // CHUNK
    axes = ("dp", "head")
    parts = lax.axis_size("head")
    me = lax.axis_index("head")

    by_kernel = lax.axis_size("dp") == 8 and parts == 4
    small = (bias_in, bias_out, gain_one, shift_one, bias_up, bias_down, gain_two, shift_two)
    tok = tokens.reshape(rows, width)
    units = groups * pairs
    plane = shape((rows, width))
    table = pltpu.VMEM((rows, LANES), F32)
    within = pltpu.VMEM((groups, CHUNK, CHUNK), F32)
    tall = pltpu.VMEM((rows, width), F32)
    flat = pltpu.VMEM((rows, width), BF16)

    def sums_scratch():
        return [
            pltpu.VMEM((units, 128, LANES), F32),
            pltpu.VMEM((units, 8, 256), F32),
            pltpu.VMEM((units * max(count - 1, 1), 128, LANES), F32),
            pltpu.VMEM((units * max(count - 1, 1), 8, 256), F32),
            pltpu.VMEM((units, 128, LANES), F32),
            pltpu.VMEM((units, 8, 256), F32),
        ]

    forward_shapes = (plane,) * 6 + (shape((units * count, 256, 256)), shape((units * count, 8, 256), F32))
    forward_scratch = [table, table, table, within] + sums_scratch() + [tall, tall]
    ff = weight_up.shape[1]
    if by_kernel:
        slab = jnp.stack([jnp.pad(item, (0, LANES - item.shape[0])) for item in small])
        square = shape((width, width))
        sizes = [item.shape[0] for item in small]
        half = (2 * weight_in.shape[0], width // 2)
        (
            q, k, v, joined, rest, inverse, states, state_rows, w_q, w_k, w_v, w_out, w_up, vectors
        ) = pl.pallas_call(
            functools.partial(front_kernel, groups, local, sizes),
            out_shape=forward_shapes
            + (square,) * 4
            + (shape((width, ff)), shape((len(small), ff), F32)),
            in_specs=[SMEM] + [VMEM] * 5,
            out_specs=(ANY,) * 7 + (VMEM,) + (ANY,) * 5 + (VMEM,),
            scratch_shapes=forward_scratch
            + [flat] * 6
            + [pltpu.VMEM((units * count, 256, 256), BF16)]
            + [pltpu.VMEM((width, width), BF16)] * 4
            + [pltpu.VMEM((width, ff), BF16), pltpu.SemaphoreType.DMA((8 + 4 * groups,))]
            + [pltpu.VMEM((32, 8, LANES), F32)]
            + [pltpu.VMEM((32,) + half, BF16)] * 4
            + [pltpu.VMEM((32, 4 * weight_up.shape[0], ff // 4), BF16)]
            + [pltpu.SemaphoreType.DMA((7, 31)), pltpu.SemaphoreType.DMA((7, 31))]
            + chain_scratch(groups, pairs),
            compiler_params=params(3),
        )(lengths, tok, slab, weight_in, weight_out, weight_up)
    else:

        def gather(item):
            return lax.all_gather(item.astype(BF16), axes, axis=0, tiled=True)

        w_in, w_out, w_up, w_down = map(gather, (weight_in, weight_out, weight_up, weight_down))
        sizes = [item.shape[0] for item in small]
        gathered = lax.all_gather(jnp.concatenate([item.astype(BF16) for item in small]), axes, axis=0)
        cuts = [sum(sizes[:i]) for i in range(len(sizes) + 1)]
        b_in, b_out, g_one, s_one, b_up, b_down, g_two, s_two = (
            gathered[:, a:b].reshape(1, -1).astype(F32) for a, b in zip(cuts, cuts[1:])
        )
        w_q, w_k, w_v = (w_in[:, j * width : (j + 1) * width] for j in range(3))
        q, k, v, joined, rest, inverse, states, state_rows = pl.pallas_call(
            functools.partial(attend_kernel, groups, local),
            out_shape=forward_shapes,
            in_specs=[SMEM] + [VMEM] * 5,
            out_specs=(VMEM,) * 8,
            scratch_shapes=forward_scratch + chain_scratch(groups, pairs),
            compiler_params=params(1),
        )(lengths, tok, w_q, w_k, w_v, b_in)

    tile = local

    if by_kernel:
        slabs96 = shape((32, 96, width))
        term_out = shape((32,) + half)
        kept = pltpu.VMEM((rows // 96 * (ff // width), 96, width), BF16)
        tile_s = pltpu.VMEM((TALL, width), F32)
        activations, g_first, g_joined, gw_up, gw_out, gw_down, small_sums = pl.pallas_call(
            middle_kernel,
            out_shape=[
                plane, shape((rows, width), F32), plane, slabs96, term_out,
                shape(weight_down.shape, F32), shape((16, width), F32),
            ],
            in_specs=[ANY] * 3 + [VMEM, ANY, VMEM, VMEM],
            out_specs=[ANY] * 5 + [VMEM] * 2,
            scratch_shapes=[flat] * 4
            + [tall, tall, table, kept, kept]
            + [pltpu.VMEM((width, ff), BF16), pltpu.VMEM((32, 96, width), BF16), pltpu.VMEM((31, 96, width), BF16)]
            + [tile_s, tile_s, pltpu.VMEM((32,) + half, BF16)]
            + [pltpu.VMEM((6, 8, width), F32), pltpu.VMEM((8, ff), F32)]
            + [pltpu.SemaphoreType.DMA((5,))]
            + [pltpu.SemaphoreType.DMA((1, 31))] * 2
            + [pltpu.SemaphoreType.DMA((2, 10))] * 2,
            compiler_params=params(5),
        )(tok, joined, cotangent.reshape(rows, width), w_out, w_up, weight_down, vectors)
        terms = [gw_up.shape, gw_out.shape] + [(32,) + half] * 3
        row_shape = (weight_out.shape[0], width)
        input_grad, gw_up, gw_out, gw_q, gw_k, gw_v, sums = pl.pallas_call(
            functools.partial(tail_kernel, groups, local),
            out_shape=[shape((rows, width), F32), shape(weight_up.shape, F32)]
            + [shape(row_shape, F32)] * 4
            + [shape(small_sums.shape, F32)],
            in_specs=[SMEM] + [ANY] * 7 + [VMEM] * 2 + [ANY] * 7 + [VMEM],
            out_specs=[ANY] + [VMEM] * 6,
            scratch_shapes=[flat] * 7
            + [table, table, within]
            + sums_scratch()
            + [pltpu.VMEM((3, CHUNK, width), F32)]
            + [pltpu.SemaphoreType.DMA((9,)), pltpu.SemaphoreType.DMA((3, 2))]
            + [pltpu.VMEM(item, BF16) for item in terms]
            + [pltpu.VMEM((31,) + item[1:], BF16) for item in terms]
            + [pltpu.VMEM((5,) + small_sums.shape, F32), pltpu.VMEM((6,) + small_sums.shape, F32)]
            + [pltpu.SemaphoreType.DMA((6, 10))] * 2
            + [pltpu.SemaphoreType.DMA((1, 6))] * 2
            + chain_scratch(groups, pairs),
            compiler_params=params(4),
        )(
            lengths, q, k, v, g_joined, joined, rest, inverse, states, state_rows,
            tok, w_q, w_k, w_v, g_first, gw_up, gw_out, small_sums,
        )
        sums = sums.reshape(-1)
        me = lax.axis_index(axes)
        mine, at = [], 0
        for item in (2 * width, width, width, width, width, ff, width, width, width):
            mine.append(lax.dynamic_slice(sums, (at + me * (item // 32),), (item // 32,)))
            at += item
        gb_front, gb_value, gb_out, gg_one, gs_one, gb_up, gb_down, gg_two, gs_two = mine
        return (
            activations.reshape(groups, local, width),
            input_grad.reshape(groups, local, width),
            jnp.concatenate([gw_q, gw_k, gw_v], axis=1), gb_front, gb_value, gw_out, gb_out, gg_one, gs_one,
            gw_up, gb_up, gw_down, gb_down, gg_two, gs_two,
        )

    def block(cols):
        return pl.BlockSpec((tile, cols), lambda i: (i, 0))

    def fixed(*dims):
        return pl.BlockSpec(dims, lambda i: (0,) * len(dims), pipeline_mode=pl.Buffered(1))

    vectors = [fixed(1, width)] * 3 + [fixed(1, ff)] + [fixed(1, width)] * 3
    weights = [fixed(width, width), fixed(width, ff), fixed(ff, width)]
    vector_shapes = [shape((1, width), F32)] * 3 + [shape((1, ff), F32)] + [shape((1, width), F32)] * 3
    (
        activations, g_first, g_joined, gw_out, gw_up, gw_down,
        gb_out, gg_one, gs_one, gb_up, gb_down, gg_two, gs_two,
    ) = pl.pallas_call(
        feed_kernel,
        grid=(rows // tile,),
        out_shape=[plane, shape((rows, width), F32), plane]
        + [shape((width, width), F32), shape((width, ff), F32), shape((ff, width), F32)]
        + vector_shapes,
        in_specs=[block(width)] * 3 + weights + vectors,
        out_specs=[block(width)] * 3 + weights + vectors,
        scratch_shapes=[
            pltpu.VMEM((tile, width), F32),
            pltpu.VMEM((tile, width), BF16),
            pltpu.VMEM((tile, ff), BF16),
            pltpu.VMEM((tile, ff), BF16),
            pltpu.VMEM((tile, width), F32),
            pltpu.VMEM((tile, width), BF16),
        ],
        compiler_params=params(),
    )(
        tok, joined, cotangent.reshape(rows, width), w_out, w_up, w_down,
        b_out, g_one, s_one, b_up, b_down, g_two, s_two,
    )
    g_mixed = pl.pallas_call(
        functools.partial(back_kernel, groups, local),
        out_shape=shape((rows, 3 * width)),
        in_specs=[SMEM] + [VMEM] * 9,
        out_specs=VMEM,
        scratch_shapes=[table, table, within] + sums_scratch()
        + [pltpu.VMEM((rows, width), BF16), tall, pltpu.VMEM((rows, width), BF16)] + chain_scratch(groups, pairs),
        compiler_params=params(2),
    )(lengths, q, k, v, g_joined, joined, rest, inverse, states, state_rows)
    input_grad, gw_in, gb_in = pl.pallas_call(
        input_kernel,
        grid=(rows // tile,),
        out_shape=[shape((rows, width), F32), shape((width, 3 * width), F32), shape((1, 3 * width), F32)],
        in_specs=[block(width), block(3 * width), fixed(width, 3 * width), block(width)],
        out_specs=[block(width), fixed(width, 3 * width), fixed(1, 3 * width)],
        compiler_params=params(),
    )(tok, g_mixed, w_in, g_first)

    gb_in = gb_in.reshape(-1)
    cols = [gb_in[: 2 * width], gb_in[2 * width :]] + [
        item.reshape(-1) for item in (gb_out, gg_one, gs_one, gb_up, gb_down, gg_two, gs_two)
    ]
    total = lax.axis_size(axes)
    def scatter(item):
        return lax.psum_scatter(item, axes, scatter_dimension=0, tiled=True)

    cut = [item.shape[0] // total for item in cols]
    merged = scatter(jnp.concatenate([item.reshape(total, -1) for item in cols], axis=1).reshape(-1))
    places = [sum(cut[:i]) for i in range(len(cut) + 1)]
    (gb_front, gb_value, gb_out, gg_one, gs_one, gb_up, gb_down, gg_two, gs_two) = (
        merged[a:b] for a, b in zip(places, places[1:])
    )
    return (
        activations.reshape(groups, local, width),
        input_grad.reshape(groups, local, width),
        scatter(gw_in), gb_front, gb_value, scatter(gw_out), gb_out, gg_one, gs_one,
        scatter(gw_up), gb_up, scatter(gw_down), gb_down, gg_two, gs_two,
    )


def solution(mesh):
    spread_rows = P("dp", "head", None)
    matrix = P(("dp", "head"), None)
    vector = P(("dp", "head"))
    return jax.shard_map(
        shards,
        mesh=mesh,
        in_specs=(
            spread_rows, P("dp"), matrix, vector, matrix, vector, vector, vector,
            matrix, vector, matrix, vector, vector, vector, spread_rows,
        ),
        out_specs=(
            spread_rows, spread_rows, matrix, vector, vector, matrix, vector, vector, vector,
            matrix, vector, matrix, vector, vector, vector,
        ),
        check_vma=False,
    )
```

```python
import functools
import math

import jax
import jax.numpy as jnp
from jax import lax
from jax.experimental import pallas as pl
from jax.experimental.pallas import tpu as pltpu
from jax.sharding import PartitionSpec as P

F32 = jnp.float32
BF16 = jnp.bfloat16
CHUNK = 256
LANES = 128
HALF = 64
BIG = 62 * 1024 * 1024
MESH = pl.DeviceIdType.MESH


def dot(a, b):
    return lax.dot_general(a, b, (((1,), (0,)), ((), ())), preferred_element_type=F32)


def dot_t(a, b):
    return lax.dot_general(a, b, (((1,), (1,)), ((), ())), preferred_element_type=F32)


def tdot(a, b):
    return lax.dot_general(a, b, (((0,), (0,)), ((), ())), preferred_element_type=F32)


def iota(shape, dim):
    return lax.broadcasted_iota(jnp.int32, shape, dim)


def block_mask(rows, cols):
    return ((iota((rows, cols), 0) & HALF) == (iota((rows, cols), 1) & HALF)).astype(F32)


def head_masks():
    lane = iota((1, LANES), 1)
    first = (lane < HALF).astype(F32)
    place = lane & (HALF - 1)
    return first, 1.0 - first, (place == 0).astype(F32), (place == 1).astype(F32)


def cos_poly(z):
    t = z * z
    r = -1.0 / 3628800 + t * (1.0 / 479001600)
    r = 1.0 / 40320 + t * r
    r = -1.0 / 720 + t * r
    r = 1.0 / 24 + t * r
    r = -0.5 + t * r
    return 1.0 + t * r


def sin_poly(z):
    t = z * z
    r = -1.0 / 39916800 + t * (1.0 / 6227020800)
    r = 1.0 / 362880 + t * r
    r = -1.0 / 5040 + t * r
    r = 1.0 / 120 + t * r
    r = -1.0 / 6 + t * r
    return z + z * (t * r)


def angles(start, limit, rows):
    place = iota((rows, LANES), 0) + start
    theta = jnp.minimum((0.5 * math.pi * place.astype(F32)) / limit.astype(F32), 0.5 * math.pi)
    return cos_poly(theta), sin_poly(theta), (place < limit).astype(F32)


def weights_within(limit):
    apart = iota((CHUNK, CHUNK), 0) - iota((CHUNK, CHUNK), 1)
    theta = jnp.minimum((0.5 * math.pi * apart.astype(F32)) / limit.astype(F32), 0.5 * math.pi)
    return jnp.where(apart >= 0, cos_poly(theta), 0.0)


def softplus(x):
    t = jnp.exp(-jnp.abs(x))
    tail = jnp.where(t < 1e-3, t * (1.0 - 0.5 * t), jnp.log(1.0 + t))
    return jnp.maximum(x, 0.0) + tail


def slope(feature):
    small = feature * (1.0 - feature * (0.5 - feature * (1.0 / 6)))
    return jnp.where(feature < 0.01, small, 1.0 - jnp.exp(-feature))


def pack(state):
    return jnp.concatenate([state[0:64] + state[64:128], state[128:192] + state[192:256]], axis=0)


def unpack(packed, mask):
    top, bottom = packed[0:64], packed[64:128]
    return jnp.concatenate([top, top, bottom, bottom], axis=0) * mask


def column_of(row, first):
    halves = []
    for at in (0, LANES):
        turned = jnp.broadcast_to(row[:, at : at + LANES], (LANES, LANES)).T
        halves.append(jnp.where(first > 0, turned[0:64], turned[64:128]))
    return jnp.concatenate(halves, axis=0)


def two_parts(state):
    high = state.astype(BF16)
    return jnp.concatenate([high, (state - high.astype(F32)).astype(BF16)], axis=1)


def twice(value):
    return jnp.concatenate([value, value], axis=1)


def spread(feature, cosine, sine):
    return jnp.concatenate([feature * cosine, feature * sine], axis=1).astype(BF16)


def stacked_heads(value, first, second):
    return jnp.concatenate([value * first, value * second], axis=0).astype(BF16)


def rows_of(s, c, local):
    return pl.ds(pl.multiple_of(s * local + c * CHUNK, CHUNK), CHUNK)


def lanes_of(p):
    return pl.ds(pl.multiple_of(p * LANES, LANES), LANES)


def fill_tables(groups, local, base, lens, cos_s, sin_s, ok_s, within):
    for s in range(groups):
        cosine, sine, valid = angles(base, lens[s], local)
        cos_s[s * local : (s + 1) * local] = cosine
        sin_s[s * local : (s + 1) * local] = sine
        if ok_s is not None:
            ok_s[s * local : (s + 1) * local] = valid
        within[s] = weights_within(lens[s])


def meet(targets):
    barrier = pltpu.get_barrier_semaphore()
    for target in targets:
        pl.semaphore_signal(barrier, inc=1, device_id=target, device_id_type=MESH)
    pl.semaphore_wait(barrier, len(targets))


class Chain:
    def __init__(self, step, pairs, refs):
        self.at, self.parts, self.pairs = lax.axis_index("head"), lax.axis_size("head"), pairs
        self.out_state, self.out_rows, self.in_state, self.in_rows, self.send, self.recv = refs
        self.before = {"head": lax.rem(self.at + self.parts - step, self.parts)}
        self.after = {"head": lax.rem(self.at + self.parts + step, self.parts)}
        last = self.parts - 1
        self.is_first = self.at == (0 if step > 0 else last)
        self.is_last = self.at == (last if step > 0 else 0)

    def copies(self, s):
        some = pl.ds(s * self.pairs, self.pairs)
        return [
            pltpu.make_async_remote_copy(
                src_ref=src.at[some], dst_ref=dst.at[some],
                send_sem=self.send.at[s, j], recv_sem=self.recv.at[s, j],
                device_id=self.after, device_id_type=MESH,
            )
            for j, (src, dst) in enumerate(
                ((self.out_state, self.in_state), (self.out_rows, self.in_rows))
            )
        ]

    def start(self, s):
        for copy in self.copies(s):
            copy.start()

    def arrive(self, s):
        for copy in self.copies(s):
            copy.wait_recv()

    def sent(self, s):
        for copy in self.copies(s):
            copy.wait_send()


def chain_scratch(groups, pairs):
    return [
        pltpu.VMEM((groups * pairs, 128, LANES), BF16),
        pltpu.VMEM((groups * pairs, 8, 256), F32),
        pltpu.VMEM((groups * pairs, 128, LANES), BF16),
        pltpu.VMEM((groups * pairs, 8, 256), F32),
        pltpu.SemaphoreType.DMA((groups, 2)),
        pltpu.SemaphoreType.DMA((groups, 2)),
    ]


class Forward:
    def __init__(self, groups, local, lens, chain, outs, tables, sums):
        self.groups, self.local, self.lens, self.chain = groups, local, lens, chain
        self.outs, self.tables, self.sums_refs = outs, tables, sums
        self.pairs = outs[0].shape[1] // LANES
        self.count = local // CHUNK

    def prepare(self):
        cos_s, sin_s, ok_s, within = self.tables[:4]
        fill_tables(self.groups, self.local, self.chain.at * self.local, self.lens, cos_s, sin_s, ok_s, within)

    def project(self, piece, tok, weight, bias):
        out, ok_s, width = self.outs[piece], self.tables[2], tok.shape[1]

        def body(i, _):
            r = pl.ds(pl.multiple_of(i * self.local, self.local), self.local)
            for n in range(0, width, 256):
                m = piece * width + n
                y = dot(tok[r], weight[:, n : n + 256]) + bias[:, m : m + 256]
                out[r, n : n + 256] = (softplus(y) * twice(ok_s[r]) if piece < 2 else y).astype(BF16)
            return 0

        lax.fori_loop(0, self.groups, body, 0)

    def over(self, step, s=None):
        low, high = (0, self.groups) if s is None else (s, s + 1)
        lax.fori_loop(low * self.pairs, high * self.pairs, step, 0)

    def names(self):
        return (self.local, self.pairs, self.count, self.chain) + tuple(self.outs) + tuple(self.tables) + tuple(self.sums_refs)

    def steps(self):
        (
            local, pairs, count, chain, q, k, v, joined, rest, inverse, states, rows_out,
            cos_s, sin_s, ok_s, within, num_s, den_s, own, own_rows, part, part_rows, came, came_rows,
        ) = self.names()

        def sums(i, _):
            s, p = i // pairs, i % pairs
            mask = block_mask(256, LANES)
            total = jnp.zeros((256, LANES), F32)
            row = jnp.zeros((1, 256), F32)
            for c in range(count):
                r, n = rows_of(s, c, local), lanes_of(p)
                k2 = spread(k[r, n].astype(F32), cos_s[r], sin_s[r])
                total = total + tdot(k2, v[r, n])
                row = row + column_sum(k2.astype(F32))
                if c + 1 < count:
                    part[i * (count - 1) + c] = pack(total * mask)
                    part_rows[i * (count - 1) + c] = jnp.broadcast_to(row, (8, 256))
            own[i] = pack(total * mask)
            own_rows[i] = jnp.broadcast_to(row, (8, 256))
            came[i] = jnp.zeros((128, LANES), F32)
            came_rows[i] = jnp.zeros((8, 256), F32)
            return 0

        def arrive(s):
            chain.arrive(s)

            def one(p, _):
                i = s * pairs + p
                rows = chain.in_rows[i]
                column = column_of(rows[0:1], head_masks()[0])
                came[i] = chain.in_state[i].astype(F32) + column * rows[1:2, 0:LANES]
                came_rows[i] = rows
                return 0

            lax.fori_loop(0, pairs, one, 0)

        def leave(s):
            def one(p, _):
                i = s * pairs + p
                total = came[i] + own[i]
                row = came_rows[i][0:1] + own_rows[i][0:1]
                column = column_of(row, head_masks()[0])
                centre = column_sum(total) / jnp.maximum(column_sum(column), 1e-30)
                centre = centre.astype(BF16).astype(F32)
                chain.out_state[i] = (total - column * centre).astype(BF16)
                chain.out_rows[i] = jnp.concatenate([row, twice(centre), jnp.zeros((6, 256), F32)], axis=0)
                return 0

            lax.fori_loop(0, pairs, one, 0)
            chain.start(s)

        def intra(i, _):
            s, p = i // pairs, i % pairs
            n = lanes_of(p)
            first, second, _, _ = head_masks()
            ones = jnp.ones((CHUNK, LANES), BF16)
            m = within[s]
            m = jnp.concatenate([m, m], axis=0)
            for c in range(count):
                r = rows_of(s, c, local)
                scores = dot_t(stacked_heads(q[r, n].astype(F32), first, second), k[r, n])
                inner = dot((scores * m).astype(BF16), jnp.concatenate([v[r, n], ones], axis=1))
                both = jnp.where(twice(first) > 0, inner[:CHUNK], inner[CHUNK:])
                num_s[r, n] = both[:, :LANES]
                den_s[r, n] = both[:, LANES:]
            return 0

        def inter(i, _):
            s, p = i // pairs, i % pairs
            n = lanes_of(p)
            mask = block_mask(256, LANES)
            ones = block_mask(LANES, LANES).astype(BF16)
            for c in range(count):
                r = rows_of(s, c, local)
                state, row = came[i], came_rows[i][0:1]
                if c > 0:
                    state = state + part[i * (count - 1) + c - 1]
                    row = row + part_rows[i * (count - 1) + c - 1][0:1]
                state = two_parts(unpack(state, mask))
                states[i * count + c] = state
                rows_out[i * count + c] = jnp.broadcast_to(row, (8, 256))
                q2 = spread(q[r, n].astype(F32), cos_s[r], sin_s[r])
                both = dot(q2, state)
                num = both[:, :LANES] + both[:, LANES:] + num_s[r, n]
                weighed = q2.astype(F32) * row
                weighed = (weighed[:, :LANES] + weighed[:, LANES:]).astype(BF16)
                den = dot(weighed, ones) + den_s[r, n]
                above = 1.0 / jnp.maximum(den, 1.0)
                attended = num * above
                rounded = attended.astype(BF16)
                joined[r, n] = rounded
                rest[r, n] = (attended - rounded.astype(F32)).astype(BF16)
                inverse[r, n] = jnp.where(den > 1.0, above, -1.0).astype(BF16)
            return 0

        return sums, arrive, leave, intra, inter


def attend_kernel(
    groups, local, lens, tok, w_q, w_k, w_v, bias,
    q, k, v, joined, rest, inverse, states, rows_out,
    cos_s, sin_s, ok_s, within, own, own_rows, part, part_rows, came, came_rows, num_s, den_s, *link,
):
    chain = Chain(1, tok.shape[1] // LANES, link)
    meet([chain.before, chain.after])
    work = Forward(
        groups, local, lens, chain, (q, k, v, joined, rest, inverse, states, rows_out),
        (cos_s, sin_s, ok_s, within, num_s, den_s), (own, own_rows, part, part_rows, came, came_rows),
    )
    work.prepare()
    for piece, weight in enumerate((w_q, w_k, w_v)):
        work.project(piece, tok, weight, bias)
    sums, arrive, leave, intra, inter = work.steps()
    work.over(sums)

    @pl.when(chain.is_first)
    def _():
        for s in range(groups):
            leave(s)

    work.over(intra)

    @pl.when(jnp.logical_not(chain.is_first))
    def _():
        for s in range(groups):
            arrive(s)

            @pl.when(jnp.logical_not(chain.is_last))
            def _():
                leave(s)

    work.over(inter)

    @pl.when(jnp.logical_not(chain.is_last))
    def _():
        for s in range(groups):
            chain.sent(s)


def gelu_both(x):
    phi = 0.5 + 0.5 * lax.erf(x * (1.0 / math.sqrt(2.0)))
    return x * phi, phi + x * (jnp.exp(-0.5 * x * x) * (1.0 / math.sqrt(2.0 * math.pi)))


def mean_of(x):
    return jnp.mean(x, axis=1, keepdims=True)


def column_sum(x):
    return jnp.sum(x, axis=0, keepdims=True)


def normalised(x):
    centred = x - mean_of(x)
    inv = lax.rsqrt(mean_of(centred * centred) + 1e-05)
    return centred * inv, inv


def feed_kernel(
    tok, joined, cot, w_out, w_up, w_down, b_out, g_one, s_one, b_up, b_down, g_two, s_two,
    act, g_first, g_joined, gw_out, gw_up, gw_down, gb_out, gg_one, gs_one, gb_up, gb_down, gg_two, gs_two,
    norm_s, low_s, hid_s, der_s, sec_s, branch_s,
):
    rows = tok.shape[0]
    ff = w_up.shape[1]
    step = 768
    count = ff // step

    @pl.when(pl.program_id(0) == 0)
    def _():
        for ref in (gw_out, gw_up, gw_down, gb_out, gg_one, gs_one, gb_up, gb_down, gg_two, gs_two):
            ref[...] = jnp.zeros_like(ref)

    first = tok[...].astype(F32) + (dot(joined[...], w_out[...]) + b_out[...])
    unit_one, inv_one = normalised(first)
    norm_s[...] = unit_one
    normed = unit_one * g_one[...] + s_one[...]
    low_s[...] = normed.astype(BF16)
    sec_s[...] = normed + b_down[...]

    def up(j, _):
        n = pl.ds(pl.multiple_of(j * step, step), step)
        x = dot(low_s[...], w_up[:, n]) + b_up[:, n]
        y, d = gelu_both(x)
        hid_s[:, n] = y.astype(BF16)
        der_s[:, n] = d.astype(BF16)
        return 0

    lax.fori_loop(0, count, up, 0)
    second = sec_s[...] + dot(hid_s[...], w_down[...])
    unit_two, inv_two = normalised(second)
    act[...] = (unit_two * g_two[...] + s_two[...]).astype(BF16)
    c = cot[...].astype(F32)
    gg_two[...] += column_sum(c * unit_two)
    gs_two[...] += column_sum(c)
    e = c * g_two[...]
    g_second = inv_two * (e - mean_of(e) - unit_two * mean_of(e * unit_two))
    sec_s[...] = g_second
    branch = g_second.astype(BF16)
    branch_s[...] = branch
    gb_down[...] += column_sum(branch.astype(F32))

    def down(j, _):
        n = pl.ds(pl.multiple_of(j * step, step), step)
        gh = dot_t(branch_s[...], w_down[n, :])
        gu = gh * der_s[:, n].astype(F32)
        gu = gu.astype(BF16)
        der_s[:, n] = gu
        gb_up[:, n] += column_sum(gu.astype(F32))
        gw_down[n, :] += tdot(hid_s[:, n], branch_s[...])
        gw_up[:, n] += tdot(low_s[...], gu)
        return 0

    lax.fori_loop(0, count, down, 0)
    g_normed = sec_s[...] + dot_t(der_s[...], w_up[...])
    unit_one = norm_s[...]
    gg_one[...] += column_sum(g_normed * unit_one)
    gs_one[...] += column_sum(g_normed)
    e = g_normed * g_one[...]
    gf = inv_one * (e - mean_of(e) - unit_one * mean_of(e * unit_one))
    g_first[...] = gf
    go = gf.astype(BF16)
    gb_out[...] += column_sum(go.astype(F32))
    gw_out[...] += tdot(joined[...], go)
    g_joined[...] = dot_t(go, w_out[...]).astype(BF16)


def back_kernel(
    groups, local, lens, q, k, v, gj, joined, rest, inverse, states, rows_in, out,
    cos_s, sin_s, within, own, own_rows, part, part_rows, came, came_rows, gnum_s, gden_s, lane_s, *link,
):
    width = q.shape[1]
    pairs = width // LANES
    count = local // CHUNK
    chain = Chain(-1, pairs, link)
    meet([chain.before, chain.after])
    fill_tables(groups, local, chain.at * local, lens, cos_s, sin_s, None, within)

    def sums(i, _):
        s, p = i // pairs, i % pairs
        n = lanes_of(p)
        _, _, one, two = head_masks()
        mask = block_mask(256, LANES)
        ones = block_mask(2 * LANES, LANES).astype(BF16)
        total = jnp.zeros((256, LANES), F32)
        row = jnp.zeros((1, 256), F32)
        for c in reversed(range(count)):
            r = rows_of(s, c, local)
            ri = inverse[r, n].astype(F32)
            gnum = (gj[r, n].astype(F32) * jnp.abs(ri)).astype(BF16)
            product = gnum.astype(F32) * (joined[r, n].astype(F32) + rest[r, n].astype(F32))
            gden = jnp.where(ri > 0, -dot(two_parts(product), ones), 0.0)
            high = gden.astype(BF16).astype(F32)
            gnum_s[r, n] = gnum
            gden_s[r, n] = gden
            lane_s[r, n] = (high * one + (gden - high) * two).astype(BF16)
            q2 = spread(q[r, n].astype(F32), cos_s[r], sin_s[r])
            total = total + tdot(q2, gnum)
            row = row + column_sum(q2.astype(F32) * twice(gden))
            if c > 0:
                part[i * (count - 1) + c - 1] = pack(total * mask)
                part_rows[i * (count - 1) + c - 1] = jnp.broadcast_to(row, (8, 256))
        own[i] = pack(total * mask)
        own_rows[i] = jnp.broadcast_to(row, (8, 256))
        came[i] = jnp.zeros((128, LANES), F32)
        came_rows[i] = jnp.zeros((8, 256), F32)
        return 0

    def arrive(s):
        chain.arrive(s)

        def one(p, _):
            i = s * pairs + p
            came[i] = chain.in_state[i].astype(F32)
            came_rows[i] = chain.in_rows[i]
            return 0

        lax.fori_loop(0, pairs, one, 0)

    def leave(s):
        def one(p, _):
            i = s * pairs + p
            n = lanes_of(p)
            total = came[i] + own[i]
            low = total.astype(BF16)
            chain.out_state[i] = low
            lost = unpack(total - low.astype(F32), block_mask(256, LANES)).astype(BF16)
            mean = column_sum(v[pl.ds(s * local, local), n].astype(F32)) * (1.0 / local)
            row = dot_t(jnp.broadcast_to(mean, (8, LANES)).astype(BF16), lost)
            chain.out_rows[i] = came_rows[i] + own_rows[i] + row
            return 0

        lax.fori_loop(0, pairs, one, 0)
        chain.start(s)

    def main(i, _):
        s, p = i // pairs, i % pairs
        n = lanes_of(p)
        first, second, one, two = head_masks()
        mask = block_mask(256, LANES)
        ones = jnp.ones((CHUNK, LANES), BF16)
        m = within[s]
        m = jnp.concatenate([m, m], axis=0)
        for c in range(count):
            r = rows_of(s, c, local)
            cosine, sine = cos_s[r], sin_s[r]
            feature, key, value = q[r, n].astype(F32), k[r, n], v[r, n]
            gnum, gden, lane = gnum_s[r, n], gden_s[r, n], lane_s[r, n].astype(F32)
            row = rows_in[i * count + c][0:1]
            outer = dot_t(twice(gnum), states[i * count + c]) + twice(gden) * row
            gq = outer[:, :LANES] * cosine + outer[:, LANES:] * sine
            heads = stacked_heads(feature, first, second)
            scores = (dot_t(heads, key) * m).astype(BF16)
            gheads = stacked_heads(gnum.astype(F32), first, second)
            left = jnp.concatenate([gheads, stacked_heads(lane, first, second)], axis=1)
            g = (dot_t(left, jnp.concatenate([value, ones], axis=1)) * m).astype(BF16)
            inner = dot(g, key)
            gq = gq + jnp.where(first > 0, inner[:CHUNK], inner[CHUNK:])
            state, row = came[i], came_rows[i][0:1]
            if c + 1 < count:
                state = state + part[i * (count - 1) + c]
                row = row + part_rows[i * (count - 1) + c][0:1]
            state = two_parts(unpack(state, mask))
            k2 = spread(key.astype(F32), cosine, sine)
            gv = dot(k2, state[:, :LANES]) + tdot(gheads, scores).T
            outer = dot_t(twice(value), state) + row
            gk = outer[:, :LANES] * cosine + outer[:, LANES:] * sine + tdot(heads, g).T
            out[r, n] = (gq * slope(feature)).astype(BF16)
            out[r, pl.ds(pl.multiple_of(width + p * LANES, LANES), LANES)] = (
                gk * slope(key.astype(F32))
            ).astype(BF16)
            out[r, pl.ds(pl.multiple_of(2 * width + p * LANES, LANES), LANES)] = gv.astype(BF16)
        return 0

    lax.fori_loop(0, groups * pairs, sums, 0)

    @pl.when(chain.is_first)
    def _():
        for s in range(groups):
            leave(s)

    @pl.when(jnp.logical_not(chain.is_first))
    def _():
        for s in range(groups):
            arrive(s)

            @pl.when(jnp.logical_not(chain.is_last))
            def _():
                leave(s)

    lax.fori_loop(0, groups * pairs, main, 0)

    @pl.when(jnp.logical_not(chain.is_last))
    def _():
        for s in range(groups):
            chain.sent(s)


def input_kernel(tok, gm, weight, g_first, grad, gw, gb):
    @pl.when(pl.program_id(0) == 0)
    def _():
        gw[...] = jnp.zeros_like(gw)
        gb[...] = jnp.zeros_like(gb)

    low = gm[...]
    gb[...] += column_sum(low.astype(F32))
    gw[...] += tdot(tok[...], low)
    grad[...] = g_first[...] + dot_t(low, weight[...])


def peers():
    dp, z = lax.axis_index("dp"), lax.axis_index("head")
    core, x, y = lax.rem(dp, 2), lax.rem(dp // 2, 2), dp // 4
    twin = dp + 1 - 2 * core
    along_x, along_y = dp + 2 - 4 * x, dp + 4 - 8 * y
    one = along_x + core * (along_y - along_x)
    two = along_y + core * (along_x - along_y)
    return dp, z, twin, one, two, one + two - dp


class Copies:
    def __init__(self, send, recv):
        self.send, self.recv, self.all = send, recv, []

    def start(self, a, slot, src, dst, target):
        copy = pltpu.make_async_remote_copy(
            src_ref=src, dst_ref=dst, send_sem=self.send.at[a, slot], recv_sem=self.recv.at[a, slot],
            device_id=target, device_id_type=MESH,
        )
        copy.start()
        self.all.append(copy)
        return copy

    def finish(self):
        for copy in self.all:
            copy.wait_send()


class Gather:
    def __init__(self, arrays, send, recv):
        self.arrays = arrays
        self.copies, self.had = Copies(send, recv), {}
        self.dp, self.z, twin, one, two, self.far = peers()
        self.me = self.dp * 4 + self.z
        self.one, self.two = one, two
        self.to_z = [{"dp": self.dp, "head": lax.rem(self.z + k, 4)} for k in (1, 2, 3)]
        self.to_twin, self.to_one, self.to_two = (
            {"dp": d, "head": self.z} for d in (twin, one, two)
        )

    def targets(self):
        return self.to_z + [self.to_twin, self.to_one, self.to_two]

    def begin(self, a):
        ref, low, rows, fine = self.arrays[a]
        place = ref.at[self.me, pl.ds(low, rows)]
        for k in range(3):
            self.had[a, k] = self.copies.start(a, k, place, place, self.to_z[k])
        if fine:
            self.pass_one(a, 0, self.dp, ((3, self.to_one), (7, self.to_two), (15, self.to_twin)))

    def pass_one(self, a, k, block, ways):
        ref, low, rows, _ = self.arrays[a]
        place = ref.at[block * 4 + lax.rem(self.z + 4 - k, 4), pl.ds(low, rows)]
        for slot, target in ways:
            self.had[a, slot + k] = self.copies.start(a, slot + k, place, place, target)

    def fine_stage(self, a, g):
        if g == 5:
            for slot in range(15, 31):
                self.had[a, slot].wait_recv()
            return
        if g < 3:
            self.had[a, g].wait_recv()
            self.pass_one(a, g + 1, self.dp, ((3, self.to_one), (7, self.to_two), (15, self.to_twin)))
        if g < 4:
            self.had[a, 3 + g].wait_recv()
            self.pass_one(a, g, self.one, ((11, self.to_two), (19, self.to_twin)))
            self.had[a, 7 + g].wait_recv()
            self.pass_one(a, g, self.two, ((23, self.to_twin),))
        if g > 0:
            self.had[a, 10 + g].wait_recv()
            self.pass_one(a, g - 1, self.far, ((27, self.to_twin),))

    def pass_on(self, a, slot, block, target):
        ref, low, rows, _ = self.arrays[a]
        place = ref.at[pl.ds(block * 4, 4), pl.ds(low, rows)]
        self.had[a, slot] = self.copies.start(a, slot, place, place, target)

    def stage(self, a, step):
        if self.arrays[a][3]:
            self.fine_stage(a, step)
        elif step == 0:
            for k in range(3):
                self.had[a, k].wait_recv()
            self.pass_on(a, 3, self.dp, self.to_one)
            self.pass_on(a, 4, self.dp, self.to_two)
            self.pass_on(a, 5, self.dp, self.to_twin)
        elif step == 1:
            self.had[a, 3].wait_recv()
            self.pass_on(a, 6, self.one, self.to_two)
            self.pass_on(a, 7, self.one, self.to_twin)
        elif step == 2:
            self.had[a, 4].wait_recv()
            self.pass_on(a, 8, self.two, self.to_twin)
        elif step == 3:
            self.had[a, 6].wait_recv()
            self.pass_on(a, 9, self.far, self.to_twin)
        elif step == 4:
            for slot in (5, 7, 8, 9):
                self.had[a, slot].wait_recv()

    def finish(self):
        self.copies.finish()


class Scatter:
    def __init__(self, arrays, send, recv, place=lambda dp: dp * 4):
        self.arrays, self.place = arrays, place
        self.copies, self.had = Copies(send, recv), {}
        self.dp, self.z, self.twin, self.one, self.two, self.far = peers()
        self.to_z = [{"dp": self.dp, "head": lax.rem(self.z + k, 4)} for k in (1, 2, 3)]
        self.to_twin, self.to_one, self.to_two = (
            {"dp": d, "head": self.z} for d in (self.twin, self.one, self.two)
        )

    def targets(self):
        return self.to_z + [self.to_twin, self.to_one, self.to_two]

    def send(self, a, slot, src, count, box, target):
        buf, boxes, _, low, rows = self.arrays[a]
        some = pl.ds(low, rows)
        self.had[a, slot] = self.copies.start(
            a, slot, buf.at[pl.ds(src, count), some], boxes.at[pl.ds(box, count), some], target
        )

    def begin(self, a):
        shift = self.twin - self.dp
        for slot, dp in enumerate((self.far, self.one, self.two, self.dp)):
            self.send(a, slot, self.place(dp + shift), 4, slot * 4, self.to_twin)

    def wait(self, a, *slots):
        for slot in slots:
            self.had[a, slot].wait_recv()

    def add(self, a, dp, slots):
        buf, box, _, low, rows = self.arrays[a]
        start, some = self.place(dp), pl.ds(low, rows)

        def one(j, _):
            total = buf[start + j, some].astype(F32)
            for slot in slots:
                total = total + box[slot * 4 + j, some].astype(F32)
            buf[start + j, some] = total.astype(BF16)
            return 0

        lax.fori_loop(0, 4, one, 0)

    def stage(self, a, step):
        if step == 0:
            self.wait(a, 0)
            self.add(a, self.far, (0,))
            self.send(a, 4, self.place(self.far), 4, 16, self.to_two)
            self.wait(a, 1)
            self.add(a, self.two, (1,))
            self.send(a, 5, self.place(self.two), 4, 20, self.to_two)
        elif step == 1:
            self.wait(a, 2, 4)
            self.add(a, self.one, (2, 4))
            self.send(a, 6, self.place(self.one), 4, 24, self.to_one)
        elif step == 2:
            self.wait(a, 3, 5, 6)
            self.add(a, self.dp, (3, 5, 6))
            for k in range(3):
                self.send(a, 7 + k, self.place(self.dp) + lax.rem(self.z + k + 1, 4), 1, 28 + k, self.to_z[k])
        elif step == 3:
            self.wait(a, 7, 8, 9)
            buf, box, out, low, rows = self.arrays[a]
            some = pl.ds(low, rows)
            total = buf[self.place(self.dp) + self.z, some].astype(F32)
            for k in range(3):
                total = total + box[28 + k, some].astype(F32)
            have, cols = out.shape[0], total.shape[1]
            if have >= low + rows:
                out[low : low + rows] = total
            else:
                for j in range(rows // have):
                    m = (low // have + j) * cols
                    out[:, m : m + cols] = total[j * have : (j + 1) * have]

    def finish(self):
        self.copies.finish()


class Total:
    def __init__(self, scatter, value, box, send, recv):
        self.value, self.box, self.to = value, box, scatter
        self.copies, self.had = Copies(send, recv), {}

    def pass_on(self, slot, target):
        self.had[slot] = self.copies.start(0, slot, self.value.at[slot if slot < 3 else 3], self.box.at[slot], target)

    def stage(self, step):
        value, box = self.value, self.box
        targets = (self.to.to_twin, self.to.to_two, self.to.to_one)
        if step > 0 and step < 4:
            self.had[step - 1].wait_recv()
            value[step] = value[step - 1] + box[step - 1]
        if step < 3:
            self.pass_on(step, targets[step])
        elif step == 3:
            for k in range(3):
                self.pass_on(3 + k, self.to.to_z[k])
        elif step == 4:
            for k in range(3):
                self.had[3 + k].wait_recv()
            value[4] = (value[3] + box[3]) + (box[4] + box[5])

    def finish(self):
        self.copies.finish()


def fold_block(block, parts=2):
    cols = block.shape[1] // parts
    return jnp.concatenate([block[:, j * cols : (j + 1) * cols] for j in range(parts)], axis=0).astype(BF16)


class Column:
    def __init__(self, own, blocks, local, send, recv, gather):
        self.own, self.blocks, self.gather = own, blocks, gather
        self.copies, self.had = Copies(send, recv), {}
        self.keep = pltpu.make_async_copy(own, blocks.at[gather.z], local.at[0])

    def begin(self):
        self.keep.start()
        for k in range(3):
            self.had[k] = self.copies.start(0, k, self.own, self.blocks.at[self.gather.z], self.gather.to_z[k])

    def finish(self):
        self.keep.wait()
        for k in range(3):
            self.had[k].wait_recv()
        self.copies.finish()


class Spread:
    def __init__(self, column, blocks, local, send, recv, place):
        self.column, self.blocks, self.place = column, blocks, place
        self.copies, self.had = Copies(send, recv), {}
        self.here = pltpu.make_async_copy(column, blocks.at[pl.ds(place.dp * 4, 4)], local)

    def pass_on(self, j, dp, ways, src=None):
        at = self.blocks.at[dp * 4 + j]
        for slot, target in ways:
            self.had[slot + j] = self.copies.start(0, slot + j, at if src is None else src, at, target)

    def begin(self):
        place = self.place
        self.here.start()
        for j in range(4):
            ways = ((0, place.to_one), (4, place.to_two), (8, place.to_twin))
            self.pass_on(j, place.dp, ways, self.column.at[j])

    def stage(self, step):
        place = self.place
        for j in range(4):
            if step == 0:
                self.had[j].wait_recv()
                self.pass_on(j, place.one, ((12, place.to_two), (16, place.to_twin)))
                self.had[4 + j].wait_recv()
                self.pass_on(j, place.two, ((20, place.to_twin),))
            elif step == 1:
                self.had[12 + j].wait_recv()
                self.pass_on(j, place.far, ((24, place.to_twin),))
            else:
                for slot in (8, 16, 20, 24):
                    self.had[slot + j].wait_recv()
        if step == 2:
            self.here.wait()

    def finish(self):
        self.copies.finish()


def unfold_into(out, blocks, rows):
    n, have, cols = blocks.shape

    def body(j, _):
        pair = [blocks[2 * j + i].astype(F32) for i in (0, 1)]
        r = pl.ds(pl.multiple_of(2 * rows * j, 2 * rows), 2 * rows)
        for m in range(have // rows):
            both = jnp.concatenate([item[m * rows : (m + 1) * rows] for item in pair], axis=0)
            out[r, m * cols : (m + 1) * cols] = both.astype(BF16)
        return 0

    lax.fori_loop(0, n // 2, body, 0)


def unpack_vectors(slabs, out, sizes, some):
    n, _, lanes = slabs.shape
    step = 768
    for size in sorted({sizes[j] for j in some}):
        for at in range(0, n * size, step):
            lane = iota((1, step), 1) + at
            owner = lane // size
            places = (iota((lanes, step), 0) == lane - owner * size).astype(BF16)
            mine = (iota((n, step), 0) == owner).astype(F32)
            for j in some:
                if sizes[j] == size:
                    out[j : j + 1, at : at + step] = column_sum(dot(slabs[:, j, :].astype(BF16), places) * mine)


def front_kernel(
    groups, local, sizes, lens, tok, s_in, s_out, s_up, s_down, *refs,
):
    vecs, refs = refs[: len(sizes)], refs[len(sizes) :]
    front_steps(groups, local, sizes, vecs, lens, tok, s_in, s_out, s_up, s_down, *refs)


def front_steps(
    groups, local, sizes, vecs, lens, tok, s_in, s_out, s_up, s_down,
    q_h, k_h, v_h, joined_h, rest_h, inverse_h, states_h, rows_out, wq_h, wk_h, wv_h, wout_h, wup_h, wdown_h, vectors,
    cos_s, sin_s, ok_s, within, own, own_rows, part, part_rows, came, came_rows, num_s, den_s,
    q, k, v, joined, rest, inverse, states, w_q, w_k, w_v, w_out, w_up, save_sem,
    own_down, d_local, d_send, d_recv, g_vec, g_q, g_k, g_v, g_out, g_up, g_send, g_recv, *link,
):
    width = tok.shape[1]
    pairs = width // LANES
    chain = Chain(1, pairs, link)
    saved = []

    def save(*pairs_of_refs):
        for src, dst in pairs_of_refs:
            saved.append(pltpu.make_async_copy(src, dst, save_sem.at[len(saved)]))
            saved[-1].start()

    half = g_up.shape[1] // 2
    arrays = [(ref, 0, ref.shape[1], True) for ref in (g_vec, g_k, g_v, g_q)]
    arrays += [(g_out, 0, g_out.shape[1], False), (g_up, 0, half, False), (g_up, half, half, False)]
    gather = Gather(arrays, g_send, g_recv)
    me = gather.me
    g_vec[me] = jnp.zeros(g_vec.shape[1:], F32)
    for j, vec in enumerate(vecs):
        g_vec[me, j : j + 1, 0 : sizes[j]] = vec[...].astype(BF16).astype(F32)
    for j, ref in ((1, g_k), (2, g_v), (0, g_q)):
        ref[me] = fold_block(s_in[:, j * width : (j + 1) * width])
    meet(gather.targets())
    for a in range(4):
        gather.begin(a)
    g_out[me] = fold_block(s_out[...])
    g_up[me] = fold_block(s_up[...], 4)
    own_down[...] = s_down[...].astype(BF16)
    column = Column(own_down, wdown_h, d_local, d_send, d_recv, gather)
    starts = (0, 0, 1, 2, 5, 6, 7)

    def wave(t):
        for a in range(7):
            if 0 <= t - starts[a] < (6 if a < 4 else 5):
                gather.stage(a, t - starts[a])

    work = Forward(
        groups, local, lens, chain, (q, k, v, joined, rest, inverse, states, rows_out),
        (cos_s, sin_s, ok_s, within, num_s, den_s), (own, own_rows, part, part_rows, came, came_rows),
    )
    sums, arrive, leave, intra, inter = work.steps()
    work.prepare()
    wave(0)
    wave(1)
    for a in range(4, 7):
        gather.begin(a)
    for t in range(2, 6):
        wave(t)
    unpack_vectors(g_vec, vectors, sizes, (0,))
    bias = vectors.at[0:1]
    unfold_into(w_k, g_k, s_in.shape[0])
    work.project(1, tok, w_k, bias)
    wave(6)
    unfold_into(w_v, g_v, s_in.shape[0])
    work.project(2, tok, w_v, bias)

    def relay(at, *some):
        @pl.when(chain.at == at)
        def _():
            for s in some:
                arrive(s)
                if at < 3:
                    leave(s)

    for s in range(groups):
        work.over(sums, s)
        pl.when(chain.is_first)(functools.partial(leave, s))
    wave(7)
    unfold_into(w_q, g_q, s_in.shape[0])
    work.project(0, tok, w_q, bias)
    save((q, q_h), (k, k_h), (v, v_h), (w_q, wq_h), (w_k, wk_h), (w_v, wv_h))
    relay(1, 0)
    wave(8)
    work.over(intra, 0)
    relay(1, 1)
    wave(9)
    work.over(intra, 1)
    relay(1, 2)
    relay(2, 0)
    unpack_vectors(g_vec, vectors, sizes, range(1, 8))
    wave(10)
    unfold_into(w_out, g_out, s_out.shape[0])
    work.over(intra, 2)
    relay(2, 1)
    wave(11)
    relay(2, 2)
    column.begin()
    unfold_into(w_up, g_up, s_up.shape[0])
    save((w_out, wout_h), (w_up, wup_h))
    for s in range(groups):
        relay(3, s)
        work.over(inter, s)
        r = pl.ds(s * local, local)
        u = pl.ds(s * pairs * work.count, pairs * work.count)
        save((joined.at[r], joined_h.at[r]), (rest.at[r], rest_h.at[r]), (inverse.at[r], inverse_h.at[r]))
        save((states.at[u], states_h.at[u]))

    @pl.when(jnp.logical_not(chain.is_last))
    def _():
        for s in range(groups):
            chain.sent(s)

    gather.finish()
    column.finish()
    for copy in saved:
        copy.wait()


TALL = 384


def by_eight(x):
    return jnp.sum(x.reshape(x.shape[0] // 8, 8, x.shape[1]), axis=0)


def middle_kernel(
    tok_h, joined_h, cot_h, w_out, up_h, down_h, vectors,
    act_h, first_h, gj_h, gup_h, gout_h, gw_down, small,
    low, joined, cot, branch, norm, sec, inv, hid, der, w_up, w_dn, box, xa, xb, fold_s, acc, acc_up,
    io, g_send, g_recv, r_send, r_recv,
):
    rows, width = joined.shape
    ff = w_up.shape[1]
    chunks = ff // width
    tiles = rows // TALL
    slabs = TALL // 96
    depth = rows // 96
    _, b_out, g_one, s_one, b_up, b_down, g_two, s_two = (
        (lambda j: lambda at=0, n=width: vectors[j : j + 1, at : at + n])(j) for j in range(8)
    )
    scatter = Scatter(
        [(hid, box, gw_down, 0, 48), (hid, box, gw_down, 48, 48)],
        r_send, r_recv, lambda dp: depth * (dp // 2) + 4 * lax.rem(dp, 2),
    )
    loads = [
        pltpu.make_async_copy(src, dst, io.at[j])
        for j, (src, dst) in enumerate(((joined_h, joined), (tok_h, low), (up_h, w_up), (cot_h, cot)))
    ]
    for load in loads:
        load.start()
    meet(scatter.targets())
    spread_down = Spread(down_h, w_dn, io.at[5], g_send, g_recv, scatter)
    spread_down.begin()
    acc[...] = jnp.zeros_like(acc)
    acc_up[...] = jnp.zeros_like(acc_up)

    def tile(t):
        return pl.ds(t * TALL, TALL) if isinstance(t, int) else pl.ds(pl.multiple_of(t * TALL, TALL), TALL)

    def of_chunk(ref, j, t=None):
        if t is None:
            return ref[pl.ds(depth * j, depth)].reshape(rows, width)
        return ref[pl.ds(depth * j + slabs * t, slabs)].reshape(TALL, width)

    def down_chunk(j):
        return w_dn[pl.ds(8 * j, 8)].reshape(width, width)

    loads[0].wait()
    loads[1].wait()
    def rows32(t, i):
        return pl.ds(pl.multiple_of(t * TALL + i, 32), 32)

    def by_tiles(body, low=0, high=tiles):
        def both(u, _):
            for i in range(2):
                body(2 * u + i, (xa, xb)[i])
            return 0

        lax.fori_loop(low // 2, high // 2, both, 0)

    def enter(t, x):
        x[...] = dot(joined[tile(t)], w_out[...])
        for i in range(0, TALL, 32):
            r = rows32(t, i)
            unit, scale = normalised(low[r].astype(F32) + (x[i : i + 32] + b_out()))
            norm[r] = unit
            inv[r] = jnp.broadcast_to(scale, (32, LANES))
            low[r] = (unit * g_one() + s_one()).astype(BF16)

    by_tiles(enter)
    loads[2].wait()

    def up(t, _):
        for j in range(chunks):
            x = (xa, xb)[j % 2]
            x[...] = dot(low[tile(t)], w_up[:, j * width : (j + 1) * width])
            for i in range(slabs):
                for m in range(0, 96, 32):
                    for n in range(0, width, 256):
                        y, d = gelu_both(x[96 * i + m : 96 * i + m + 32, n : n + 256] + b_up(j * width + n, 256))
                        hid[depth * j + slabs * t + i, m : m + 32, n : n + 256] = y.astype(BF16)
                        der[depth * j + slabs * t + i, m : m + 32, n : n + 256] = d.astype(BF16)
        return 0

    lax.fori_loop(0, tiles // 2, up, 0)
    spread_down.stage(0)
    lax.fori_loop(tiles // 2, tiles - 1, up, 0)
    spread_down.stage(1)
    lax.fori_loop(tiles - 1, tiles, up, 0)
    spread_down.stage(2)
    loads[3].wait()

    def second(t, x):
        x[...] = dot(of_chunk(hid, 0, t), down_chunk(0))
        for j in range(1, chunks):
            x[...] += dot(of_chunk(hid, j, t), down_chunk(j))
        for i in range(0, TALL, 32):
            r = rows32(t, i)
            unit, scale = normalised(norm[r] * g_one() + (s_one() + b_down()) + x[i : i + 32])
            c = cot[r].astype(F32)
            cot[r] = (unit * g_two() + s_two()).astype(BF16)
            acc[4] += by_eight(c * unit)
            acc[5] += by_eight(c)
            e = c * g_two()
            g = scale * (e - mean_of(e) - unit * mean_of(e * unit))
            sec[r] = g
            g = g.astype(BF16)
            branch[r] = g
            acc[3] += by_eight(g.astype(F32))

    by_tiles(second)
    act = pltpu.make_async_copy(cot, act_h, io.at[3])
    act.start()
    for j in range(chunks):
        for m in range(2):
            x = (xa, xb)[m]
            x[...] = tdot(
                hid[pl.ds(depth * j, depth), :, m * TALL : (m + 1) * TALL].reshape(rows, TALL), branch[...]
            )
        for m in range(2):
            hid[pl.ds(depth * j + 4 * m, 4)] = (xa, xb)[m][...].astype(BF16).reshape(4, 96, width)
    scatter.begin(0)
    scatter.begin(1)

    def back(t, _):
        for j in range(chunks):
            x = (xa, xb)[j % 2]
            x[...] = dot_t(branch[tile(t)], down_chunk(j))
            for i in range(slabs):
                for m in range(0, 96, 32):
                    at = depth * j + slabs * t + i
                    g = x[96 * i + m : 96 * i + m + 32] * der[at, m : m + 32].astype(F32)
                    g = g.astype(BF16)
                    der[at, m : m + 32] = g
                    acc_up[:, j * width : (j + 1) * width] += by_eight(g.astype(F32))
        return 0

    lax.fori_loop(0, tiles // 2, back, 0)
    scatter.stage(0, 0)
    lax.fori_loop(tiles // 2, tiles, back, 0)
    scatter.stage(1, 0)
    out = []

    def first(t, x):
        x[...] = dot_t(of_chunk(der, 0, t), w_up[:, 0:width])
        for j in range(1, chunks):
            x[...] += dot_t(of_chunk(der, j, t), w_up[:, j * width : (j + 1) * width])
        for i in range(0, TALL, 32):
            r = rows32(t, i)
            g = sec[r] + x[i : i + 32]
            unit = norm[r]
            acc[1] += by_eight(g * unit)
            acc[2] += by_eight(g)
            e = g * g_one()
            g = inv[r, 0:1] * (e - mean_of(e) - unit * mean_of(e * unit))
            sec[r] = g
            g = g.astype(BF16)
            branch[r] = g
            acc[0] += by_eight(g.astype(F32))

    by_tiles(first)
    out.append(pltpu.make_async_copy(sec, first_h, io.at[0]))
    out[-1].start()
    scatter.stage(0, 1)
    spread_down.finish()
    for m in range(2):
        for jj in range(chunks // 2):
            for i in range(2):
                (xa, xb)[i][...] = tdot(low[:, m * TALL : (m + 1) * TALL], of_chunk(der, 2 * jj + i))
            for i in range(16):
                both = [x[24 * i : 24 * i + 24] for x in (xa, xb)]
                w_dn[16 * m + i, 48 * jj : 48 * jj + 48] = jnp.concatenate(both, axis=0).astype(BF16)
        scatter.stage(1 - m, 1 + m)
    out.append(pltpu.make_async_copy(w_dn, gup_h, io.at[1]))
    out[-1].start()
    for m in range(2):
        x = (xa, xb)[m]
        x[...] = tdot(joined[:, m * TALL : (m + 1) * TALL], branch[...])
        for i in range(16):
            fold_s[16 * m + i] = fold_block(x[24 * i : 24 * i + 24])
    out.append(pltpu.make_async_copy(fold_s, gout_h, io.at[2]))
    out[-1].start()
    scatter.stage(1, 2)
    for t in range(tiles):
        joined[tile(t)] = dot_t(branch[tile(t)], w_out[...]).astype(BF16)
    out.append(pltpu.make_async_copy(joined, gj_h, io.at[4]))
    out[-1].start()
    small[...] = jnp.zeros_like(small)
    for row, at in ((3, 0), (4, 1), (5, 2), (10, 3), (11, 4), (12, 5)):
        small[row : row + 1] = column_sum(acc[at])
    for j in range(chunks):
        small[6 + j : 7 + j] = column_sum(acc_up[:, j * width : (j + 1) * width])
    scatter.stage(0, 3)
    scatter.stage(1, 3)
    act.wait()
    for copy in out:
        copy.wait()
    scatter.finish()


def own_slices(value, me):
    width = value.shape[1]
    parts, left = [], value
    for _ in range(3):
        parts.append(left.astype(BF16))
        left = left - parts[-1].astype(F32)

    def pick(size):
        lane = iota((width, LANES), 1)
        at = iota((width, LANES), 0) - size * lax.rem(me, width // size)
        ones = ((at == lane) & (lane < size)).astype(BF16)
        return sum(dot(part, ones) for part in parts)

    def row(picked, at):
        return column_sum(jnp.where(iota(picked.shape, 0) == at, picked, 0.0))

    few, some, many = pick(width // 32), pick(width // 16), pick(width // 8)
    rows = [row(some, me // 16)] + [few[j : j + 1] for j in range(2, 6)] + [row(many, 6 + me // 8)]
    rows += [few[j : j + 1] for j in range(10, 13)]
    return jnp.concatenate(rows + [jnp.zeros((16 - len(rows), LANES), F32)], axis=0)


def finish_kernel(act, grad, down, up, out, q, k, v, act_o, grad_o, down_o, up_o, out_o, in_o, *scratch):
    boxes, (sems,) = scratch[:8], scratch[8:]
    width = q.shape[1]
    plan = []
    for src, dst, box, cuts in ((grad, grad_o, boxes[0], 6), (act, act_o, boxes[1], 3)):
        step = src.shape[0] // cuts
        plan += [tuple(ref.at[pl.ds(j * step, step)] for ref in (src, box, dst)) for j in range(cuts)]
    plan += [(down, boxes[2], down_o), (up, boxes[3], up_o), (out, boxes[4], out_o)]
    for j, ref in enumerate((q, k, v)):
        plan.append((ref, boxes[5 + j], in_o.at[:, j * width : (j + 1) * width]))
    come = [pltpu.make_async_copy(src, box, sems.at[0, j]) for j, (src, box, _) in enumerate(plan)]
    go = [pltpu.make_async_copy(box, dst, sems.at[1, j]) for j, (_, box, dst) in enumerate(plan)]
    for copy in come:
        copy.start()
    for first, second in zip(come, go):
        first.wait()
        second.start()
    for copy in go:
        copy.wait()


def tail_kernel(
    groups, local, lens, q_h, k_h, v_h, gj_h, joined_h, rest_h, inverse_h, states, rows_in,
    tok_h, wq_h, wk_h, wv_h, first_h, up_h, out_h, small,
    grad_h, gw_up, gw_out, gw_q, gw_k, gw_v, small_out,
    q, k, v, gnum, joined, lane_s, inverse, cos_s, sin_s, within,
    own, own_rows, part, part_rows, came, came_rows, slots, load_sem, slot_sem,
    b_up, b_out, b_q, b_k, b_v, x_up, x_out, x_q, x_k, x_v,
    value, box, r_send, r_recv, t_send, t_recv, *link,
):
    width = q.shape[1]
    rows = q.shape[0]
    pairs = width // LANES
    count = local // CHUNK
    chain = Chain(-1, pairs, link)
    half = b_up.shape[1] // 2
    arrays = [(b_up, x_up, gw_up, 0, half), (b_up, x_up, gw_up, half, half)]
    arrays += [
        (buf, box, out, 0, buf.shape[1])
        for buf, box, out in ((b_out, x_out, gw_out), (b_q, x_q, gw_q), (b_k, x_k, gw_k), (b_v, x_v, gw_v))
    ]
    scatter = Scatter(arrays, r_send, r_recv)
    total = Total(scatter, value, box, t_send, t_recv)
    places = (
        (inverse_h, inverse), (gj_h, gnum), (joined_h, joined), (rest_h, lane_s), (q_h, q),
        (up_h, b_up), (out_h, b_out), (k_h, k), (v_h, v),
    )
    loads = [pltpu.make_async_copy(src, dst, load_sem.at[j]) for j, (src, dst) in enumerate(places)]
    for load in loads:
        load.start()
    meet(scatter.targets())
    fill_tables(groups, local, chain.at * local, lens, cos_s, sin_s, None, within)

    def sums(i, _):
        s, p = i // pairs, i % pairs
        n = lanes_of(p)
        _, _, one, two = head_masks()
        mask = block_mask(256, LANES)
        ones = block_mask(2 * LANES, LANES).astype(BF16)
        state = jnp.zeros((256, LANES), F32)
        row = jnp.zeros((1, 256), F32)
        for c in reversed(range(count)):
            r = rows_of(s, c, local)
            ri = inverse[r, n].astype(F32)
            gn = (gnum[r, n].astype(F32) * jnp.abs(ri)).astype(BF16)
            product = gn.astype(F32) * (joined[r, n].astype(F32) + lane_s[r, n].astype(F32))
            gden = jnp.where(ri > 0, -dot(two_parts(product), ones), 0.0)
            high = gden.astype(BF16).astype(F32)
            gnum[r, n] = gn
            lane_s[r, n] = (high * one + (gden - high) * two).astype(BF16)
            q2 = spread(q[r, n].astype(F32), cos_s[r], sin_s[r])
            state = state + tdot(q2, gn)
            row = row + column_sum(q2.astype(F32) * twice(gden))
            if c > 0:
                part[i * (count - 1) + c - 1] = pack(state * mask)
                part_rows[i * (count - 1) + c - 1] = jnp.broadcast_to(row, (8, 256))
        own[i] = pack(state * mask)
        own_rows[i] = jnp.broadcast_to(row, (8, 256))
        came[i] = jnp.zeros((128, LANES), F32)
        came_rows[i] = jnp.zeros((8, 256), F32)
        return 0

    def arrive(s):
        chain.arrive(s)

        def one(p, _):
            i = s * pairs + p
            came[i] = chain.in_state[i].astype(F32)
            came_rows[i] = chain.in_rows[i]
            return 0

        lax.fori_loop(0, pairs, one, 0)

    def leave(s):
        def one(p, _):
            i = s * pairs + p
            n = lanes_of(p)
            state = came[i] + own[i]
            low = state.astype(BF16)
            chain.out_state[i] = low
            lost = unpack(state - low.astype(F32), block_mask(256, LANES)).astype(BF16)
            mean = column_sum(v[pl.ds(s * local, local), n].astype(F32)) * (1.0 / local)
            row = dot_t(jnp.broadcast_to(mean, (8, LANES)).astype(BF16), lost)
            chain.out_rows[i] = came_rows[i] + own_rows[i] + row
            return 0

        lax.fori_loop(0, pairs, one, 0)
        chain.start(s)

    def intra(i, _):
        s, p = i // pairs, i % pairs
        n = lanes_of(p)
        first, second, one, two = head_masks()
        ones = jnp.ones((CHUNK, LANES), BF16)
        picks = (block_mask(LANES, LANES) * ((iota((LANES, LANES), 0) & (HALF - 1)) < 2).astype(F32)).astype(BF16)
        m = within[s]
        m = jnp.concatenate([m, m], axis=0)
        for c in range(count):
            r = rows_of(s, c, local)
            feature, key, value_low, gn, lane = q[r, n].astype(F32), k[r, n], v[r, n], gnum[r, n], lane_s[r, n]
            gden = dot(lane, picks)
            row = rows_in[i * count + c][0:1]
            outer = dot_t(twice(gn), states[i * count + c]) + twice(gden) * row
            gq = outer[:, :LANES] * cos_s[r] + outer[:, LANES:] * sin_s[r]
            heads = stacked_heads(feature, first, second)
            scores = (dot_t(heads, key) * m).astype(BF16)
            gheads = stacked_heads(gn.astype(F32), first, second)
            left = jnp.concatenate([gheads, stacked_heads(lane.astype(F32), first, second)], axis=1)
            g = (dot_t(left, jnp.concatenate([value_low, ones], axis=1)) * m).astype(BF16)
            inner = dot(g, key)
            gq = gq + jnp.where(first > 0, inner[:CHUNK], inner[CHUNK:])
            joined[r, n] = tdot(heads, g).T.astype(BF16)
            inverse[r, n] = tdot(gheads, scores).T.astype(BF16)
            q[r, n] = (gq * slope(feature)).astype(BF16)
        return 0

    def inter(i, _):
        s, p = i // pairs, i % pairs
        n = lanes_of(p)
        mask = block_mask(256, LANES)
        for c in range(count):
            r = rows_of(s, c, local)
            cosine, sine, key = cos_s[r], sin_s[r], k[r, n].astype(F32)
            state, row = came[i], came_rows[i][0:1]
            if c + 1 < count:
                state = state + part[i * (count - 1) + c]
                row = row + part_rows[i * (count - 1) + c][0:1]
            state = two_parts(unpack(state, mask))
            outer = dot_t(twice(v[r, n]), state) + row
            gk = outer[:, :LANES] * cosine + outer[:, LANES:] * sine + joined[r, n].astype(F32)
            v[r, n] = (dot(spread(key, cosine, sine), state[:, :LANES]) + inverse[r, n].astype(F32)).astype(BF16)
            k[r, n] = (gk * slope(key)).astype(BF16)
        return 0

    def over(step, s, low=0, high=pairs):
        lax.fori_loop(s * pairs + low, s * pairs + high, step, 0)

    def weight_terms(a, g):
        buf = scatter.arrays[a][0]
        size = width // 32
        for j in range(2):
            term = tdot(gnum[:, j * (width // 2) : (j + 1) * (width // 2)], g[...])
            for i in range(16):
                buf[16 * j + i] = fold_block(term[i * size : (i + 1) * size])

    for load in loads[:5]:
        load.wait()
    loads[5].wait()
    scatter.begin(0)
    scatter.begin(1)
    loads[6].wait()
    scatter.begin(2)
    for load in loads[7:]:
        load.wait()
    for s in reversed(range(groups)):
        over(sums, s)
        pl.when(chain.is_first)(functools.partial(leave, s))
    scatter.stage(0, 0)

    def relay(place, *some):
        @pl.when(chain.at == place)
        def _():
            for s in some:
                arrive(s)
                if place > 0:
                    leave(s)

    cut = pairs // 2
    over(intra, 0, 0, cut)
    scatter.stage(1, 0)
    over(intra, 0, cut, pairs)
    relay(2, 2)
    scatter.stage(2, 0)
    over(intra, 1, 0, cut)
    relay(2, 1)
    scatter.stage(0, 1)
    over(intra, 1, cut, pairs)
    relay(2, 0)
    relay(1, 2)
    scatter.stage(1, 1)
    over(intra, 2, 0, cut)
    relay(1, 1)
    scatter.stage(0, 2)
    scatter.stage(2, 1)
    over(intra, 2, cut, pairs)
    relay(1, 0)
    scatter.stage(1, 2)
    tok_load = pltpu.make_async_copy(tok_h, gnum, load_sem.at[0])
    w_loads = [
        pltpu.make_async_copy(wq_h, lane_s.at[pl.ds(0, width)], load_sem.at[1]),
        pltpu.make_async_copy(wk_h, lane_s.at[pl.ds(width, width)], load_sem.at[2]),
        pltpu.make_async_copy(wv_h, joined.at[pl.ds(0, width)], load_sem.at[3]),
    ]
    for load in [tok_load] + w_loads[:2]:
        load.start()
    tok_load.wait()
    weight_terms(3, q)
    scatter.begin(3)
    steps = (((2, 2), (0, 3)), ((1, 3), (3, 0)), ((2, 3),))
    for j, s in enumerate(reversed(range(groups))):
        relay(0, s)
        over(inter, s)
        for a, step in steps[j]:
            scatter.stage(a, step)
    w_loads[2].start()
    weight_terms(4, k)
    scatter.begin(4)
    scatter.stage(3, 1)
    weight_terms(5, v)
    scatter.begin(5)
    value[0] = small[...]
    for j, ref in enumerate((q, k, v)):
        value[0, j : j + 1, :] = column_sum(ref[...].astype(F32))
    total.stage(0)
    for load in w_loads:
        load.wait()

    def slot(i):
        return slots.at[i % 2]

    def rows_at(ref, i):
        return ref.at[pl.ds(i * local, local)]

    n_slots = groups
    fetch = [pltpu.make_async_copy(rows_at(first_h, i), slot(i), slot_sem.at[i % 2, 0]) for i in range(n_slots)]
    store = [pltpu.make_async_copy(slot(i), rows_at(grad_h, i), slot_sem.at[i % 2, 1]) for i in range(n_slots)]
    fetch[0].start()
    rest_plan = (((4, 0), (3, 2), (5, 0)), ((4, 1), (5, 1), (3, 3)), ((4, 2), (5, 2)))
    for i in range(n_slots):
        if i + 1 < n_slots:
            if i >= 1:
                store[i - 1].wait()
            fetch[i + 1].start()
        fetch[i].wait()
        r = pl.ds(i * local, local)
        slots[i % 2] += dot_t(q[r], lane_s[pl.ds(0, width)])
        slots[i % 2] += dot_t(k[r], lane_s[pl.ds(width, width)])
        slots[i % 2] += dot_t(v[r], joined[pl.ds(0, width)])
        store[i].start()
        for a, step in rest_plan[i] if i < len(rest_plan) else ():
            scatter.stage(a, step)
        total.stage(i + 1)
    for i in range(n_slots + 1, 5):
        total.stage(i)
    small_out[...] = own_slices(value[4], scatter.dp * 4 + scatter.z)
    scatter.stage(4, 3)
    scatter.stage(5, 3)
    for i in range(max(n_slots - 2, 0), n_slots):
        store[i].wait()

    @pl.when(jnp.logical_not(chain.is_last))
    def _():
        for s in range(groups):
            chain.sent(s)

    scatter.finish()
    total.finish()


VMEM = pl.BlockSpec(memory_space=pltpu.VMEM)
SMEM = pl.BlockSpec(memory_space=pltpu.SMEM)
ANY = pl.BlockSpec(memory_space=pl.ANY)


def params(collective=None):
    if collective is None:
        return pltpu.CompilerParams(vmem_limit_bytes=BIG)
    return pltpu.CompilerParams(vmem_limit_bytes=BIG, collective_id=collective, has_side_effects=True)


def shape(dims, kind=BF16):
    return jax.ShapeDtypeStruct(dims, kind)


def shards(
    tokens, lengths, weight_in, bias_in, weight_out, bias_out, gain_one, shift_one,
    weight_up, bias_up, weight_down, bias_down, gain_two, shift_two, cotangent,
):
    groups, local, width = tokens.shape
    rows = groups * local
    pairs = width // LANES
    count = local // CHUNK
    axes = ("dp", "head")
    parts = lax.axis_size("head")
    me = lax.axis_index("head")

    by_kernel = lax.axis_size("dp") == 8 and parts == 4
    small = (bias_in, bias_out, gain_one, shift_one, bias_up, bias_down, gain_two, shift_two)
    tok = tokens.reshape(rows, width)
    units = groups * pairs
    plane = shape((rows, width))
    table = pltpu.VMEM((rows, LANES), F32)
    within = pltpu.VMEM((groups, CHUNK, CHUNK), F32)
    tall = pltpu.VMEM((rows, width), F32)
    flat = pltpu.VMEM((rows, width), BF16)

    def sums_scratch():
        return [
            pltpu.VMEM((units, 128, LANES), F32),
            pltpu.VMEM((units, 8, 256), F32),
            pltpu.VMEM((units * max(count - 1, 1), 128, LANES), F32),
            pltpu.VMEM((units * max(count - 1, 1), 8, 256), F32),
            pltpu.VMEM((units, 128, LANES), F32),
            pltpu.VMEM((units, 8, 256), F32),
        ]

    forward_shapes = (plane,) * 6 + (shape((units * count, 256, 256)), shape((units * count, 8, 256), F32))
    forward_scratch = [table, table, table, within] + sums_scratch() + [tall, tall]
    ff = weight_up.shape[1]
    if by_kernel:
        square = shape((width, width))
        sizes = [item.shape[0] for item in small]
        half = (2 * weight_in.shape[0], width // 2)
        (
            q, k, v, joined, rest, inverse, states, state_rows, w_q, w_k, w_v, w_out, w_up, w_down, vectors
        ) = pl.pallas_call(
            functools.partial(front_kernel, groups, local, sizes),
            out_shape=forward_shapes
            + (square,) * 4
            + (shape((width, ff)), shape((4,) + weight_down.shape), shape((len(small), ff), F32)),
            in_specs=[SMEM] + [VMEM] * (5 + len(small)),
            out_specs=(ANY,) * 7 + (VMEM,) + (ANY,) * 6 + (VMEM,),
            scratch_shapes=forward_scratch
            + [flat] * 6
            + [pltpu.VMEM((units * count, 256, 256), BF16)]
            + [pltpu.VMEM((width, width), BF16)] * 4
            + [pltpu.VMEM((width, ff), BF16), pltpu.SemaphoreType.DMA((8 + 4 * groups,))]
            + [pltpu.VMEM(weight_down.shape, BF16), pltpu.SemaphoreType.DMA((1,))]
            + [pltpu.SemaphoreType.DMA((1, 3))] * 2
            + [pltpu.VMEM((32, 8, LANES), F32)]
            + [pltpu.VMEM((32,) + half, BF16)] * 4
            + [pltpu.VMEM((32, 4 * weight_up.shape[0], ff // 4), BF16)]
            + [pltpu.SemaphoreType.DMA((7, 31)), pltpu.SemaphoreType.DMA((7, 31))]
            + chain_scratch(groups, pairs),
            compiler_params=params(3),
        )(lengths, tok, weight_in, weight_out, weight_up, weight_down, *(item.reshape(1, -1) for item in small))
    else:

        def gather(item):
            return lax.all_gather(item.astype(BF16), axes, axis=0, tiled=True)

        w_in, w_out, w_up, w_down = map(gather, (weight_in, weight_out, weight_up, weight_down))
        sizes = [item.shape[0] for item in small]
        gathered = lax.all_gather(jnp.concatenate([item.astype(BF16) for item in small]), axes, axis=0)
        cuts = [sum(sizes[:i]) for i in range(len(sizes) + 1)]
        b_in, b_out, g_one, s_one, b_up, b_down, g_two, s_two = (
            gathered[:, a:b].reshape(1, -1).astype(F32) for a, b in zip(cuts, cuts[1:])
        )
        w_q, w_k, w_v = (w_in[:, j * width : (j + 1) * width] for j in range(3))
        q, k, v, joined, rest, inverse, states, state_rows = pl.pallas_call(
            functools.partial(attend_kernel, groups, local),
            out_shape=forward_shapes,
            in_specs=[SMEM] + [VMEM] * 5,
            out_specs=(VMEM,) * 8,
            scratch_shapes=forward_scratch + chain_scratch(groups, pairs),
            compiler_params=params(1),
        )(lengths, tok, w_q, w_k, w_v, b_in)

    tile = local

    if by_kernel:
        slabs96 = shape((32, 96, width))
        term_out = shape((32,) + half)
        kept = pltpu.VMEM((rows // 96 * (ff // width), 96, width), BF16)
        tile_s = pltpu.VMEM((TALL, width), F32)
        activations, g_first, g_joined, gw_up, gw_out, gw_down, small_sums = pl.pallas_call(
            middle_kernel,
            out_shape=[
                plane, shape((rows, width), F32), plane, slabs96, term_out,
                shape(weight_down.shape, F32), shape((16, width), F32),
            ],
            in_specs=[ANY] * 3 + [VMEM, ANY, ANY, VMEM],
            out_specs=[ANY] * 5 + [VMEM] * 2,
            scratch_shapes=[flat] * 4
            + [tall, tall, table, kept, kept]
            + [pltpu.VMEM((width, ff), BF16), pltpu.VMEM((32, 96, width), BF16), pltpu.VMEM((31, 96, width), BF16)]
            + [tile_s, tile_s, pltpu.VMEM((32,) + half, BF16)]
            + [pltpu.VMEM((6, 8, width), F32), pltpu.VMEM((8, ff), F32)]
            + [pltpu.SemaphoreType.DMA((6,))]
            + [pltpu.SemaphoreType.DMA((1, 28))] * 2
            + [pltpu.SemaphoreType.DMA((2, 10))] * 2,
            compiler_params=params(5),
        )(tok, joined, cotangent.reshape(rows, width), w_out, w_up, w_down, vectors)
        terms = [gw_up.shape, gw_out.shape] + [(32,) + half] * 3
        row_shape = (weight_out.shape[0], width)
        input_grad, gw_up, gw_out, gw_q, gw_k, gw_v, sums = pl.pallas_call(
            functools.partial(tail_kernel, groups, local),
            out_shape=[shape((rows, width), F32), shape(weight_up.shape, F32)]
            + [shape(row_shape, F32)] * 4
            + [shape((16, LANES), F32)],
            in_specs=[SMEM] + [ANY] * 7 + [VMEM] * 2 + [ANY] * 7 + [VMEM],
            out_specs=[ANY] + [VMEM] * 6,
            scratch_shapes=[flat] * 7
            + [table, table, within]
            + sums_scratch()
            + [pltpu.VMEM((2, local, width), F32)]
            + [pltpu.SemaphoreType.DMA((9,)), pltpu.SemaphoreType.DMA((2, 2))]
            + [pltpu.VMEM(item, BF16) for item in terms]
            + [pltpu.VMEM((31,) + item[1:], BF16) for item in terms]
            + [pltpu.VMEM((5,) + small_sums.shape, F32), pltpu.VMEM((6,) + small_sums.shape, F32)]
            + [pltpu.SemaphoreType.DMA((6, 10))] * 2
            + [pltpu.SemaphoreType.DMA((1, 6))] * 2
            + chain_scratch(groups, pairs),
            compiler_params=params(4),
        )(
            lengths, q, k, v, g_joined, joined, rest, inverse, states, state_rows,
            tok, w_q, w_k, w_v, g_first, gw_up, gw_out, small_sums,
        )
        kinds = (3 * width, width, width, width, width, ff, width, width, width)
        mine = [sums[j, : (2 * width if j == 0 else size) // 32] for j, size in enumerate(kinds)]
        gb_front, gb_value, gb_out, gg_one, gs_one, gb_up, gb_down, gg_two, gs_two = mine
        activations, input_grad, gw_down, gw_up, gw_out, gw_in = pl.pallas_call(
            finish_kernel,
            out_shape=[plane, shape((rows, width), F32)]
            + [shape(item.shape, F32) for item in (weight_down, weight_up, weight_out, weight_in)],
            in_specs=[ANY] * 8,
            out_specs=[ANY] * 6,
            scratch_shapes=[
                pltpu.VMEM(item.shape, item.dtype)
                for item in (input_grad, activations, gw_down, gw_up, gw_out, gw_q, gw_k, gw_v)
            ]
            + [pltpu.SemaphoreType.DMA((2, 15))],
            compiler_params=params(),
        )(activations, input_grad, gw_down, gw_up, gw_out, gw_q, gw_k, gw_v)
        return (
            activations.reshape(groups, local, width),
            input_grad.reshape(groups, local, width),
            gw_in, gb_front, gb_value, gw_out, gb_out, gg_one, gs_one,
            gw_up, gb_up, gw_down, gb_down, gg_two, gs_two,
        )

    def block(cols):
        return pl.BlockSpec((tile, cols), lambda i: (i, 0))

    def fixed(*dims):
        return pl.BlockSpec(dims, lambda i: (0,) * len(dims), pipeline_mode=pl.Buffered(1))

    vectors = [fixed(1, width)] * 3 + [fixed(1, ff)] + [fixed(1, width)] * 3
    weights = [fixed(width, width), fixed(width, ff), fixed(ff, width)]
    vector_shapes = [shape((1, width), F32)] * 3 + [shape((1, ff), F32)] + [shape((1, width), F32)] * 3
    (
        activations, g_first, g_joined, gw_out, gw_up, gw_down,
        gb_out, gg_one, gs_one, gb_up, gb_down, gg_two, gs_two,
    ) = pl.pallas_call(
        feed_kernel,
        grid=(rows // tile,),
        out_shape=[plane, shape((rows, width), F32), plane]
        + [shape((width, width), F32), shape((width, ff), F32), shape((ff, width), F32)]
        + vector_shapes,
        in_specs=[block(width)] * 3 + weights + vectors,
        out_specs=[block(width)] * 3 + weights + vectors,
        scratch_shapes=[
            pltpu.VMEM((tile, width), F32),
            pltpu.VMEM((tile, width), BF16),
            pltpu.VMEM((tile, ff), BF16),
            pltpu.VMEM((tile, ff), BF16),
            pltpu.VMEM((tile, width), F32),
            pltpu.VMEM((tile, width), BF16),
        ],
        compiler_params=params(),
    )(
        tok, joined, cotangent.reshape(rows, width), w_out, w_up, w_down,
        b_out, g_one, s_one, b_up, b_down, g_two, s_two,
    )
    g_mixed = pl.pallas_call(
        functools.partial(back_kernel, groups, local),
        out_shape=shape((rows, 3 * width)),
        in_specs=[SMEM] + [VMEM] * 9,
        out_specs=VMEM,
        scratch_shapes=[table, table, within] + sums_scratch()
        + [pltpu.VMEM((rows, width), BF16), tall, pltpu.VMEM((rows, width), BF16)] + chain_scratch(groups, pairs),
        compiler_params=params(2),
    )(lengths, q, k, v, g_joined, joined, rest, inverse, states, state_rows)
    input_grad, gw_in, gb_in = pl.pallas_call(
        input_kernel,
        grid=(rows // tile,),
        out_shape=[shape((rows, width), F32), shape((width, 3 * width), F32), shape((1, 3 * width), F32)],
        in_specs=[block(width), block(3 * width), fixed(width, 3 * width), block(width)],
        out_specs=[block(width), fixed(width, 3 * width), fixed(1, 3 * width)],
        compiler_params=params(),
    )(tok, g_mixed, w_in, g_first)

    gb_in = gb_in.reshape(-1)
    cols = [gb_in[: 2 * width], gb_in[2 * width :]] + [
        item.reshape(-1) for item in (gb_out, gg_one, gs_one, gb_up, gb_down, gg_two, gs_two)
    ]
    total = lax.axis_size(axes)
    def scatter(item):
        return lax.psum_scatter(item, axes, scatter_dimension=0, tiled=True)

    cut = [item.shape[0] // total for item in cols]
    merged = scatter(jnp.concatenate([item.reshape(total, -1) for item in cols], axis=1).reshape(-1))
    places = [sum(cut[:i]) for i in range(len(cut) + 1)]
    (gb_front, gb_value, gb_out, gg_one, gs_one, gb_up, gb_down, gg_two, gs_two) = (
        merged[a:b] for a, b in zip(places, places[1:])
    )
    return (
        activations.reshape(groups, local, width),
        input_grad.reshape(groups, local, width),
        scatter(gw_in), gb_front, gb_value, scatter(gw_out), gb_out, gg_one, gs_one,
        scatter(gw_up), gb_up, scatter(gw_down), gb_down, gg_two, gs_two,
    )


def solution(mesh):
    spread_rows = P("dp", "head", None)
    matrix = P(("dp", "head"), None)
    vector = P(("dp", "head"))
    return jax.shard_map(
        shards,
        mesh=mesh,
        in_specs=(
            spread_rows, P("dp"), matrix, vector, matrix, vector, vector, vector,
            matrix, vector, matrix, vector, vector, vector, spread_rows,
        ),
        out_specs=(
            spread_rows, spread_rows, matrix, vector, vector, matrix, vector, vector, vector,
            matrix, vector, matrix, vector, vector, vector,
        ),
        check_vma=False,
    )
```

```python
import functools
import math

import jax
import jax.numpy as jnp
from jax import lax
from jax.experimental import pallas as pl
from jax.experimental.pallas import tpu as pltpu
from jax.sharding import PartitionSpec as P

F32 = jnp.float32
BF16 = jnp.bfloat16
CHUNK = 256
LANES = 128
HALF = 64
BIG = 62 * 1024 * 1024
MESH = pl.DeviceIdType.MESH


def dot(a, b):
    return lax.dot_general(a, b, (((1,), (0,)), ((), ())), preferred_element_type=F32)


def dot_t(a, b):
    return lax.dot_general(a, b, (((1,), (1,)), ((), ())), preferred_element_type=F32)


def tdot(a, b):
    return lax.dot_general(a, b, (((0,), (0,)), ((), ())), preferred_element_type=F32)


def iota(shape, dim):
    return lax.broadcasted_iota(jnp.int32, shape, dim)


def block_mask(rows, cols):
    return ((iota((rows, cols), 0) & HALF) == (iota((rows, cols), 1) & HALF)).astype(F32)


def head_masks():
    lane = iota((1, LANES), 1)
    first = (lane < HALF).astype(F32)
    place = lane & (HALF - 1)
    return first, 1.0 - first, (place == 0).astype(F32), (place == 1).astype(F32)


def cos_poly(z):
    t = z * z
    r = -1.0 / 3628800 + t * (1.0 / 479001600)
    r = 1.0 / 40320 + t * r
    r = -1.0 / 720 + t * r
    r = 1.0 / 24 + t * r
    r = -0.5 + t * r
    return 1.0 + t * r


def sin_poly(z):
    t = z * z
    r = -1.0 / 39916800 + t * (1.0 / 6227020800)
    r = 1.0 / 362880 + t * r
    r = -1.0 / 5040 + t * r
    r = 1.0 / 120 + t * r
    r = -1.0 / 6 + t * r
    return z + z * (t * r)


def angles(start, limit, rows):
    place = iota((rows, LANES), 0) + start
    theta = jnp.minimum((0.5 * math.pi * place.astype(F32)) / limit.astype(F32), 0.5 * math.pi)
    return cos_poly(theta), sin_poly(theta), (place < limit).astype(F32)


def weights_within(limit):
    apart = iota((CHUNK, CHUNK), 0) - iota((CHUNK, CHUNK), 1)
    theta = jnp.minimum((0.5 * math.pi * apart.astype(F32)) / limit.astype(F32), 0.5 * math.pi)
    return jnp.where(apart >= 0, cos_poly(theta), 0.0)


def softplus(x):
    t = jnp.exp(-jnp.abs(x))
    tail = jnp.where(t < 1e-3, t * (1.0 - 0.5 * t), jnp.log(1.0 + t))
    return jnp.maximum(x, 0.0) + tail


def slope(feature):
    small = feature * (1.0 - feature * (0.5 - feature * (1.0 / 6)))
    return jnp.where(feature < 0.01, small, 1.0 - jnp.exp(-feature))


def pack(state):
    return jnp.concatenate([state[0:64] + state[64:128], state[128:192] + state[192:256]], axis=0)


def unpack(packed, mask):
    top, bottom = packed[0:64], packed[64:128]
    return jnp.concatenate([top, top, bottom, bottom], axis=0) * mask


def column_of(row, first):
    halves = []
    for at in (0, LANES):
        turned = jnp.broadcast_to(row[:, at : at + LANES], (LANES, LANES)).T
        halves.append(jnp.where(first > 0, turned[0:64], turned[64:128]))
    return jnp.concatenate(halves, axis=0)


def two_parts(state):
    high = state.astype(BF16)
    return jnp.concatenate([high, (state - high.astype(F32)).astype(BF16)], axis=1)


def twice(value):
    return jnp.concatenate([value, value], axis=1)


def spread(feature, cosine, sine):
    return jnp.concatenate([feature * cosine, feature * sine], axis=1).astype(BF16)


def stacked_heads(value, first, second):
    return jnp.concatenate([value * first, value * second], axis=0).astype(BF16)


def rows_of(s, c, local):
    return pl.ds(pl.multiple_of(s * local + c * CHUNK, CHUNK), CHUNK)


def lanes_of(p):
    return pl.ds(pl.multiple_of(p * LANES, LANES), LANES)


def fill_tables(groups, local, base, lens, cos_s, sin_s, ok_s, within):
    for s in range(groups):
        cosine, sine, valid = angles(base, lens[s], local)
        cos_s[s * local : (s + 1) * local] = cosine
        sin_s[s * local : (s + 1) * local] = sine
        if ok_s is not None:
            ok_s[s * local : (s + 1) * local] = valid
        within[s] = weights_within(lens[s])


def meet(targets):
    barrier = pltpu.get_barrier_semaphore()
    for target in targets:
        pl.semaphore_signal(barrier, inc=1, device_id=target, device_id_type=MESH)
    pl.semaphore_wait(barrier, len(targets))


class Chain:
    def __init__(self, step, pairs, refs):
        self.at, self.parts, self.pairs = lax.axis_index("head"), lax.axis_size("head"), pairs
        self.out_state, self.out_rows, self.in_state, self.in_rows, self.send, self.recv = refs
        self.before = {"head": lax.rem(self.at + self.parts - step, self.parts)}
        self.after = {"head": lax.rem(self.at + self.parts + step, self.parts)}
        last = self.parts - 1
        self.is_first = self.at == (0 if step > 0 else last)
        self.is_last = self.at == (last if step > 0 else 0)

    def copies(self, s):
        some = pl.ds(s * self.pairs, self.pairs)
        return [
            pltpu.make_async_remote_copy(
                src_ref=src.at[some], dst_ref=dst.at[some],
                send_sem=self.send.at[s, j], recv_sem=self.recv.at[s, j],
                device_id=self.after, device_id_type=MESH,
            )
            for j, (src, dst) in enumerate(
                ((self.out_state, self.in_state), (self.out_rows, self.in_rows))
            )
        ]

    def start(self, s):
        for copy in self.copies(s):
            copy.start()

    def arrive(self, s):
        for copy in self.copies(s):
            copy.wait_recv()

    def sent(self, s):
        for copy in self.copies(s):
            copy.wait_send()


def chain_scratch(groups, pairs):
    return [
        pltpu.VMEM((groups * pairs, 128, LANES), BF16),
        pltpu.VMEM((groups * pairs, 8, 256), F32),
        pltpu.VMEM((groups * pairs, 128, LANES), BF16),
        pltpu.VMEM((groups * pairs, 8, 256), F32),
        pltpu.SemaphoreType.DMA((groups, 2)),
        pltpu.SemaphoreType.DMA((groups, 2)),
    ]


class Forward:
    def __init__(self, groups, local, lens, chain, outs, tables, sums):
        self.groups, self.local, self.lens, self.chain = groups, local, lens, chain
        self.outs, self.tables, self.sums_refs = outs, tables, sums
        self.pairs = outs[0].shape[1] // LANES
        self.count = local // CHUNK

    def prepare(self):
        cos_s, sin_s, ok_s, within = self.tables[:4]
        fill_tables(self.groups, self.local, self.chain.at * self.local, self.lens, cos_s, sin_s, ok_s, within)

    def project(self, piece, tok, weight, bias, s=None):
        out, ok_s, width = self.outs[piece], self.tables[2], tok.shape[1]

        def body(i, _):
            r = pl.ds(pl.multiple_of(i * self.local, self.local), self.local)
            for n in range(0, width, 256):
                m = piece * width + n
                y = dot(tok[r], weight[:, n : n + 256]) + bias[:, m : m + 256]
                out[r, n : n + 256] = (softplus(y) * twice(ok_s[r]) if piece < 2 else y).astype(BF16)
            return 0

        low, high = (0, self.groups) if s is None else (s, s + 1)
        lax.fori_loop(low, high, body, 0)

    def over(self, step, s=None):
        low, high = (0, self.groups) if s is None else (s, s + 1)
        lax.fori_loop(low * self.pairs, high * self.pairs, step, 0)

    def names(self):
        return (self.local, self.pairs, self.count, self.chain) + tuple(self.outs) + tuple(self.tables) + tuple(self.sums_refs)

    def steps(self):
        (
            local, pairs, count, chain, q, k, v, joined, rest, inverse, states, rows_out,
            cos_s, sin_s, ok_s, within, num_s, den_s, own, own_rows, part, part_rows, came, came_rows,
        ) = self.names()

        def sums(i, _):
            s, p = i // pairs, i % pairs
            mask = block_mask(256, LANES)
            total = jnp.zeros((256, LANES), F32)
            row = jnp.zeros((1, 256), F32)
            for c in range(count):
                r, n = rows_of(s, c, local), lanes_of(p)
                k2 = spread(k[r, n].astype(F32), cos_s[r], sin_s[r])
                total = total + tdot(k2, v[r, n])
                row = row + column_sum(k2.astype(F32))
                if c + 1 < count:
                    part[i * (count - 1) + c] = pack(total * mask)
                    part_rows[i * (count - 1) + c] = jnp.broadcast_to(row, (8, 256))
            own[i] = pack(total * mask)
            own_rows[i] = jnp.broadcast_to(row, (8, 256))
            came[i] = jnp.zeros((128, LANES), F32)
            came_rows[i] = jnp.zeros((8, 256), F32)
            return 0

        def arrive(s):
            chain.arrive(s)

            def one(p, _):
                i = s * pairs + p
                rows = chain.in_rows[i]
                column = column_of(rows[0:1], head_masks()[0])
                came[i] = chain.in_state[i].astype(F32) + column * rows[1:2, 0:LANES]
                came_rows[i] = rows
                return 0

            lax.fori_loop(0, pairs, one, 0)

        def leave(s):
            def one(p, _):
                i = s * pairs + p
                total = came[i] + own[i]
                row = came_rows[i][0:1] + own_rows[i][0:1]
                column = column_of(row, head_masks()[0])
                centre = column_sum(total) / jnp.maximum(column_sum(column), 1e-30)
                centre = centre.astype(BF16).astype(F32)
                chain.out_state[i] = (total - column * centre).astype(BF16)
                chain.out_rows[i] = jnp.concatenate([row, twice(centre), jnp.zeros((6, 256), F32)], axis=0)
                return 0

            lax.fori_loop(0, pairs, one, 0)
            chain.start(s)

        def intra(i, _):
            s, p = i // pairs, i % pairs
            n = lanes_of(p)
            first, second, _, _ = head_masks()
            ones = jnp.ones((CHUNK, LANES), BF16)
            m = within[s]
            m = jnp.concatenate([m, m], axis=0)
            for c in range(count):
                r = rows_of(s, c, local)
                scores = dot_t(stacked_heads(q[r, n].astype(F32), first, second), k[r, n])
                inner = dot((scores * m).astype(BF16), jnp.concatenate([v[r, n], ones], axis=1))
                both = jnp.where(twice(first) > 0, inner[:CHUNK], inner[CHUNK:])
                num_s[r, n] = both[:, :LANES]
                den_s[r, n] = both[:, LANES:]
            return 0

        def inter(i, _):
            s, p = i // pairs, i % pairs
            n = lanes_of(p)
            mask = block_mask(256, LANES)
            ones = block_mask(LANES, LANES).astype(BF16)
            for c in range(count):
                r = rows_of(s, c, local)
                state, row = came[i], came_rows[i][0:1]
                if c > 0:
                    state = state + part[i * (count - 1) + c - 1]
                    row = row + part_rows[i * (count - 1) + c - 1][0:1]
                state = two_parts(unpack(state, mask))
                states[i * count + c] = state
                rows_out[i * count + c] = jnp.broadcast_to(row, (8, 256))
                q2 = spread(q[r, n].astype(F32), cos_s[r], sin_s[r])
                both = dot(q2, state)
                num = both[:, :LANES] + both[:, LANES:] + num_s[r, n]
                weighed = q2.astype(F32) * row
                weighed = (weighed[:, :LANES] + weighed[:, LANES:]).astype(BF16)
                den = dot(weighed, ones) + den_s[r, n]
                above = 1.0 / jnp.maximum(den, 1.0)
                attended = num * above
                rounded = attended.astype(BF16)
                joined[r, n] = rounded
                rest[r, n] = (attended - rounded.astype(F32)).astype(BF16)
                inverse[r, n] = jnp.where(den > 1.0, above, -1.0).astype(BF16)
            return 0

        return sums, arrive, leave, intra, inter


def attend_kernel(
    groups, local, lens, tok, w_q, w_k, w_v, bias,
    q, k, v, joined, rest, inverse, states, rows_out,
    cos_s, sin_s, ok_s, within, own, own_rows, part, part_rows, came, came_rows, num_s, den_s, *link,
):
    chain = Chain(1, tok.shape[1] // LANES, link)
    meet([chain.before, chain.after])
    work = Forward(
        groups, local, lens, chain, (q, k, v, joined, rest, inverse, states, rows_out),
        (cos_s, sin_s, ok_s, within, num_s, den_s), (own, own_rows, part, part_rows, came, came_rows),
    )
    work.prepare()
    for piece, weight in enumerate((w_q, w_k, w_v)):
        work.project(piece, tok, weight, bias)
    sums, arrive, leave, intra, inter = work.steps()
    work.over(sums)

    @pl.when(chain.is_first)
    def _():
        for s in range(groups):
            leave(s)

    work.over(intra)

    @pl.when(jnp.logical_not(chain.is_first))
    def _():
        for s in range(groups):
            arrive(s)

            @pl.when(jnp.logical_not(chain.is_last))
            def _():
                leave(s)

    work.over(inter)

    @pl.when(jnp.logical_not(chain.is_last))
    def _():
        for s in range(groups):
            chain.sent(s)


def gelu_both(x):
    phi = 0.5 + 0.5 * lax.erf(x * (1.0 / math.sqrt(2.0)))
    return x * phi, phi + x * (jnp.exp(-0.5 * x * x) * (1.0 / math.sqrt(2.0 * math.pi)))


def mean_of(x):
    return jnp.mean(x, axis=1, keepdims=True)


def column_sum(x):
    return jnp.sum(x, axis=0, keepdims=True)


def normalised(x):
    centred = x - mean_of(x)
    inv = lax.rsqrt(mean_of(centred * centred) + 1e-05)
    return centred * inv, inv


def feed_kernel(
    tok, joined, cot, w_out, w_up, w_down, b_out, g_one, s_one, b_up, b_down, g_two, s_two,
    act, g_first, g_joined, gw_out, gw_up, gw_down, gb_out, gg_one, gs_one, gb_up, gb_down, gg_two, gs_two,
    norm_s, low_s, hid_s, der_s, sec_s, branch_s,
):
    rows = tok.shape[0]
    ff = w_up.shape[1]
    step = 768
    count = ff // step

    @pl.when(pl.program_id(0) == 0)
    def _():
        for ref in (gw_out, gw_up, gw_down, gb_out, gg_one, gs_one, gb_up, gb_down, gg_two, gs_two):
            ref[...] = jnp.zeros_like(ref)

    first = tok[...].astype(F32) + (dot(joined[...], w_out[...]) + b_out[...])
    unit_one, inv_one = normalised(first)
    norm_s[...] = unit_one
    normed = unit_one * g_one[...] + s_one[...]
    low_s[...] = normed.astype(BF16)
    sec_s[...] = normed + b_down[...]

    def up(j, _):
        n = pl.ds(pl.multiple_of(j * step, step), step)
        x = dot(low_s[...], w_up[:, n]) + b_up[:, n]
        y, d = gelu_both(x)
        hid_s[:, n] = y.astype(BF16)
        der_s[:, n] = d.astype(BF16)
        return 0

    lax.fori_loop(0, count, up, 0)
    second = sec_s[...] + dot(hid_s[...], w_down[...])
    unit_two, inv_two = normalised(second)
    act[...] = (unit_two * g_two[...] + s_two[...]).astype(BF16)
    c = cot[...].astype(F32)
    gg_two[...] += column_sum(c * unit_two)
    gs_two[...] += column_sum(c)
    e = c * g_two[...]
    g_second = inv_two * (e - mean_of(e) - unit_two * mean_of(e * unit_two))
    sec_s[...] = g_second
    branch = g_second.astype(BF16)
    branch_s[...] = branch
    gb_down[...] += column_sum(branch.astype(F32))

    def down(j, _):
        n = pl.ds(pl.multiple_of(j * step, step), step)
        gh = dot_t(branch_s[...], w_down[n, :])
        gu = gh * der_s[:, n].astype(F32)
        gu = gu.astype(BF16)
        der_s[:, n] = gu
        gb_up[:, n] += column_sum(gu.astype(F32))
        gw_down[n, :] += tdot(hid_s[:, n], branch_s[...])
        gw_up[:, n] += tdot(low_s[...], gu)
        return 0

    lax.fori_loop(0, count, down, 0)
    g_normed = sec_s[...] + dot_t(der_s[...], w_up[...])
    unit_one = norm_s[...]
    gg_one[...] += column_sum(g_normed * unit_one)
    gs_one[...] += column_sum(g_normed)
    e = g_normed * g_one[...]
    gf = inv_one * (e - mean_of(e) - unit_one * mean_of(e * unit_one))
    g_first[...] = gf
    go = gf.astype(BF16)
    gb_out[...] += column_sum(go.astype(F32))
    gw_out[...] += tdot(joined[...], go)
    g_joined[...] = dot_t(go, w_out[...]).astype(BF16)


def back_kernel(
    groups, local, lens, q, k, v, gj, joined, rest, inverse, states, rows_in, out,
    cos_s, sin_s, within, own, own_rows, part, part_rows, came, came_rows, gnum_s, gden_s, lane_s, *link,
):
    width = q.shape[1]
    pairs = width // LANES
    count = local // CHUNK
    chain = Chain(-1, pairs, link)
    meet([chain.before, chain.after])
    fill_tables(groups, local, chain.at * local, lens, cos_s, sin_s, None, within)

    def sums(i, _):
        s, p = i // pairs, i % pairs
        n = lanes_of(p)
        _, _, one, two = head_masks()
        mask = block_mask(256, LANES)
        ones = block_mask(2 * LANES, LANES).astype(BF16)
        total = jnp.zeros((256, LANES), F32)
        row = jnp.zeros((1, 256), F32)
        for c in reversed(range(count)):
            r = rows_of(s, c, local)
            ri = inverse[r, n].astype(F32)
            gnum = (gj[r, n].astype(F32) * jnp.abs(ri)).astype(BF16)
            product = gnum.astype(F32) * (joined[r, n].astype(F32) + rest[r, n].astype(F32))
            gden = jnp.where(ri > 0, -dot(two_parts(product), ones), 0.0)
            high = gden.astype(BF16).astype(F32)
            gnum_s[r, n] = gnum
            gden_s[r, n] = gden
            lane_s[r, n] = (high * one + (gden - high) * two).astype(BF16)
            q2 = spread(q[r, n].astype(F32), cos_s[r], sin_s[r])
            total = total + tdot(q2, gnum)
            row = row + column_sum(q2.astype(F32) * twice(gden))
            if c > 0:
                part[i * (count - 1) + c - 1] = pack(total * mask)
                part_rows[i * (count - 1) + c - 1] = jnp.broadcast_to(row, (8, 256))
        own[i] = pack(total * mask)
        own_rows[i] = jnp.broadcast_to(row, (8, 256))
        came[i] = jnp.zeros((128, LANES), F32)
        came_rows[i] = jnp.zeros((8, 256), F32)
        return 0

    def arrive(s):
        chain.arrive(s)

        def one(p, _):
            i = s * pairs + p
            came[i] = chain.in_state[i].astype(F32)
            came_rows[i] = chain.in_rows[i]
            return 0

        lax.fori_loop(0, pairs, one, 0)

    def leave(s):
        def one(p, _):
            i = s * pairs + p
            n = lanes_of(p)
            total = came[i] + own[i]
            low = total.astype(BF16)
            chain.out_state[i] = low
            lost = unpack(total - low.astype(F32), block_mask(256, LANES)).astype(BF16)
            mean = column_sum(v[pl.ds(s * local, local), n].astype(F32)) * (1.0 / local)
            row = dot_t(jnp.broadcast_to(mean, (8, LANES)).astype(BF16), lost)
            chain.out_rows[i] = came_rows[i] + own_rows[i] + row
            return 0

        lax.fori_loop(0, pairs, one, 0)
        chain.start(s)

    def main(i, _):
        s, p = i // pairs, i % pairs
        n = lanes_of(p)
        first, second, one, two = head_masks()
        mask = block_mask(256, LANES)
        ones = jnp.ones((CHUNK, LANES), BF16)
        m = within[s]
        m = jnp.concatenate([m, m], axis=0)
        for c in range(count):
            r = rows_of(s, c, local)
            cosine, sine = cos_s[r], sin_s[r]
            feature, key, value = q[r, n].astype(F32), k[r, n], v[r, n]
            gnum, gden, lane = gnum_s[r, n], gden_s[r, n], lane_s[r, n].astype(F32)
            row = rows_in[i * count + c][0:1]
            outer = dot_t(twice(gnum), states[i * count + c]) + twice(gden) * row
            gq = outer[:, :LANES] * cosine + outer[:, LANES:] * sine
            heads = stacked_heads(feature, first, second)
            scores = (dot_t(heads, key) * m).astype(BF16)
            gheads = stacked_heads(gnum.astype(F32), first, second)
            left = jnp.concatenate([gheads, stacked_heads(lane, first, second)], axis=1)
            g = (dot_t(left, jnp.concatenate([value, ones], axis=1)) * m).astype(BF16)
            inner = dot(g, key)
            gq = gq + jnp.where(first > 0, inner[:CHUNK], inner[CHUNK:])
            state, row = came[i], came_rows[i][0:1]
            if c + 1 < count:
                state = state + part[i * (count - 1) + c]
                row = row + part_rows[i * (count - 1) + c][0:1]
            state = two_parts(unpack(state, mask))
            k2 = spread(key.astype(F32), cosine, sine)
            gv = dot(k2, state[:, :LANES]) + tdot(gheads, scores).T
            outer = dot_t(twice(value), state) + row
            gk = outer[:, :LANES] * cosine + outer[:, LANES:] * sine + tdot(heads, g).T
            out[r, n] = (gq * slope(feature)).astype(BF16)
            out[r, pl.ds(pl.multiple_of(width + p * LANES, LANES), LANES)] = (
                gk * slope(key.astype(F32))
            ).astype(BF16)
            out[r, pl.ds(pl.multiple_of(2 * width + p * LANES, LANES), LANES)] = gv.astype(BF16)
        return 0

    lax.fori_loop(0, groups * pairs, sums, 0)

    @pl.when(chain.is_first)
    def _():
        for s in range(groups):
            leave(s)

    @pl.when(jnp.logical_not(chain.is_first))
    def _():
        for s in range(groups):
            arrive(s)

            @pl.when(jnp.logical_not(chain.is_last))
            def _():
                leave(s)

    lax.fori_loop(0, groups * pairs, main, 0)

    @pl.when(jnp.logical_not(chain.is_last))
    def _():
        for s in range(groups):
            chain.sent(s)


def input_kernel(tok, gm, weight, g_first, grad, gw, gb):
    @pl.when(pl.program_id(0) == 0)
    def _():
        gw[...] = jnp.zeros_like(gw)
        gb[...] = jnp.zeros_like(gb)

    low = gm[...]
    gb[...] += column_sum(low.astype(F32))
    gw[...] += tdot(tok[...], low)
    grad[...] = g_first[...] + dot_t(low, weight[...])


def peers():
    dp, z = lax.axis_index("dp"), lax.axis_index("head")
    core, x, y = lax.rem(dp, 2), lax.rem(dp // 2, 2), dp // 4
    twin = dp + 1 - 2 * core
    along_x, along_y = dp + 2 - 4 * x, dp + 4 - 8 * y
    one = along_x + core * (along_y - along_x)
    two = along_y + core * (along_x - along_y)
    return dp, z, twin, one, two, one + two - dp


class Copies:
    def __init__(self, send, recv):
        self.send, self.recv, self.all = send, recv, []

    def start(self, a, slot, src, dst, target):
        copy = pltpu.make_async_remote_copy(
            src_ref=src, dst_ref=dst, send_sem=self.send.at[a, slot], recv_sem=self.recv.at[a, slot],
            device_id=target, device_id_type=MESH,
        )
        copy.start()
        self.all.append(copy)
        return copy

    def finish(self):
        for copy in self.all:
            copy.wait_send()


class Gather:
    def __init__(self, arrays, send, recv):
        self.arrays = arrays
        self.copies, self.had = Copies(send, recv), {}
        self.dp, self.z, twin, one, two, self.far = peers()
        self.me = self.dp * 4 + self.z
        self.one, self.two = one, two
        self.to_z = [{"dp": self.dp, "head": lax.rem(self.z + k, 4)} for k in (1, 2, 3)]
        self.to_twin, self.to_one, self.to_two = (
            {"dp": d, "head": self.z} for d in (twin, one, two)
        )

    def targets(self):
        return self.to_z + [self.to_twin, self.to_one, self.to_two]

    def begin(self, a):
        ref, low, rows, fine = self.arrays[a]
        place = ref.at[self.me, pl.ds(low, rows)]
        for k in range(3):
            self.had[a, k] = self.copies.start(a, k, place, place, self.to_z[k])
        if fine:
            self.pass_one(a, 0, self.dp, ((3, self.to_one), (7, self.to_two), (15, self.to_twin)))

    def pass_one(self, a, k, block, ways):
        ref, low, rows, _ = self.arrays[a]
        place = ref.at[block * 4 + lax.rem(self.z + 4 - k, 4), pl.ds(low, rows)]
        for slot, target in ways:
            self.had[a, slot + k] = self.copies.start(a, slot + k, place, place, target)

    def fine_stage(self, a, g):
        if g == 5:
            for slot in range(15, 31):
                self.had[a, slot].wait_recv()
            return
        if g < 3:
            self.had[a, g].wait_recv()
            self.pass_one(a, g + 1, self.dp, ((3, self.to_one), (7, self.to_two), (15, self.to_twin)))
        if g < 4:
            self.had[a, 3 + g].wait_recv()
            self.pass_one(a, g, self.one, ((11, self.to_two), (19, self.to_twin)))
            self.had[a, 7 + g].wait_recv()
            self.pass_one(a, g, self.two, ((23, self.to_twin),))
        if g > 0:
            self.had[a, 10 + g].wait_recv()
            self.pass_one(a, g - 1, self.far, ((27, self.to_twin),))

    def pass_on(self, a, slot, block, target):
        ref, low, rows, _ = self.arrays[a]
        place = ref.at[pl.ds(block * 4, 4), pl.ds(low, rows)]
        self.had[a, slot] = self.copies.start(a, slot, place, place, target)

    def stage(self, a, step):
        if self.arrays[a][3]:
            self.fine_stage(a, step)
        elif step == 0:
            for k in range(3):
                self.had[a, k].wait_recv()
            self.pass_on(a, 3, self.dp, self.to_one)
            self.pass_on(a, 4, self.dp, self.to_two)
            self.pass_on(a, 5, self.dp, self.to_twin)
        elif step == 1:
            self.had[a, 3].wait_recv()
            self.pass_on(a, 6, self.one, self.to_two)
            self.pass_on(a, 7, self.one, self.to_twin)
        elif step == 2:
            self.had[a, 4].wait_recv()
            self.pass_on(a, 8, self.two, self.to_twin)
        elif step == 3:
            self.had[a, 6].wait_recv()
            self.pass_on(a, 9, self.far, self.to_twin)
        elif step == 4:
            for slot in (5, 7, 8, 9):
                self.had[a, slot].wait_recv()

    def finish(self):
        self.copies.finish()


class Scatter:
    def __init__(self, arrays, send, recv, place=lambda dp: dp * 4, straight=()):
        self.arrays, self.place, self.straight = arrays, place, straight
        self.copies, self.had = Copies(send, recv), {}
        self.dp, self.z, self.twin, self.one, self.two, self.far = peers()
        self.to_z = [{"dp": self.dp, "head": lax.rem(self.z + k, 4)} for k in (1, 2, 3)]
        self.to_twin, self.to_one, self.to_two, self.to_far = (
            {"dp": d, "head": self.z} for d in (self.twin, self.one, self.two, self.far)
        )

    def targets(self):
        return self.to_z + [self.to_twin, self.to_one, self.to_two] + ([self.to_far] if self.straight else [])

    def send(self, a, slot, src, count, box, target):
        buf, boxes, _, low, rows = self.arrays[a]
        some = pl.ds(low, rows)
        self.had[a, slot] = self.copies.start(
            a, slot, buf.at[pl.ds(src, count), some], boxes.at[pl.ds(box, count), some], target
        )

    def begin(self, a):
        shift = self.twin - self.dp
        for slot, dp in enumerate((self.far, self.one, self.two, self.dp)):
            self.send(a, slot, self.place(dp + shift), 4, slot * 4, self.to_twin)

    def wait(self, a, *slots):
        for slot in slots:
            self.had[a, slot].wait_recv()

    def add(self, a, dp, slots):
        buf, box, _, low, rows = self.arrays[a]
        start, some = self.place(dp), pl.ds(low, rows)

        def one(j, _):
            total = buf[start + j, some].astype(F32)
            for slot in slots:
                total = total + box[slot * 4 + j, some].astype(F32)
            buf[start + j, some] = total.astype(BF16)
            return 0

        lax.fori_loop(0, 4, one, 0)

    def finish_column(self, a, slots):
        self.wait(a, *(slot for slot in slots if slot != 4))
        self.add(a, self.dp, slots)
        for k in range(3):
            self.send(a, 7 + k, self.place(self.dp) + lax.rem(self.z + k + 1, 4), 1, 28 + k, self.to_z[k])

    def straight_stage(self, a):
        ways = ((self.far, 0, 4, 16, self.to_far), (self.two, 1, 5, 20, self.to_two), (self.one, 2, 6, 24, self.to_one))
        for dp, came, slot, box, target in ways:
            self.wait(a, came)
            self.add(a, dp, (came,))
            self.send(a, slot, self.place(dp), 4, box, target)

    def stage(self, a, step):
        if a in self.straight and step == 0:
            self.straight_stage(a)
        elif a in self.straight and step == 2:
            self.wait(a, 4)
            self.finish_column(a, (3, 4, 5, 6))
        elif step == 0:
            self.wait(a, 0)
            self.add(a, self.far, (0,))
            self.send(a, 4, self.place(self.far), 4, 16, self.to_two)
            self.wait(a, 1)
            self.add(a, self.two, (1,))
            self.send(a, 5, self.place(self.two), 4, 20, self.to_two)
        elif step == 1:
            self.wait(a, 2, 4)
            self.add(a, self.one, (2, 4))
            self.send(a, 6, self.place(self.one), 4, 24, self.to_one)
        elif step == 2:
            self.finish_column(a, (3, 5, 6))
        elif step == 3:
            self.wait(a, 7, 8, 9)
            buf, box, out, low, rows = self.arrays[a]
            some = pl.ds(low, rows)
            total = buf[self.place(self.dp) + self.z, some].astype(F32)
            for k in range(3):
                total = total + box[28 + k, some].astype(F32)
            have, cols = out.shape[0], total.shape[1]
            if have >= low + rows:
                out[low : low + rows] = total
            else:
                for j in range(rows // have):
                    m = (low // have + j) * cols
                    out[:, m : m + cols] = total[j * have : (j + 1) * have]

    def finish(self):
        self.copies.finish()


class Total:
    def __init__(self, scatter, value, box, send, recv):
        self.value, self.box, self.to = value, box, scatter
        self.copies, self.had = Copies(send, recv), {}

    def pass_on(self, slot, target):
        self.had[slot] = self.copies.start(0, slot, self.value.at[slot if slot < 3 else 3], self.box.at[slot], target)

    def stage(self, step):
        value, box = self.value, self.box
        targets = (self.to.to_twin, self.to.to_two, self.to.to_one)
        if step > 0 and step < 4:
            self.had[step - 1].wait_recv()
            value[step] = value[step - 1] + box[step - 1]
        if step < 3:
            self.pass_on(step, targets[step])
        elif step == 3:
            for k in range(3):
                self.pass_on(3 + k, self.to.to_z[k])
        elif step == 4:
            for k in range(3):
                self.had[3 + k].wait_recv()
            value[4] = (value[3] + box[3]) + (box[4] + box[5])

    def finish(self):
        self.copies.finish()


def fold_block(block, parts=2):
    cols = block.shape[1] // parts
    return jnp.concatenate([block[:, j * cols : (j + 1) * cols] for j in range(parts)], axis=0).astype(BF16)


class Column:
    def __init__(self, own, blocks, local, send, recv, gather):
        self.own, self.blocks, self.gather = own, blocks, gather
        self.copies, self.had = Copies(send, recv), {}
        self.keep = pltpu.make_async_copy(own, blocks.at[gather.z], local.at[0])

    def begin(self):
        self.keep.start()
        for k in range(3):
            self.had[k] = self.copies.start(0, k, self.own, self.blocks.at[self.gather.z], self.gather.to_z[k])

    def finish(self):
        self.keep.wait()
        for k in range(3):
            self.had[k].wait_recv()
        self.copies.finish()


class Spread:
    def __init__(self, column, blocks, local, send, recv, place):
        self.column, self.blocks, self.place = column, blocks, place
        self.copies, self.had = Copies(send, recv), {}
        self.here = pltpu.make_async_copy(column, blocks.at[pl.ds(place.dp * 4, 4)], local)

    def pass_on(self, j, dp, ways, src=None):
        at = self.blocks.at[dp * 4 + j]
        for slot, target in ways:
            self.had[slot + j] = self.copies.start(0, slot + j, at if src is None else src, at, target)

    def begin(self):
        place = self.place
        self.here.start()
        for j in range(4):
            ways = ((0, place.to_one), (4, place.to_two), (8, place.to_twin))
            self.pass_on(j, place.dp, ways, self.column.at[j])

    def stage(self, step):
        place = self.place
        for j in range(4):
            if step == 0:
                self.had[j].wait_recv()
                self.pass_on(j, place.one, ((12, place.to_two), (16, place.to_twin)))
                self.had[4 + j].wait_recv()
                self.pass_on(j, place.two, ((20, place.to_twin),))
            elif step == 1:
                self.had[12 + j].wait_recv()
                self.pass_on(j, place.far, ((24, place.to_twin),))
            else:
                for slot in (8, 16, 20, 24):
                    self.had[slot + j].wait_recv()
        if step == 2:
            self.here.wait()

    def finish(self):
        self.copies.finish()


def unfold_into(out, blocks, rows):
    n, have, cols = blocks.shape

    def body(j, _):
        pair = [blocks[2 * j + i].astype(F32) for i in (0, 1)]
        r = pl.ds(pl.multiple_of(2 * rows * j, 2 * rows), 2 * rows)
        for m in range(have // rows):
            both = jnp.concatenate([item[m * rows : (m + 1) * rows] for item in pair], axis=0)
            out[r, m * cols : (m + 1) * cols] = both.astype(BF16)
        return 0

    lax.fori_loop(0, n // 2, body, 0)


def unpack_vectors(slabs, out, sizes, some):
    n, _, lanes = slabs.shape
    step = 768
    for size in sorted({sizes[j] for j in some}):
        for at in range(0, n * size, step):
            lane = iota((1, step), 1) + at
            owner = lane // size
            places = (iota((lanes, step), 0) == lane - owner * size).astype(BF16)
            mine = (iota((n, step), 0) == owner).astype(F32)
            for j in some:
                if sizes[j] == size:
                    out[j : j + 1, at : at + step] = column_sum(dot(slabs[:, j, :].astype(BF16), places) * mine)


def front_kernel(
    groups, local, sizes, lens, tok, s_in, s_out, s_up, s_down, *refs,
):
    vecs, refs = refs[: len(sizes)], refs[len(sizes) :]
    front_steps(groups, local, sizes, vecs, lens, tok, s_in, s_out, s_up, s_down, *refs)


def front_steps(
    groups, local, sizes, vecs, lens, tok, s_in, s_out, s_up, s_down,
    q_h, k_h, v_h, joined_h, rest_h, inverse_h, states_h, rows_out, wq_h, wk_h, wv_h, wout_h, wup_h, wdown_h, vectors,
    cos_s, sin_s, ok_s, within, own, own_rows, part, part_rows, came, came_rows, num_s, den_s,
    q, k, v, joined, rest, inverse, states, w_q, w_k, w_v, w_out, w_up, save_sem,
    own_down, d_local, d_send, d_recv, g_vec, g_q, g_k, g_v, g_out, g_up, g_send, g_recv, *link,
):
    width = tok.shape[1]
    pairs = width // LANES
    chain = Chain(1, pairs, link)
    saved = []

    def save(*pairs_of_refs):
        for src, dst in pairs_of_refs:
            saved.append(pltpu.make_async_copy(src, dst, save_sem.at[len(saved)]))
            saved[-1].start()

    half = g_up.shape[1] // 2
    arrays = [(ref, 0, ref.shape[1], True) for ref in (g_vec, g_k, g_v, g_q)]
    arrays += [(g_out, 0, g_out.shape[1], False), (g_up, 0, half, False), (g_up, half, half, False)]
    gather = Gather(arrays, g_send, g_recv)
    me = gather.me
    g_vec[me] = jnp.zeros(g_vec.shape[1:], F32)
    for j, vec in enumerate(vecs):
        g_vec[me, j : j + 1, 0 : sizes[j]] = vec[...].astype(BF16).astype(F32)
    for j, ref in ((1, g_k), (2, g_v), (0, g_q)):
        ref[me] = fold_block(s_in[:, j * width : (j + 1) * width])
    meet(gather.targets())
    for a in range(4):
        gather.begin(a)
    g_out[me] = fold_block(s_out[...])
    g_up[me] = fold_block(s_up[...], 4)
    own_down[...] = s_down[...].astype(BF16)
    column = Column(own_down, wdown_h, d_local, d_send, d_recv, gather)
    starts = (0, 0, 1, 2, 5, 6, 7)

    def wave(t):
        for a in range(7):
            if 0 <= t - starts[a] < (6 if a < 4 else 5):
                gather.stage(a, t - starts[a])

    work = Forward(
        groups, local, lens, chain, (q, k, v, joined, rest, inverse, states, rows_out),
        (cos_s, sin_s, ok_s, within, num_s, den_s), (own, own_rows, part, part_rows, came, came_rows),
    )
    sums, arrive, leave, intra, inter = work.steps()
    work.prepare()
    wave(0)
    wave(1)
    for a in range(4, 7):
        gather.begin(a)
    for t in range(2, 6):
        wave(t)
    unpack_vectors(g_vec, vectors, sizes, (0,))
    bias = vectors.at[0:1]
    unfold_into(w_k, g_k, s_in.shape[0])
    work.project(1, tok, w_k, bias)
    wave(6)
    unfold_into(w_v, g_v, s_in.shape[0])
    work.project(2, tok, w_v, bias)

    def relay(at, *some):
        @pl.when(chain.at == at)
        def _():
            for s in some:
                arrive(s)
                if at < 3:
                    leave(s)

    for s in range(groups):
        work.over(sums, s)
        pl.when(chain.is_first)(functools.partial(leave, s))
    wave(7)
    unfold_into(w_q, g_q, s_in.shape[0])
    for s in range(groups):
        work.project(0, tok, w_q, bias, s)
        relay(1, s)
    save((q, q_h), (k, k_h), (v, v_h), (w_q, wq_h), (w_k, wk_h), (w_v, wv_h))
    wave(8)
    work.over(intra, 0)
    relay(2, 0)
    wave(9)
    work.over(intra, 1)
    relay(2, 1)
    unpack_vectors(g_vec, vectors, sizes, range(1, 8))
    wave(10)
    unfold_into(w_out, g_out, s_out.shape[0])
    relay(2, 2)
    work.over(intra, 2)
    wave(11)
    column.begin()
    unfold_into(w_up, g_up, s_up.shape[0])
    save((w_out, wout_h), (w_up, wup_h))
    for s in range(groups):
        relay(3, s)
        work.over(inter, s)
        r = pl.ds(s * local, local)
        u = pl.ds(s * pairs * work.count, pairs * work.count)
        save((joined.at[r], joined_h.at[r]), (rest.at[r], rest_h.at[r]), (inverse.at[r], inverse_h.at[r]))
        save((states.at[u], states_h.at[u]))

    @pl.when(jnp.logical_not(chain.is_last))
    def _():
        for s in range(groups):
            chain.sent(s)

    gather.finish()
    column.finish()
    for copy in saved:
        copy.wait()


TALL = 384


def by_eight(x):
    return jnp.sum(x.reshape(x.shape[0] // 8, 8, x.shape[1]), axis=0)


def middle_kernel(
    tok_h, joined_h, cot_h, w_out, up_h, down_h, vectors,
    act_h, first_h, gj_h, gup_h, gout_h, gw_down, small,
    low, joined, cot, branch, norm, sec, inv, hid, der, w_up, w_dn, box, xa, xb, fold_s, acc, acc_up,
    io, g_send, g_recv, r_send, r_recv,
):
    rows, width = joined.shape
    ff = w_up.shape[1]
    chunks = ff // width
    tiles = rows // TALL
    slabs = TALL // 96
    depth = rows // 96
    _, b_out, g_one, s_one, b_up, b_down, g_two, s_two = (
        (lambda j: lambda at=0, n=width: vectors[j : j + 1, at : at + n])(j) for j in range(8)
    )
    scatter = Scatter(
        [(hid, box, gw_down, 0, 48), (hid, box, gw_down, 48, 48)],
        r_send, r_recv, lambda dp: depth * (dp // 2) + 4 * lax.rem(dp, 2),
    )
    loads = [
        pltpu.make_async_copy(src, dst, io.at[j])
        for j, (src, dst) in enumerate(((joined_h, joined), (tok_h, low), (up_h, w_up), (cot_h, cot)))
    ]
    for load in loads:
        load.start()
    meet(scatter.targets())
    spread_down = Spread(down_h, w_dn, io.at[5], g_send, g_recv, scatter)
    spread_down.begin()
    acc[...] = jnp.zeros_like(acc)
    acc_up[...] = jnp.zeros_like(acc_up)

    def tile(t):
        return pl.ds(t * TALL, TALL) if isinstance(t, int) else pl.ds(pl.multiple_of(t * TALL, TALL), TALL)

    def of_chunk(ref, j, t=None):
        if t is None:
            return ref[pl.ds(depth * j, depth)].reshape(rows, width)
        return ref[pl.ds(depth * j + slabs * t, slabs)].reshape(TALL, width)

    def down_chunk(j):
        return w_dn[pl.ds(8 * j, 8)].reshape(width, width)

    loads[0].wait()
    loads[1].wait()
    def rows32(t, i):
        return pl.ds(pl.multiple_of(t * TALL + i, 32), 32)

    def by_tiles(body, low=0, high=tiles):
        def both(u, _):
            for i in range(2):
                body(2 * u + i, (xa, xb)[i])
            return 0

        lax.fori_loop(low // 2, high // 2, both, 0)

    def enter(t, x):
        x[...] = dot(joined[tile(t)], w_out[...])
        for i in range(0, TALL, 32):
            r = rows32(t, i)
            unit, scale = normalised(low[r].astype(F32) + (x[i : i + 32] + b_out()))
            norm[r] = unit
            inv[r] = jnp.broadcast_to(scale, (32, LANES))
            low[r] = (unit * g_one() + s_one()).astype(BF16)

    by_tiles(enter)
    loads[2].wait()

    def up(t, _):
        for j in range(chunks):
            x = (xa, xb)[j % 2]
            x[...] = dot(low[tile(t)], w_up[:, j * width : (j + 1) * width])
            for i in range(slabs):
                for m in range(0, 96, 32):
                    for n in range(0, width, 256):
                        y, d = gelu_both(x[96 * i + m : 96 * i + m + 32, n : n + 256] + b_up(j * width + n, 256))
                        hid[depth * j + slabs * t + i, m : m + 32, n : n + 256] = y.astype(BF16)
                        der[depth * j + slabs * t + i, m : m + 32, n : n + 256] = d.astype(BF16)
        return 0

    lax.fori_loop(0, tiles // 2, up, 0)
    spread_down.stage(0)
    lax.fori_loop(tiles // 2, tiles - 1, up, 0)
    spread_down.stage(1)
    lax.fori_loop(tiles - 1, tiles, up, 0)
    spread_down.stage(2)
    loads[3].wait()

    def second(t, x):
        x[...] = dot(of_chunk(hid, 0, t), down_chunk(0))
        for j in range(1, chunks):
            x[...] += dot(of_chunk(hid, j, t), down_chunk(j))
        for i in range(0, TALL, 32):
            r = rows32(t, i)
            unit, scale = normalised(norm[r] * g_one() + (s_one() + b_down()) + x[i : i + 32])
            c = cot[r].astype(F32)
            cot[r] = (unit * g_two() + s_two()).astype(BF16)
            acc[4] += by_eight(c * unit)
            acc[5] += by_eight(c)
            e = c * g_two()
            g = scale * (e - mean_of(e) - unit * mean_of(e * unit))
            sec[r] = g
            g = g.astype(BF16)
            branch[r] = g
            acc[3] += by_eight(g.astype(F32))

    by_tiles(second)
    act = pltpu.make_async_copy(cot, act_h, io.at[3])
    act.start()
    for j in range(chunks):
        for m in range(2):
            x = (xa, xb)[m]
            x[...] = tdot(
                hid[pl.ds(depth * j, depth), :, m * TALL : (m + 1) * TALL].reshape(rows, TALL), branch[...]
            )
        for m in range(2):
            hid[pl.ds(depth * j + 4 * m, 4)] = (xa, xb)[m][...].astype(BF16).reshape(4, 96, width)
    scatter.begin(0)
    scatter.begin(1)

    def back(t, _):
        for j in range(chunks):
            x = (xa, xb)[j % 2]
            x[...] = dot_t(branch[tile(t)], down_chunk(j))
            for i in range(slabs):
                for m in range(0, 96, 32):
                    at = depth * j + slabs * t + i
                    g = x[96 * i + m : 96 * i + m + 32] * der[at, m : m + 32].astype(F32)
                    g = g.astype(BF16)
                    der[at, m : m + 32] = g
                    acc_up[:, j * width : (j + 1) * width] += by_eight(g.astype(F32))
        return 0

    lax.fori_loop(0, tiles // 2, back, 0)
    scatter.stage(0, 0)
    lax.fori_loop(tiles // 2, tiles, back, 0)
    scatter.stage(1, 0)
    out = []

    def first(t, x):
        x[...] = dot_t(of_chunk(der, 0, t), w_up[:, 0:width])
        for j in range(1, chunks):
            x[...] += dot_t(of_chunk(der, j, t), w_up[:, j * width : (j + 1) * width])
        for i in range(0, TALL, 32):
            r = rows32(t, i)
            g = sec[r] + x[i : i + 32]
            unit = norm[r]
            acc[1] += by_eight(g * unit)
            acc[2] += by_eight(g)
            e = g * g_one()
            g = inv[r, 0:1] * (e - mean_of(e) - unit * mean_of(e * unit))
            sec[r] = g
            g = g.astype(BF16)
            branch[r] = g
            acc[0] += by_eight(g.astype(F32))

    by_tiles(first)
    out.append(pltpu.make_async_copy(sec, first_h, io.at[0]))
    out[-1].start()
    scatter.stage(0, 1)
    spread_down.finish()
    for m in range(2):
        for jj in range(chunks // 2):
            for i in range(2):
                (xa, xb)[i][...] = tdot(low[:, m * TALL : (m + 1) * TALL], of_chunk(der, 2 * jj + i))
            for i in range(16):
                both = [x[24 * i : 24 * i + 24] for x in (xa, xb)]
                w_dn[16 * m + i, 48 * jj : 48 * jj + 48] = jnp.concatenate(both, axis=0).astype(BF16)
        scatter.stage(1 - m, 1 + m)
    out.append(pltpu.make_async_copy(w_dn, gup_h, io.at[1]))
    out[-1].start()
    for m in range(2):
        x = (xa, xb)[m]
        x[...] = tdot(joined[:, m * TALL : (m + 1) * TALL], branch[...])
        for i in range(16):
            fold_s[16 * m + i] = fold_block(x[24 * i : 24 * i + 24])
    out.append(pltpu.make_async_copy(fold_s, gout_h, io.at[2]))
    out[-1].start()
    scatter.stage(1, 2)
    for t in range(tiles):
        joined[tile(t)] = dot_t(branch[tile(t)], w_out[...]).astype(BF16)
    out.append(pltpu.make_async_copy(joined, gj_h, io.at[4]))
    out[-1].start()
    small[...] = jnp.zeros_like(small)
    for row, at in ((3, 0), (4, 1), (5, 2), (10, 3), (11, 4), (12, 5)):
        small[row : row + 1] = column_sum(acc[at])
    for j in range(chunks):
        small[6 + j : 7 + j] = column_sum(acc_up[:, j * width : (j + 1) * width])
    scatter.stage(0, 3)
    scatter.stage(1, 3)
    act.wait()
    for copy in out:
        copy.wait()
    scatter.finish()


def own_slices(value, me):
    width = value.shape[1]
    parts, left = [], value
    for _ in range(3):
        parts.append(left.astype(BF16))
        left = left - parts[-1].astype(F32)

    def pick(size):
        lane = iota((width, LANES), 1)
        at = iota((width, LANES), 0) - size * lax.rem(me, width // size)
        ones = ((at == lane) & (lane < size)).astype(BF16)
        return sum(dot(part, ones) for part in parts)

    def row(picked, at):
        return column_sum(jnp.where(iota(picked.shape, 0) == at, picked, 0.0))

    few, some, many = pick(width // 32), pick(width // 16), pick(width // 8)
    rows = [row(some, me // 16)] + [few[j : j + 1] for j in range(2, 6)] + [row(many, 6 + me // 8)]
    rows += [few[j : j + 1] for j in range(10, 13)]
    return jnp.concatenate(rows + [jnp.zeros((16 - len(rows), LANES), F32)], axis=0)


def finish_kernel(act, grad, down, up, out, q, k, v, act_o, grad_o, down_o, up_o, out_o, in_o, *scratch):
    boxes, (sems,) = scratch[:8], scratch[8:]
    width = q.shape[1]
    plan = []
    for src, dst, box, cuts in ((grad, grad_o, boxes[0], 12), (act, act_o, boxes[1], 6)):
        step = src.shape[0] // cuts
        plan += [tuple(ref.at[pl.ds(j * step, step)] for ref in (src, box, dst)) for j in range(cuts)]
    plan += [(down, boxes[2], down_o), (up, boxes[3], up_o), (out, boxes[4], out_o)]
    for j, ref in enumerate((q, k, v)):
        plan.append((ref, boxes[5 + j], in_o.at[:, j * width : (j + 1) * width]))
    come = [pltpu.make_async_copy(src, box, sems.at[0, j]) for j, (src, box, _) in enumerate(plan)]
    go = [pltpu.make_async_copy(box, dst, sems.at[1, j]) for j, (_, box, dst) in enumerate(plan)]
    for copy in come:
        copy.start()
    for first, second in zip(come, go):
        first.wait()
        second.start()
    for copy in go:
        copy.wait()


def tail_kernel(
    groups, local, lens, q_h, k_h, v_h, gj_h, joined_h, rest_h, inverse_h, states, rows_in,
    tok_h, wq_h, wk_h, wv_h, first_h, up_h, out_h, small,
    grad_h, gw_up, gw_out, gw_q, gw_k, gw_v, small_out,
    q, k, v, gnum, joined, lane_s, inverse, cos_s, sin_s, within,
    own, own_rows, part, part_rows, came, came_rows, slots, load_sem, slot_sem,
    b_up, b_out, b_q, b_k, b_v, x_up, x_out, x_q, x_k, x_v,
    value, box, r_send, r_recv, t_send, t_recv, *link,
):
    width = q.shape[1]
    rows = q.shape[0]
    pairs = width // LANES
    count = local // CHUNK
    chain = Chain(-1, pairs, link)
    half = b_up.shape[1] // 2
    arrays = [(b_up, x_up, gw_up, 0, half), (b_up, x_up, gw_up, half, half)]
    arrays += [
        (buf, box, out, 0, buf.shape[1])
        for buf, box, out in ((b_out, x_out, gw_out), (b_q, x_q, gw_q), (b_k, x_k, gw_k), (b_v, x_v, gw_v))
    ]
    scatter = Scatter(arrays, r_send, r_recv, straight=(3, 4, 5))
    total = Total(scatter, value, box, t_send, t_recv)
    places = (
        (inverse_h, inverse), (gj_h, gnum), (joined_h, joined), (rest_h, lane_s), (q_h, q),
        (up_h, b_up), (out_h, b_out), (k_h, k), (v_h, v),
    )
    loads = [pltpu.make_async_copy(src, dst, load_sem.at[j]) for j, (src, dst) in enumerate(places)]
    for load in loads:
        load.start()
    meet(scatter.targets())
    fill_tables(groups, local, chain.at * local, lens, cos_s, sin_s, None, within)

    def sums(i, _):
        s, p = i // pairs, i % pairs
        n = lanes_of(p)
        _, _, one, two = head_masks()
        mask = block_mask(256, LANES)
        ones = block_mask(2 * LANES, LANES).astype(BF16)
        state = jnp.zeros((256, LANES), F32)
        row = jnp.zeros((1, 256), F32)
        for c in reversed(range(count)):
            r = rows_of(s, c, local)
            ri = inverse[r, n].astype(F32)
            gn = (gnum[r, n].astype(F32) * jnp.abs(ri)).astype(BF16)
            product = gn.astype(F32) * (joined[r, n].astype(F32) + lane_s[r, n].astype(F32))
            gden = jnp.where(ri > 0, -dot(two_parts(product), ones), 0.0)
            high = gden.astype(BF16).astype(F32)
            gnum[r, n] = gn
            lane_s[r, n] = (high * one + (gden - high) * two).astype(BF16)
            q2 = spread(q[r, n].astype(F32), cos_s[r], sin_s[r])
            state = state + tdot(q2, gn)
            row = row + column_sum(q2.astype(F32) * twice(gden))
            if c > 0:
                part[i * (count - 1) + c - 1] = pack(state * mask)
                part_rows[i * (count - 1) + c - 1] = jnp.broadcast_to(row, (8, 256))
        own[i] = pack(state * mask)
        own_rows[i] = jnp.broadcast_to(row, (8, 256))
        came[i] = jnp.zeros((128, LANES), F32)
        came_rows[i] = jnp.zeros((8, 256), F32)
        return 0

    def arrive(s):
        chain.arrive(s)

        def one(p, _):
            i = s * pairs + p
            came[i] = chain.in_state[i].astype(F32)
            came_rows[i] = chain.in_rows[i]
            return 0

        lax.fori_loop(0, pairs, one, 0)

    def leave(s):
        def one(p, _):
            i = s * pairs + p
            n = lanes_of(p)
            state = came[i] + own[i]
            low = state.astype(BF16)
            chain.out_state[i] = low
            lost = unpack(state - low.astype(F32), block_mask(256, LANES)).astype(BF16)
            mean = column_sum(v[pl.ds(s * local, local), n].astype(F32)) * (1.0 / local)
            row = dot_t(jnp.broadcast_to(mean, (8, LANES)).astype(BF16), lost)
            chain.out_rows[i] = came_rows[i] + own_rows[i] + row
            return 0

        lax.fori_loop(0, pairs, one, 0)
        chain.start(s)

    def intra(i, _):
        s, p = i // pairs, i % pairs
        n = lanes_of(p)
        first, second, one, two = head_masks()
        ones = jnp.ones((CHUNK, LANES), BF16)
        picks = (block_mask(LANES, LANES) * ((iota((LANES, LANES), 0) & (HALF - 1)) < 2).astype(F32)).astype(BF16)
        m = within[s]
        m = jnp.concatenate([m, m], axis=0)
        for c in range(count):
            r = rows_of(s, c, local)
            feature, key, value_low, gn, lane = q[r, n].astype(F32), k[r, n], v[r, n], gnum[r, n], lane_s[r, n]
            gden = dot(lane, picks)
            row = rows_in[i * count + c][0:1]
            outer = dot_t(twice(gn), states[i * count + c]) + twice(gden) * row
            gq = outer[:, :LANES] * cos_s[r] + outer[:, LANES:] * sin_s[r]
            heads = stacked_heads(feature, first, second)
            scores = (dot_t(heads, key) * m).astype(BF16)
            gheads = stacked_heads(gn.astype(F32), first, second)
            left = jnp.concatenate([gheads, stacked_heads(lane.astype(F32), first, second)], axis=1)
            g = (dot_t(left, jnp.concatenate([value_low, ones], axis=1)) * m).astype(BF16)
            inner = dot(g, key)
            gq = gq + jnp.where(first > 0, inner[:CHUNK], inner[CHUNK:])
            joined[r, n] = tdot(heads, g).T.astype(BF16)
            inverse[r, n] = tdot(gheads, scores).T.astype(BF16)
            q[r, n] = (gq * slope(feature)).astype(BF16)
        return 0

    def inter(i, _):
        s, p = i // pairs, i % pairs
        n = lanes_of(p)
        mask = block_mask(256, LANES)
        for c in range(count):
            r = rows_of(s, c, local)
            cosine, sine, key = cos_s[r], sin_s[r], k[r, n].astype(F32)
            state, row = came[i], came_rows[i][0:1]
            if c + 1 < count:
                state = state + part[i * (count - 1) + c]
                row = row + part_rows[i * (count - 1) + c][0:1]
            state = two_parts(unpack(state, mask))
            outer = dot_t(twice(v[r, n]), state) + row
            gk = outer[:, :LANES] * cosine + outer[:, LANES:] * sine + joined[r, n].astype(F32)
            v[r, n] = (dot(spread(key, cosine, sine), state[:, :LANES]) + inverse[r, n].astype(F32)).astype(BF16)
            k[r, n] = (gk * slope(key)).astype(BF16)
        return 0

    def over(step, s, low=0, high=pairs):
        lax.fori_loop(s * pairs + low, s * pairs + high, step, 0)

    def weight_terms(a, g):
        buf = scatter.arrays[a][0]
        size = width // 32
        for j in range(2):
            term = tdot(gnum[:, j * (width // 2) : (j + 1) * (width // 2)], g[...])
            for i in range(16):
                buf[16 * j + i] = fold_block(term[i * size : (i + 1) * size])

    for load in loads[:5]:
        load.wait()
    loads[5].wait()
    scatter.begin(0)
    scatter.begin(1)
    loads[6].wait()
    scatter.begin(2)
    for load in loads[7:]:
        load.wait()
    for s in reversed(range(groups)):
        over(sums, s)
        pl.when(chain.is_first)(functools.partial(leave, s))
    scatter.stage(0, 0)

    def relay(place, *some):
        @pl.when(chain.at == place)
        def _():
            for s in some:
                arrive(s)
                if place > 0:
                    leave(s)

    cut = pairs // 2
    over(intra, 0, 0, cut)
    scatter.stage(1, 0)
    over(intra, 0, cut, pairs)
    relay(2, 2)
    scatter.stage(2, 0)
    over(intra, 1, 0, cut)
    relay(2, 1)
    over(intra, 1, cut, pairs)
    relay(2, 0)
    relay(1, 2)
    scatter.stage(0, 1)
    over(intra, 2, 0, cut)
    relay(1, 1)
    over(intra, 2, cut, pairs)
    relay(1, 0)
    scatter.stage(1, 1)
    tok_load = pltpu.make_async_copy(tok_h, gnum, load_sem.at[0])
    w_loads = [
        pltpu.make_async_copy(wq_h, lane_s.at[pl.ds(0, width)], load_sem.at[1]),
        pltpu.make_async_copy(wk_h, lane_s.at[pl.ds(width, width)], load_sem.at[2]),
        pltpu.make_async_copy(wv_h, joined.at[pl.ds(0, width)], load_sem.at[3]),
    ]
    for load in [tok_load] + w_loads[:2]:
        load.start()
    tok_load.wait()
    weight_terms(3, q)
    scatter.begin(3)
    scatter.stage(0, 2)
    steps = (((2, 1), (1, 2)), ((3, 0), (2, 2)), ((0, 3), (1, 3)))
    for j, s in enumerate(reversed(range(groups))):
        relay(0, s)
        over(inter, s)
        for a, step in steps[j]:
            scatter.stage(a, step)
    w_loads[2].start()
    weight_terms(4, k)
    scatter.begin(4)
    scatter.stage(3, 2)
    scatter.stage(2, 3)
    weight_terms(5, v)
    scatter.begin(5)
    value[0] = small[...]
    for j, ref in enumerate((q, k, v)):
        value[0, j : j + 1, :] = column_sum(ref[...].astype(F32))
    total.stage(0)
    for load in w_loads:
        load.wait()

    def slot(i):
        return slots.at[i % 2]

    def rows_at(ref, i):
        return ref.at[pl.ds(i * local, local)]

    n_slots = groups
    fetch = [pltpu.make_async_copy(rows_at(first_h, i), slot(i), slot_sem.at[i % 2, 0]) for i in range(n_slots)]
    store = [pltpu.make_async_copy(slot(i), rows_at(grad_h, i), slot_sem.at[i % 2, 1]) for i in range(n_slots)]
    fetch[0].start()
    rest_plan = (((4, 0),), ((5, 0), (3, 3)), ((4, 2), (5, 2)))
    for i in range(n_slots):
        if i + 1 < n_slots:
            if i >= 1:
                store[i - 1].wait()
            fetch[i + 1].start()
        fetch[i].wait()
        r = pl.ds(i * local, local)
        slots[i % 2] += dot_t(q[r], lane_s[pl.ds(0, width)])
        slots[i % 2] += dot_t(k[r], lane_s[pl.ds(width, width)])
        slots[i % 2] += dot_t(v[r], joined[pl.ds(0, width)])
        store[i].start()
        for a, step in rest_plan[i] if i < len(rest_plan) else ():
            scatter.stage(a, step)
        total.stage(i + 1)
    for i in range(n_slots + 1, 5):
        total.stage(i)
    small_out[...] = own_slices(value[4], scatter.dp * 4 + scatter.z)
    scatter.stage(4, 3)
    scatter.stage(5, 3)
    for i in range(max(n_slots - 2, 0), n_slots):
        store[i].wait()

    @pl.when(jnp.logical_not(chain.is_last))
    def _():
        for s in range(groups):
            chain.sent(s)

    scatter.finish()
    total.finish()


VMEM = pl.BlockSpec(memory_space=pltpu.VMEM)
SMEM = pl.BlockSpec(memory_space=pltpu.SMEM)
ANY = pl.BlockSpec(memory_space=pl.ANY)


def params(collective=None):
    if collective is None:
        return pltpu.CompilerParams(vmem_limit_bytes=BIG)
    return pltpu.CompilerParams(vmem_limit_bytes=BIG, collective_id=collective, has_side_effects=True)


def shape(dims, kind=BF16):
    return jax.ShapeDtypeStruct(dims, kind)


def shards(
    tokens, lengths, weight_in, bias_in, weight_out, bias_out, gain_one, shift_one,
    weight_up, bias_up, weight_down, bias_down, gain_two, shift_two, cotangent,
):
    groups, local, width = tokens.shape
    rows = groups * local
    pairs = width // LANES
    count = local // CHUNK
    axes = ("dp", "head")
    parts = lax.axis_size("head")
    me = lax.axis_index("head")

    by_kernel = lax.axis_size("dp") == 8 and parts == 4
    small = (bias_in, bias_out, gain_one, shift_one, bias_up, bias_down, gain_two, shift_two)
    tok = tokens.reshape(rows, width)
    units = groups * pairs
    plane = shape((rows, width))
    table = pltpu.VMEM((rows, LANES), F32)
    within = pltpu.VMEM((groups, CHUNK, CHUNK), F32)
    tall = pltpu.VMEM((rows, width), F32)
    flat = pltpu.VMEM((rows, width), BF16)

    def sums_scratch():
        return [
            pltpu.VMEM((units, 128, LANES), F32),
            pltpu.VMEM((units, 8, 256), F32),
            pltpu.VMEM((units * max(count - 1, 1), 128, LANES), F32),
            pltpu.VMEM((units * max(count - 1, 1), 8, 256), F32),
            pltpu.VMEM((units, 128, LANES), F32),
            pltpu.VMEM((units, 8, 256), F32),
        ]

    forward_shapes = (plane,) * 6 + (shape((units * count, 256, 256)), shape((units * count, 8, 256), F32))
    forward_scratch = [table, table, table, within] + sums_scratch() + [tall, tall]
    ff = weight_up.shape[1]
    if by_kernel:
        square = shape((width, width))
        sizes = [item.shape[0] for item in small]
        half = (2 * weight_in.shape[0], width // 2)
        (
            q, k, v, joined, rest, inverse, states, state_rows, w_q, w_k, w_v, w_out, w_up, w_down, vectors
        ) = pl.pallas_call(
            functools.partial(front_kernel, groups, local, sizes),
            out_shape=forward_shapes
            + (square,) * 4
            + (shape((width, ff)), shape((4,) + weight_down.shape), shape((len(small), ff), F32)),
            in_specs=[SMEM] + [VMEM] * (5 + len(small)),
            out_specs=(ANY,) * 7 + (VMEM,) + (ANY,) * 6 + (VMEM,),
            scratch_shapes=forward_scratch
            + [flat] * 6
            + [pltpu.VMEM((units * count, 256, 256), BF16)]
            + [pltpu.VMEM((width, width), BF16)] * 4
            + [pltpu.VMEM((width, ff), BF16), pltpu.SemaphoreType.DMA((8 + 4 * groups,))]
            + [pltpu.VMEM(weight_down.shape, BF16), pltpu.SemaphoreType.DMA((1,))]
            + [pltpu.SemaphoreType.DMA((1, 3))] * 2
            + [pltpu.VMEM((32, 8, LANES), F32)]
            + [pltpu.VMEM((32,) + half, BF16)] * 4
            + [pltpu.VMEM((32, 4 * weight_up.shape[0], ff // 4), BF16)]
            + [pltpu.SemaphoreType.DMA((7, 31)), pltpu.SemaphoreType.DMA((7, 31))]
            + chain_scratch(groups, pairs),
            compiler_params=params(3),
        )(lengths, tok, weight_in, weight_out, weight_up, weight_down, *(item.reshape(1, -1) for item in small))
    else:

        def gather(item):
            return lax.all_gather(item.astype(BF16), axes, axis=0, tiled=True)

        w_in, w_out, w_up, w_down = map(gather, (weight_in, weight_out, weight_up, weight_down))
        sizes = [item.shape[0] for item in small]
        gathered = lax.all_gather(jnp.concatenate([item.astype(BF16) for item in small]), axes, axis=0)
        cuts = [sum(sizes[:i]) for i in range(len(sizes) + 1)]
        b_in, b_out, g_one, s_one, b_up, b_down, g_two, s_two = (
            gathered[:, a:b].reshape(1, -1).astype(F32) for a, b in zip(cuts, cuts[1:])
        )
        w_q, w_k, w_v = (w_in[:, j * width : (j + 1) * width] for j in range(3))
        q, k, v, joined, rest, inverse, states, state_rows = pl.pallas_call(
            functools.partial(attend_kernel, groups, local),
            out_shape=forward_shapes,
            in_specs=[SMEM] + [VMEM] * 5,
            out_specs=(VMEM,) * 8,
            scratch_shapes=forward_scratch + chain_scratch(groups, pairs),
            compiler_params=params(1),
        )(lengths, tok, w_q, w_k, w_v, b_in)

    tile = local

    if by_kernel:
        slabs96 = shape((32, 96, width))
        term_out = shape((32,) + half)
        kept = pltpu.VMEM((rows // 96 * (ff // width), 96, width), BF16)
        tile_s = pltpu.VMEM((TALL, width), F32)
        activations, g_first, g_joined, gw_up, gw_out, gw_down, small_sums = pl.pallas_call(
            middle_kernel,
            out_shape=[
                plane, shape((rows, width), F32), plane, slabs96, term_out,
                shape(weight_down.shape, F32), shape((16, width), F32),
            ],
            in_specs=[ANY] * 3 + [VMEM, ANY, ANY, VMEM],
            out_specs=[ANY] * 5 + [VMEM] * 2,
            scratch_shapes=[flat] * 4
            + [tall, tall, table, kept, kept]
            + [pltpu.VMEM((width, ff), BF16), pltpu.VMEM((32, 96, width), BF16), pltpu.VMEM((31, 96, width), BF16)]
            + [tile_s, tile_s, pltpu.VMEM((32,) + half, BF16)]
            + [pltpu.VMEM((6, 8, width), F32), pltpu.VMEM((8, ff), F32)]
            + [pltpu.SemaphoreType.DMA((6,))]
            + [pltpu.SemaphoreType.DMA((1, 28))] * 2
            + [pltpu.SemaphoreType.DMA((2, 10))] * 2,
            compiler_params=params(5),
        )(tok, joined, cotangent.reshape(rows, width), w_out, w_up, w_down, vectors)
        terms = [gw_up.shape, gw_out.shape] + [(32,) + half] * 3
        row_shape = (weight_out.shape[0], width)
        input_grad, gw_up, gw_out, gw_q, gw_k, gw_v, sums = pl.pallas_call(
            functools.partial(tail_kernel, groups, local),
            out_shape=[shape((rows, width), F32), shape(weight_up.shape, F32)]
            + [shape(row_shape, F32)] * 4
            + [shape((16, LANES), F32)],
            in_specs=[SMEM] + [ANY] * 7 + [VMEM] * 2 + [ANY] * 7 + [VMEM],
            out_specs=[ANY] + [VMEM] * 6,
            scratch_shapes=[flat] * 7
            + [table, table, within]
            + sums_scratch()
            + [pltpu.VMEM((2, local, width), F32)]
            + [pltpu.SemaphoreType.DMA((9,)), pltpu.SemaphoreType.DMA((2, 2))]
            + [pltpu.VMEM(item, BF16) for item in terms]
            + [pltpu.VMEM((31,) + item[1:], BF16) for item in terms]
            + [pltpu.VMEM((5,) + small_sums.shape, F32), pltpu.VMEM((6,) + small_sums.shape, F32)]
            + [pltpu.SemaphoreType.DMA((6, 10))] * 2
            + [pltpu.SemaphoreType.DMA((1, 6))] * 2
            + chain_scratch(groups, pairs),
            compiler_params=params(4),
        )(
            lengths, q, k, v, g_joined, joined, rest, inverse, states, state_rows,
            tok, w_q, w_k, w_v, g_first, gw_up, gw_out, small_sums,
        )
        kinds = (3 * width, width, width, width, width, ff, width, width, width)
        mine = [sums[j, : (2 * width if j == 0 else size) // 32] for j, size in enumerate(kinds)]
        gb_front, gb_value, gb_out, gg_one, gs_one, gb_up, gb_down, gg_two, gs_two = mine
        activations, input_grad, gw_down, gw_up, gw_out, gw_in = pl.pallas_call(
            finish_kernel,
            out_shape=[plane, shape((rows, width), F32)]
            + [shape(item.shape, F32) for item in (weight_down, weight_up, weight_out, weight_in)],
            in_specs=[ANY] * 8,
            out_specs=[ANY] * 6,
            scratch_shapes=[
                pltpu.VMEM(item.shape, item.dtype)
                for item in (input_grad, activations, gw_down, gw_up, gw_out, gw_q, gw_k, gw_v)
            ]
            + [pltpu.SemaphoreType.DMA((2, 24))],
            compiler_params=params(),
        )(activations, input_grad, gw_down, gw_up, gw_out, gw_q, gw_k, gw_v)
        return (
            activations.reshape(groups, local, width),
            input_grad.reshape(groups, local, width),
            gw_in, gb_front, gb_value, gw_out, gb_out, gg_one, gs_one,
            gw_up, gb_up, gw_down, gb_down, gg_two, gs_two,
        )

    def block(cols):
        return pl.BlockSpec((tile, cols), lambda i: (i, 0))

    def fixed(*dims):
        return pl.BlockSpec(dims, lambda i: (0,) * len(dims), pipeline_mode=pl.Buffered(1))

    vectors = [fixed(1, width)] * 3 + [fixed(1, ff)] + [fixed(1, width)] * 3
    weights = [fixed(width, width), fixed(width, ff), fixed(ff, width)]
    vector_shapes = [shape((1, width), F32)] * 3 + [shape((1, ff), F32)] + [shape((1, width), F32)] * 3
    (
        activations, g_first, g_joined, gw_out, gw_up, gw_down,
        gb_out, gg_one, gs_one, gb_up, gb_down, gg_two, gs_two,
    ) = pl.pallas_call(
        feed_kernel,
        grid=(rows // tile,),
        out_shape=[plane, shape((rows, width), F32), plane]
        + [shape((width, width), F32), shape((width, ff), F32), shape((ff, width), F32)]
        + vector_shapes,
        in_specs=[block(width)] * 3 + weights + vectors,
        out_specs=[block(width)] * 3 + weights + vectors,
        scratch_shapes=[
            pltpu.VMEM((tile, width), F32),
            pltpu.VMEM((tile, width), BF16),
            pltpu.VMEM((tile, ff), BF16),
            pltpu.VMEM((tile, ff), BF16),
            pltpu.VMEM((tile, width), F32),
            pltpu.VMEM((tile, width), BF16),
        ],
        compiler_params=params(),
    )(
        tok, joined, cotangent.reshape(rows, width), w_out, w_up, w_down,
        b_out, g_one, s_one, b_up, b_down, g_two, s_two,
    )
    g_mixed = pl.pallas_call(
        functools.partial(back_kernel, groups, local),
        out_shape=shape((rows, 3 * width)),
        in_specs=[SMEM] + [VMEM] * 9,
        out_specs=VMEM,
        scratch_shapes=[table, table, within] + sums_scratch()
        + [pltpu.VMEM((rows, width), BF16), tall, pltpu.VMEM((rows, width), BF16)] + chain_scratch(groups, pairs),
        compiler_params=params(2),
    )(lengths, q, k, v, g_joined, joined, rest, inverse, states, state_rows)
    input_grad, gw_in, gb_in = pl.pallas_call(
        input_kernel,
        grid=(rows // tile,),
        out_shape=[shape((rows, width), F32), shape((width, 3 * width), F32), shape((1, 3 * width), F32)],
        in_specs=[block(width), block(3 * width), fixed(width, 3 * width), block(width)],
        out_specs=[block(width), fixed(width, 3 * width), fixed(1, 3 * width)],
        compiler_params=params(),
    )(tok, g_mixed, w_in, g_first)

    gb_in = gb_in.reshape(-1)
    cols = [gb_in[: 2 * width], gb_in[2 * width :]] + [
        item.reshape(-1) for item in (gb_out, gg_one, gs_one, gb_up, gb_down, gg_two, gs_two)
    ]
    total = lax.axis_size(axes)
    def scatter(item):
        return lax.psum_scatter(item, axes, scatter_dimension=0, tiled=True)

    cut = [item.shape[0] // total for item in cols]
    merged = scatter(jnp.concatenate([item.reshape(total, -1) for item in cols], axis=1).reshape(-1))
    places = [sum(cut[:i]) for i in range(len(cut) + 1)]
    (gb_front, gb_value, gb_out, gg_one, gs_one, gb_up, gb_down, gg_two, gs_two) = (
        merged[a:b] for a, b in zip(places, places[1:])
    )
    return (
        activations.reshape(groups, local, width),
        input_grad.reshape(groups, local, width),
        scatter(gw_in), gb_front, gb_value, scatter(gw_out), gb_out, gg_one, gs_one,
        scatter(gw_up), gb_up, scatter(gw_down), gb_down, gg_two, gs_two,
    )


def solution(mesh):
    spread_rows = P("dp", "head", None)
    matrix = P(("dp", "head"), None)
    vector = P(("dp", "head"))
    return jax.shard_map(
        shards,
        mesh=mesh,
        in_specs=(
            spread_rows, P("dp"), matrix, vector, matrix, vector, vector, vector,
            matrix, vector, matrix, vector, vector, vector, spread_rows,
        ),
        out_specs=(
            spread_rows, spread_rows, matrix, vector, vector, matrix, vector, vector, vector,
            matrix, vector, matrix, vector, vector, vector,
        ),
        check_vma=False,
    )
```
